256 devices in a mesh: row: 32 (over y_lo, z, core), col: 8 (over y_hi, x).
Axes of the slice: x: 4, y: 4 (y_hi: 2, y_lo: 2; y = y_hi * 2 + y_lo), z: 8, core: 2. Of those that a mesh axis runs over, the one named last changes fastest.
Arguments:
- pair_matrix: bfloat16 [64, 16, 3072], P('row', None, 'col'), may hold values from -0.109375 to 0.109375
- screened: bfloat16 [64, 3072, 3072], P('row', 'col'), may hold values from -6 to 6
- coulomb: float32 [3072], P('col'), may hold values from 0.2 to 2
- q_index: int32 [64, 64], replicated, may hold values from 0 to 63, as said below
Outputs:
- kernel: float32 [1024, 1024], P('row', 'col')
The draws below stay inside these ranges and needn't reach their ends.
Inputs may be any that keep to these rules, and one draw needn't show every extreme that they name: q_index[k, k'] = (m(k) - m(k')) mod 64 for a permutation m of the panel's k-points, so every row and every column holds each q exactly once.
All inputs are finite; a program needn't handle non-finite values.
Results may differ from the reference program's by a relative error of at most 0.0095.
Values may be sent and summed in bfloat16 or wider, within the bound.
No kernel may reach another device: no remote copies, remote signals or barrier semaphores. Data moves between devices by JAX's collectives and lax.ppermute only.
A program may use at most 128 MiB of HBM per device.

```python
import math
import jax
import jax.numpy as jnp
from jax import lax

NB = 16
NG = 3072
NKP = 64


def draw_q_index(key, part):
    key = jax.random.fold_in(key, 11)
    order = jax.random.permutation(key, NKP).astype(jnp.int32)
    return jnp.mod(order[:, None] - order[None, :], NKP).astype(jnp.int32)


def shard_levels(stream_key, extent, split, smallest, high):
    level, own = 1.0, jax.random.fold_in(stream_key, 6)
    for dim, shards_of in split:
        heights = jnp.exp(jax.random.uniform(jax.random.fold_in(own, dim), (shards_of,), jnp.float32, smallest / len(split), high / len(split)))
        level = level * jnp.repeat(heights, extent[dim] // shards_of).reshape([-1 if axis == dim else 1 for axis in range(len(extent))])
    return level


def gaussian(own_key, shape, width, bound, shards=(), kind=jnp.bfloat16):
    result = width * jax.random.normal(own_key, shape, jnp.float32)
    if shards:
        result = result * shard_levels(own_key, shape, shards, -0.22, 0.18)
    return jnp.clip(result, -bound, bound).astype(kind)


def setup_inputs(seed: int = 0) -> dict:
    splits = jax.random.split(jax.random.key(seed), 5)
    return {
        "pair_matrix": gaussian(splits[0], (NKP, NB, NG), (NG ** -0.5), 0.109375, ((0, 32), (2, 8))),
        "screened": gaussian(splits[1], (NKP, NG, NG), 1.0, 6.0, ((0, 32), (1, 8))),
        "coulomb": jnp.clip(jnp.exp(math.log(2.0) - 2.3025851 * jax.random.uniform(splits[2], (NG,), jnp.float32) ** shard_levels(splits[2], (NG,), ((0, 8),), -0.2, 0.2)), 0.2, 2.0),
        "q_index": draw_q_index(jax.random.fold_in(splits[4], 71), 0),
    }


def reference(pair_matrix, screened, coulomb, q_index):
    flat = pair_matrix.reshape(NKP * NB, NG)
    positions = jnp.arange(NKP, dtype=jnp.int32)

    def one_transfer(packed):
        w_block, q_value = packed
        image = jnp.dot(flat, w_block, preferred_element_type=jnp.float32).astype(jnp.bfloat16).reshape(NKP, NB, NG)
        partner = jnp.sum(jnp.where(q_index == q_value, positions[None, :], 0), axis=1).astype(jnp.int32)
        chosen = jnp.take(pair_matrix, partner, axis=0).astype(jnp.float32)
        return jnp.einsum("kbg,kcg->kbc", image.astype(jnp.float32), chosen, precision=lax.Precision.HIGHEST)

    direct_all = lax.map(one_transfer, (screened, positions))
    direct = direct_all[q_index, positions[:, None]]
    widened = pair_matrix.astype(jnp.float32)
    weighted = (widened * coulomb).astype(jnp.bfloat16).astype(jnp.float32)
    bare = jnp.einsum("kbg,jcg->kbjc", weighted, widened, precision=lax.Precision.HIGHEST)
    kernel = 2.0 * bare - jnp.transpose(direct, (0, 2, 1, 3))
    return kernel.reshape(NKP * NB, NKP * NB)
```

```python
import jax
import jax.numpy as jnp
from jax import lax
from jax.experimental import pallas as pl
from jax.experimental.pallas import tpu as pltpu
from jax.sharding import PartitionSpec as P

AXES = ("row", "col")
NX, NY, NZ, NCORE = 4, 4, 8, 2
SHIFTS = (0, 2, 1, -1)
ZSHIFTS = (0, 2, -2, 4)
VMEM = 48 * 1024 * 1024


def device_index(x, y, z, c):
    y_hi, y_lo = divmod(y % NY, 2)
    row = (y_lo * NZ + z % NZ) * NCORE + c
    return row * 8 + y_hi * NX + x % NX


def pairs(move):
    found = []
    for x in range(NX):
        for y in range(NY):
            for z in range(NZ):
                for c in range(NCORE):
                    found.append((device_index(x, y, z, c), device_index(*move(x, y, z, c))))
    return found


SWAP = pairs(lambda x, y, z, c: (x, y, z, 1 - c))
ZPAIR = pairs(lambda x, y, z, c: (x, y, z ^ 1, c))


def along_z(s):
    return pairs(lambda x, y, z, c: (x, y, z + s, c))


def first_plane(s):
    return pairs(lambda x, y, z, c: (x + s, y, z, c) if c == 0 else (x, y + s, z, c))


def second_plane(s):
    return pairs(lambda x, y, z, c: (x, y + s, z, c) if c == 0 else (x + s, y, z, c))


def send(value, perm):
    return lax.ppermute(value, AXES, perm)


def contract(a, b):
    return lax.dot_general(a, b, (((1,), (1,)), ((), ())), preferred_element_type=jnp.float32)


def project_kernel(cols, lows, p0, p1, p2, p3, mine, coulomb, w_own, w_other, out, total):
    share = p0.shape[2]

    def run(w):
        total[...] = jnp.zeros_like(total)
        for k, panel in enumerate((p0, p1, p2, p3)):
            for half in range(2):
                at = 4 * k + 2 * half
                left = jnp.concatenate([panel[2 * half], panel[2 * half + 1]], axis=1)
                right = jnp.concatenate(
                    [
                        w[0, :, pl.ds(pl.multiple_of(cols[at + i] * share, share), share)]
                        for i in range(2)
                    ],
                    axis=1,
                )
                total[lows[at]] += contract(left, right)
        for low in range(2):
            bare = (2.0 * coulomb[...]) * mine[low].astype(jnp.float32)
            out[0, low] = (bare - total[low]).astype(out.dtype)

    @pl.when(pl.program_id(0) < 2)
    def _():
        run(w_own)

    @pl.when(pl.program_id(0) >= 2)
    def _():
        run(w_other)


def project(cols, lows, panels, mine, coulomb, w_own, w_other):
    rows, share = panels[0].shape[1:]
    whole = w_own.shape[2]
    fixed = lambda shape: pl.BlockSpec(shape, lambda q, *_: (0,) * len(shape))
    return pl.pallas_call(
        project_kernel,
        grid_spec=pltpu.PrefetchScalarGridSpec(
            num_scalar_prefetch=2,
            grid=(4,),
            in_specs=[fixed((4, rows, share))] * 4
            + [
                fixed((2, rows, share)),
                fixed((1, share)),
                pl.BlockSpec((1, share, whole), lambda q, *_: (jnp.minimum(q, 1), 0, 0)),
                pl.BlockSpec((1, share, whole), lambda q, *_: (jnp.maximum(q - 2, 0), 0, 0)),
            ],
            out_specs=pl.BlockSpec((1, 2, rows, share), lambda q, *_: (q, 0, 0, 0)),
            scratch_shapes=[pltpu.VMEM((2, rows, share), jnp.float32)],
        ),
        out_shape=jax.ShapeDtypeStruct((4, 2, rows, share), jnp.bfloat16),
        compiler_params=pltpu.CompilerParams(vmem_limit_bytes=VMEM),
        cost_estimate=pl.CostEstimate(
            flops=2 * 4 * 2 * rows * share * whole, bytes_accessed=15 << 20, transcendentals=0
        ),
        name="project",
    )(cols, lows, *panels, mine, coulomb, w_own, w_other)


def meet_kernel(starts, places, u, mine, other, out, left_rows):
    rows = mine.shape[1]
    for low in range(2):
        left_rows[pl.ds(low * rows, rows), :] = mine[low]
        left_rows[pl.ds((2 + low) * rows, rows), :] = other[low]
    lane = lax.broadcasted_iota(jnp.int32, (16, 128), 1) // 16
    for target in range(8):
        for two in range(2):
            left, right = [], []
            for q in (2 * two, 2 * two + 1):
                for i in range(4):
                    start = pl.multiple_of(starts[(q * 8 + target) * 4 + i], 16)
                    left.append(left_rows[pl.ds(start, 16), :])
                for i in range(2):
                    place = pl.multiple_of(places[(2 * target + i) % NZ] * 32, 32)
                    right.append(u[q, target // 4, pl.ds(place, 32), :])
            product = contract(jnp.concatenate(left, axis=0), jnp.concatenate(right, axis=0))
            block = jnp.zeros((16, 128), jnp.float32)
            for i in range(8):
                block = jnp.where(lane == i, product[16 * i : 16 * i + 16], block)
            out[target, two] = block


def meet(starts, places, u, mine, other):
    rows, share = mine.shape[1:]
    smem = pl.BlockSpec(memory_space=pltpu.SMEM)
    vmem = pl.BlockSpec(memory_space=pltpu.VMEM)
    return pl.pallas_call(
        meet_kernel,
        in_specs=[smem, smem, vmem, vmem, vmem],
        out_specs=vmem,
        out_shape=jax.ShapeDtypeStruct((8, 2, 16, 128), jnp.float32),
        scratch_shapes=[pltpu.VMEM((4 * rows, share), jnp.bfloat16)],
        compiler_params=pltpu.CompilerParams(vmem_limit_bytes=VMEM),
        name="meet",
    )(starts, places, u, mine, other)


def spread_kernel(mask, terms, out):
    lane = lax.broadcasted_iota(jnp.int32, (16, 128), 1)
    blocks = []
    for two in range(2):
        full = terms[0, two]
        for j in range(1, 8):
            full = full + terms[j, two]
        turned = pltpu.roll(full, 64, 1)
        blocks.append(jnp.where(lane < 64, full, turned))
        blocks.append(jnp.where(lane < 64, turned, full))
    for target in range(out.shape[0]):
        block = jnp.zeros((16, 128), jnp.float32)
        for q in range(4):
            block = jnp.where(mask[target, q : q + 1, :] > 0, blocks[q], block)
        out[target] = block.astype(out.dtype)


def spread(mask, terms):
    vmem = pl.BlockSpec(memory_space=pltpu.VMEM)
    return pl.pallas_call(
        spread_kernel,
        in_specs=[vmem, vmem],
        out_specs=vmem,
        out_shape=jax.ShapeDtypeStruct((32, 16, 128), jnp.float32),
        name="spread",
    )(mask, terms)


def settle_kernel(arrived, out):
    lane = lax.broadcasted_iota(jnp.int32, (16, 128), 1) // 32
    sums = []
    for c in range(2):
        full = arrived[c].astype(jnp.float32)
        for r in range(2 + c, arrived.shape[0], 2):
            full = full + arrived[r].astype(jnp.float32)
        sums.append(full)
    for k in range(2):
        block = jnp.zeros((16, 128), jnp.float32)
        for z in range(2):
            for c in range(2):
                move = (z * 64 + c * 32 - k * 64 - z * 32) % 128
                turned = pltpu.roll(sums[c], move, 1) if move else sums[c]
                block = jnp.where(lane == 2 * z + c, turned, block)
        out[16 * k : 16 * k + 16, :] = block


def settle(arrived):
    vmem = pl.BlockSpec(memory_space=pltpu.VMEM)
    return pl.pallas_call(
        settle_kernel,
        in_specs=[vmem],
        out_specs=vmem,
        out_shape=jax.ShapeDtypeStruct((32, 128), jnp.float32),
        name="settle",
    )(arrived)


def local(pair_matrix, screened, coulomb, q_index):
    bands, share = pair_matrix.shape[1:]
    r, j = lax.axis_index("row"), lax.axis_index("col")
    c, z, y_lo = r % 2, (r // 2) % NZ, r // 16
    x, y = j % NX, 2 * (j // NX) + y_lo

    shifts = jnp.array(SHIFTS, jnp.int32)
    first, second = shifts[None, :], shifts[:, None]
    xs = jnp.mod(x - jnp.where(c == 0, first, second), NX)
    ys = jnp.mod(y - jnp.where(c == 0, second, first), NY)
    cols = ((ys // 2) * NX + xs).reshape(-1).astype(jnp.int32)
    lows = jnp.broadcast_to(ys % 2, (4, 4)).reshape(-1).astype(jnp.int32)

    z_from = jnp.mod(
        jnp.stack([z, z ^ 1])[:, None] - jnp.array(ZSHIFTS, jnp.int32)[None, :], NZ
    ).reshape(-1)
    order = lax.iota(jnp.int32, NZ)
    places = jnp.sum(jnp.where(z_from[None, :] == order[:, None], order[None, :], 0), axis=1)

    q_mine = jnp.stack([2 * r, 2 * r + 1, 2 * (r ^ 1), 2 * (r ^ 1) + 1])
    slot = lax.iota(jnp.int32, 4)
    k_cols = 2 * (4 * lax.iota(jnp.int32, 8)[:, None] + 2 * (slot // 2) + c) + slot % 2
    chosen = jnp.take(q_index, k_cols.reshape(-1), axis=1)
    ks = lax.iota(jnp.int32, q_index.shape[0])
    partner = jnp.sum(
        jnp.where(chosen[None] == q_mine[:, None, None], ks[None, :, None], 0), axis=1
    )
    k_row = partner // 2
    z_place = jnp.sum(
        jnp.where((k_row // 2 % NZ)[..., None] == order, places, 0), axis=-1
    )
    starts = (
        (((k_row % 2) ^ c) * 2 + k_row // 16) * (NZ * 32) + z_place * 32 + (partner % 2) * 16
    )
    starts = starts.reshape(-1).astype(jnp.int32)

    my_cols = 2 * (4 * j + 2 * (slot // 2) + c) + slot % 2
    seen = jnp.take(q_index, my_cols, axis=1).reshape(32, 2, 4)
    mask = (seen[:, None] == q_mine[None, :, None, None]).astype(jnp.int32)
    mask = jnp.broadcast_to(mask[..., None], (32, 4, 2, 4, 16)).reshape(32, 4, 128)

    w_other = send(screened, SWAP)
    own = pair_matrix.reshape(1, 2 * bands, share)
    even = jnp.concatenate([own] + [send(own, along_z(s)) for s in ZSHIFTS[1:]], axis=0)
    stack = jnp.concatenate([even, send(even, ZPAIR)], axis=0).reshape(1, NZ * 32, share)
    parts = [send(stack, first_plane(s)) for s in SHIFTS[1:]]
    panel = jnp.concatenate([stack] + parts, axis=0)
    panels = [panel] + [send(panel, second_plane(s)) for s in SHIFTS[1:]]

    up = jnp.where(c == 0, panels[3][0], parts[2][0])
    down = jnp.where(c == 0, panels[2][0], parts[1][0])
    across = jnp.where(y_lo == 0, up, down)
    mine = jnp.stack(
        [jnp.where(y_lo == 0, stack[0], across), jnp.where(y_lo == 0, across, stack[0])]
    )
    other = send(mine, SWAP)

    u = project(cols, lows, panels, mine, coulomb.reshape(1, share), screened, w_other)
    terms = meet(starts, places.astype(jnp.int32), u, mine, other)
    terms = lax.all_to_all(terms, "col", split_axis=0, concat_axis=0, tiled=True)
    placed = spread(mask, terms)
    arrived = lax.all_to_all(placed, "row", split_axis=0, concat_axis=0, tiled=True)
    return settle(arrived)


def solution(mesh):
    placed = (P("row", None, "col"), P("row", "col", None), P("col"), P())
    return jax.shard_map(
        local, mesh=mesh, in_specs=placed, out_specs=P("row", "col"), check_vma=False
    )
```

```python
import jax
import jax.numpy as jnp
from jax import lax
from jax.experimental import pallas as pl
from jax.experimental.pallas import tpu as pltpu
from jax.sharding import PartitionSpec as P

AXES = ("row", "col")
NX, NY, NZ, NCORE = 4, 4, 8, 2
SHIFTS = (0, 2, 1, -1)
ZSHIFTS = (0, 2, -2, 4)
VMEM = 32 * 1024 * 1024


def device_index(x, y, z, c):
    y_hi, y_lo = divmod(y % NY, 2)
    row = (y_lo * NZ + z % NZ) * NCORE + c
    return row * 8 + y_hi * NX + x % NX


def pairs(move):
    found = []
    for x in range(NX):
        for y in range(NY):
            for z in range(NZ):
                for c in range(NCORE):
                    found.append((device_index(x, y, z, c), device_index(*move(x, y, z, c))))
    return found


SWAP = pairs(lambda x, y, z, c: (x, y, z, 1 - c))
ZPAIR = pairs(lambda x, y, z, c: (x, y, z ^ 1, c))


def along_z(s):
    return pairs(lambda x, y, z, c: (x, y, z + s, c))


def first_plane(s):
    return pairs(lambda x, y, z, c: (x + s, y, z, c) if c == 0 else (x, y + s, z, c))


def second_plane(s):
    return pairs(lambda x, y, z, c: (x, y + s, z, c) if c == 0 else (x + s, y, z, c))


def send(value, perm):
    return lax.ppermute(value, AXES, perm)


def contract(a, b):
    return lax.dot_general(a, b, (((1,), (1,)), ((), ())), preferred_element_type=jnp.float32)


def product(panel, half, w, spots):
    left = jnp.concatenate([panel[2 * half], panel[2 * half + 1]], axis=1)
    return contract(left, jnp.concatenate([w(spots[0]), w(spots[1])], axis=1))


def begin_kernel(cols, lows, panel, w_own, w_other, out, kept):
    share = panel.shape[2]

    def run(w):
        def block(at):
            return w[0, :, pl.ds(pl.multiple_of(cols[at] * share, share), share)]

        out[...] = jnp.zeros_like(out)
        for half in range(2):
            at = 2 * half
            out[0, lows[at]] -= product(panel, half, block, (at, at + 1))
        for i in range(4):
            kept[0, :, i * share : (i + 1) * share] = block(4 + i)

    @pl.when(pl.program_id(0) < 2)
    def _():
        run(w_own)

    @pl.when(pl.program_id(0) >= 2)
    def _():
        run(w_other)


def more_kernel(cols, lows, p2, p3, before, mine, coulomb, w_own, w_other, out):
    share = p2.shape[2]

    def run(w):
        def block(at):
            return w[0, :, pl.ds(pl.multiple_of(cols[at] * share, share), share)]

        for low in range(2):
            bare = (2.0 * coulomb[...]) * mine[low].astype(jnp.float32)
            out[0, low] = before[0, low] + bare
        for k, panel in ((2, p2), (3, p3)):
            for half in range(2):
                at = 4 * k + 2 * half
                out[0, lows[at]] -= product(panel, half, block, (at, at + 1))

    @pl.when(pl.program_id(0) < 2)
    def _():
        run(w_own)

    @pl.when(pl.program_id(0) >= 2)
    def _():
        run(w_other)


def fixed(shape):
    return pl.BlockSpec(shape, lambda q, *_: (0,) * len(shape))


def transfer_specs(share, whole):
    return [
        pl.BlockSpec((1, share, whole), lambda q, *_: (jnp.minimum(q, 1), 0, 0)),
        pl.BlockSpec((1, share, whole), lambda q, *_: (jnp.maximum(q - 2, 0), 0, 0)),
    ]


def begin(cols, lows, panel, w_own, w_other):
    rows, share = panel.shape[1:]
    whole = w_own.shape[2]
    return pl.pallas_call(
        begin_kernel,
        grid_spec=pltpu.PrefetchScalarGridSpec(
            num_scalar_prefetch=2,
            grid=(4,),
            in_specs=[fixed((4, rows, share))] + transfer_specs(share, whole),
            out_specs=[
                pl.BlockSpec((1, 2, rows, share), lambda q, *_: (q, 0, 0, 0)),
                pl.BlockSpec((1, share, 4 * share), lambda q, *_: (q, 0, 0)),
            ],
        ),
        out_shape=[
            jax.ShapeDtypeStruct((4, 2, rows, share), jnp.float32),
            jax.ShapeDtypeStruct((4, share, 4 * share), jnp.bfloat16),
        ],
        compiler_params=pltpu.CompilerParams(vmem_limit_bytes=VMEM),
        cost_estimate=pl.CostEstimate(
            flops=2 * 4 * 4 * rows * share * share, bytes_accessed=17 << 20, transcendentals=0
        ),
        name="begin",
    )(cols, lows, panel, w_own, w_other)


def more(cols, lows, p2, p3, before, mine, coulomb, w_own, w_other):
    rows, share = p2.shape[1:]
    whole = w_own.shape[2]
    total = pl.BlockSpec((1, 2, rows, share), lambda q, *_: (q, 0, 0, 0))
    return pl.pallas_call(
        more_kernel,
        grid_spec=pltpu.PrefetchScalarGridSpec(
            num_scalar_prefetch=2,
            grid=(4,),
            in_specs=[
                fixed((4, rows, share)),
                fixed((4, rows, share)),
                total,
                fixed((2, rows, share)),
                fixed((1, share)),
            ]
            + transfer_specs(share, whole),
            out_specs=total,
        ),
        out_shape=jax.ShapeDtypeStruct((4, 2, rows, share), jnp.float32),
        compiler_params=pltpu.CompilerParams(vmem_limit_bytes=VMEM),
        cost_estimate=pl.CostEstimate(
            flops=2 * 4 * 8 * rows * share * share, bytes_accessed=17 << 20, transcendentals=0
        ),
        name="more",
    )(cols, lows, p2, p3, before, mine, coulomb, w_own, w_other)


def finish_kernel(starts, places, lows, panel, before, kept, mine, other, out, left_rows, total, u):
    rows, share = mine.shape[1:]
    for low in range(2):
        left_rows[pl.ds(low * rows, rows), :] = mine[low]
        left_rows[pl.ds((2 + low) * rows, rows), :] = other[low]
    for q in range(4):
        total[...] = before[q]
        for half in range(2):
            left = jnp.concatenate([panel[2 * half], panel[2 * half + 1]], axis=1)
            right = kept[q, :, 2 * half * share : (2 * half + 2) * share]
            total[lows[4 + 2 * half]] -= contract(left, right)
        u[q] = total[...].astype(u.dtype)
    lane = lax.broadcasted_iota(jnp.int32, (16, 128), 1) // 16
    for target in range(8):
        for two in range(2):
            left, right = [], []
            for q in (2 * two, 2 * two + 1):
                for i in range(4):
                    start = pl.multiple_of(starts[(q * 8 + target) * 4 + i], 16)
                    left.append(left_rows[pl.ds(start, 16), :])
                for i in range(2):
                    place = pl.multiple_of(places[(2 * target + i) % NZ] * 32, 32)
                    right.append(u[q, target // 4, pl.ds(place, 32), :])
            met = contract(jnp.concatenate(left, axis=0), jnp.concatenate(right, axis=0))
            block = jnp.zeros((16, 128), jnp.float32)
            for i in range(8):
                block = jnp.where(lane == i, met[16 * i : 16 * i + 16], block)
            out[target, two] = block


def finish(starts, places, lows, panel, before, kept, mine, other):
    rows, share = mine.shape[1:]
    smem = pl.BlockSpec(memory_space=pltpu.SMEM)
    vmem = pl.BlockSpec(memory_space=pltpu.VMEM)
    return pl.pallas_call(
        finish_kernel,
        in_specs=[smem] * 3 + [vmem] * 5,
        out_specs=vmem,
        out_shape=jax.ShapeDtypeStruct((8, 2, 16, 128), jnp.float32),
        scratch_shapes=[
            pltpu.VMEM((4 * rows, share), jnp.bfloat16),
            pltpu.VMEM((2, rows, share), jnp.float32),
            pltpu.VMEM((4, 2, rows, share), jnp.bfloat16),
        ],
        compiler_params=pltpu.CompilerParams(vmem_limit_bytes=VMEM),
        cost_estimate=pl.CostEstimate(
            flops=2 * 4 * 4 * rows * share * share, bytes_accessed=9 << 20, transcendentals=0
        ),
        name="finish",
    )(starts, places, lows, panel, before, kept, mine, other)


def spread_kernel(mask, terms, out):
    lane = lax.broadcasted_iota(jnp.int32, (16, 128), 1)
    blocks = []
    for two in range(2):
        full = terms[0, two]
        for j in range(1, 8):
            full = full + terms[j, two]
        turned = pltpu.roll(full, 64, 1)
        blocks.append(jnp.where(lane < 64, full, turned))
        blocks.append(jnp.where(lane < 64, turned, full))
    for target in range(out.shape[0]):
        block = jnp.zeros((16, 128), jnp.float32)
        for q in range(4):
            block = jnp.where(mask[target, q : q + 1, :] > 0, blocks[q], block)
        out[target] = block.astype(out.dtype)


def spread(mask, terms):
    vmem = pl.BlockSpec(memory_space=pltpu.VMEM)
    return pl.pallas_call(
        spread_kernel,
        in_specs=[vmem, vmem],
        out_specs=vmem,
        out_shape=jax.ShapeDtypeStruct((32, 16, 128), jnp.float32),
        name="spread",
    )(mask, terms)


def settle_kernel(arrived, out):
    lane = lax.broadcasted_iota(jnp.int32, (16, 128), 1) // 32
    sums = []
    for c in range(2):
        full = arrived[c].astype(jnp.float32)
        for r in range(2 + c, arrived.shape[0], 2):
            full = full + arrived[r].astype(jnp.float32)
        sums.append(full)
    for k in range(2):
        block = jnp.zeros((16, 128), jnp.float32)
        for z in range(2):
            for c in range(2):
                move = (z * 64 + c * 32 - k * 64 - z * 32) % 128
                turned = pltpu.roll(sums[c], move, 1) if move else sums[c]
                block = jnp.where(lane == 2 * z + c, turned, block)
        out[16 * k : 16 * k + 16, :] = block


def settle(arrived):
    vmem = pl.BlockSpec(memory_space=pltpu.VMEM)
    return pl.pallas_call(
        settle_kernel,
        in_specs=[vmem],
        out_specs=vmem,
        out_shape=jax.ShapeDtypeStruct((32, 128), jnp.float32),
        name="settle",
    )(arrived)


def local(pair_matrix, screened, coulomb, q_index):
    bands, share = pair_matrix.shape[1:]
    r, j = lax.axis_index("row"), lax.axis_index("col")
    w_other = send(screened, SWAP)
    own = pair_matrix.reshape(1, 2 * bands, share)
    even = jnp.concatenate([own] + [send(own, along_z(s)) for s in ZSHIFTS[1:]], axis=0)
    stack = jnp.concatenate([even, send(even, ZPAIR)], axis=0).reshape(1, NZ * 32, share)
    parts = [send(stack, first_plane(s)) for s in SHIFTS[1:]]
    r, j, q_index, _ = lax.optimization_barrier((r, j, q_index, stack))
    c, z, y_lo = r % 2, (r // 2) % NZ, r // 16
    x, y = j % NX, 2 * (j // NX) + y_lo

    shifts = jnp.array(SHIFTS, jnp.int32)
    first, second = shifts[None, :], shifts[:, None]
    xs = jnp.mod(x - jnp.where(c == 0, first, second), NX)
    ys = jnp.mod(y - jnp.where(c == 0, second, first), NY)
    cols = ((ys // 2) * NX + xs).reshape(-1).astype(jnp.int32)
    lows = jnp.broadcast_to(ys % 2, (4, 4)).reshape(-1).astype(jnp.int32)

    z_from = jnp.mod(
        jnp.stack([z, z ^ 1])[:, None] - jnp.array(ZSHIFTS, jnp.int32)[None, :], NZ
    ).reshape(-1)
    order = lax.iota(jnp.int32, NZ)
    places = jnp.sum(jnp.where(z_from[None, :] == order[:, None], order[None, :], 0), axis=1)

    q_mine = jnp.stack([2 * r, 2 * r + 1, 2 * (r ^ 1), 2 * (r ^ 1) + 1])
    slot = lax.iota(jnp.int32, 4)
    k_cols = 2 * (4 * lax.iota(jnp.int32, 8)[:, None] + 2 * (slot // 2) + c) + slot % 2
    chosen = jnp.take(q_index, k_cols.reshape(-1), axis=1)
    ks = lax.iota(jnp.int32, q_index.shape[0])
    partner = jnp.sum(
        jnp.where(chosen[None] == q_mine[:, None, None], ks[None, :, None], 0), axis=1
    )
    k_row = partner // 2
    z_place = jnp.sum(
        jnp.where((k_row // 2 % NZ)[..., None] == order, places, 0), axis=-1
    )
    starts = (
        (((k_row % 2) ^ c) * 2 + k_row // 16) * (NZ * 32) + z_place * 32 + (partner % 2) * 16
    )
    starts = starts.reshape(-1).astype(jnp.int32)

    my_cols = 2 * (4 * j + 2 * (slot // 2) + c) + slot % 2
    seen = jnp.take(q_index, my_cols, axis=1).reshape(32, 2, 4)
    mask = (seen[:, None] == q_mine[None, :, None, None]).astype(jnp.int32)
    mask = jnp.broadcast_to(mask[..., None], (32, 4, 2, 4, 16)).reshape(32, 4, 128)

    panel = jnp.concatenate([stack] + parts, axis=0)
    panels = [panel] + [send(panel, second_plane(s)) for s in SHIFTS[1:]]

    up = jnp.where(c == 0, panels[3][0], parts[2][0])
    down = jnp.where(c == 0, panels[2][0], parts[1][0])
    across = jnp.where(y_lo == 0, up, down)
    mine = jnp.stack(
        [jnp.where(y_lo == 0, stack[0], across), jnp.where(y_lo == 0, across, stack[0])]
    )
    other = send(mine, SWAP)

    total, kept = begin(cols, lows, panel, screened, w_other)
    total = more(
        cols, lows, panels[2], panels[3], total, mine, coulomb.reshape(1, share), screened, w_other
    )
    terms = finish(
        starts, places.astype(jnp.int32), lows, panels[1], total, kept, mine, other
    )
    terms = lax.all_to_all(terms, "col", split_axis=0, concat_axis=0, tiled=True)
    placed = spread(mask, terms)
    arrived = lax.all_to_all(placed, "row", split_axis=0, concat_axis=0, tiled=True)
    return settle(arrived)


def solution(mesh):
    placed = (P("row", None, "col"), P("row", "col", None), P("col"), P())
    return jax.shard_map(
        local, mesh=mesh, in_specs=placed, out_specs=P("row", "col"), check_vma=False
    )
```

```python
import jax
import jax.numpy as jnp
from jax import lax
from jax.experimental import pallas as pl
from jax.experimental.pallas import tpu as pltpu
from jax.sharding import PartitionSpec as P

AXES = ("row", "col")
NX, NY, NZ, NCORE = 4, 4, 8, 2
SHIFTS = (0, 2, 1, -1)
ZSHIFTS = (0, 2, -2, 4)
VMEM = 32 * 1024 * 1024


def device_index(x, y, z, c):
    y_hi, y_lo = divmod(y % NY, 2)
    row = (y_lo * NZ + z % NZ) * NCORE + c
    return row * 8 + y_hi * NX + x % NX


def pairs(move):
    found = []
    for x in range(NX):
        for y in range(NY):
            for z in range(NZ):
                for c in range(NCORE):
                    found.append((device_index(x, y, z, c), device_index(*move(x, y, z, c))))
    return found


SWAP = pairs(lambda x, y, z, c: (x, y, z, 1 - c))
ZPAIR = pairs(lambda x, y, z, c: (x, y, z ^ 1, c))


def along_z(s):
    return pairs(lambda x, y, z, c: (x, y, z + s, c))


def first_plane(s):
    return pairs(lambda x, y, z, c: (x + s, y, z, c) if c == 0 else (x, y + s, z, c))


def second_plane(s):
    return pairs(lambda x, y, z, c: (x, y + s, z, c) if c == 0 else (x + s, y, z, c))


def send(value, perm):
    return lax.ppermute(value, AXES, perm)


def contract(a, b):
    return lax.dot_general(a, b, (((1,), (1,)), ((), ())), preferred_element_type=jnp.float32)


def product(panel, half, w, spots):
    left = jnp.concatenate([panel[2 * half], panel[2 * half + 1]], axis=1)
    return contract(left, jnp.concatenate([w(spots[0]), w(spots[1])], axis=1))


def begin_kernel(cols, lows, panel, w_own, w_other, out, kept):
    share = panel.shape[2]

    def run(w):
        def block(at):
            return w[0, :, pl.ds(pl.multiple_of(cols[at] * share, share), share)]

        out[...] = jnp.zeros_like(out)
        for half in range(2):
            at = 2 * half
            out[0, lows[at]] -= product(panel, half, block, (at, at + 1))
        for i in range(4):
            kept[0, :, i * share : (i + 1) * share] = block(4 + i)

    @pl.when(pl.program_id(0) < 2)
    def _():
        run(w_own)

    @pl.when(pl.program_id(0) >= 2)
    def _():
        run(w_other)


def more_kernel(cols, lows, p2, p3, before, mine, coulomb, w_own, w_other, out):
    share = p2.shape[2]

    def run(w):
        def block(at):
            return w[0, :, pl.ds(pl.multiple_of(cols[at] * share, share), share)]

        for low in range(2):
            bare = (2.0 * coulomb[...]) * mine[low].astype(jnp.float32)
            out[0, low] = before[0, low] + bare
        for k, panel in ((2, p2), (3, p3)):
            for half in range(2):
                at = 4 * k + 2 * half
                out[0, lows[at]] -= product(panel, half, block, (at, at + 1))

    @pl.when(pl.program_id(0) < 2)
    def _():
        run(w_own)

    @pl.when(pl.program_id(0) >= 2)
    def _():
        run(w_other)


def fixed(shape):
    return pl.BlockSpec(shape, lambda q, *_: (0,) * len(shape))


def transfer_specs(share, whole):
    return [
        pl.BlockSpec((1, share, whole), lambda q, *_: (jnp.minimum(q, 1), 0, 0)),
        pl.BlockSpec((1, share, whole), lambda q, *_: (jnp.maximum(q - 2, 0), 0, 0)),
    ]


def begin(cols, lows, panel, w_own, w_other):
    rows, share = panel.shape[1:]
    whole = w_own.shape[2]
    return pl.pallas_call(
        begin_kernel,
        grid_spec=pltpu.PrefetchScalarGridSpec(
            num_scalar_prefetch=2,
            grid=(4,),
            in_specs=[fixed((4, rows, share))] + transfer_specs(share, whole),
            out_specs=[
                pl.BlockSpec((1, 2, rows, share), lambda q, *_: (q, 0, 0, 0)),
                pl.BlockSpec((1, share, 4 * share), lambda q, *_: (q, 0, 0)),
            ],
        ),
        out_shape=[
            jax.ShapeDtypeStruct((4, 2, rows, share), jnp.float32),
            jax.ShapeDtypeStruct((4, share, 4 * share), jnp.bfloat16),
        ],
        compiler_params=pltpu.CompilerParams(vmem_limit_bytes=VMEM),
        cost_estimate=pl.CostEstimate(
            flops=2 * 4 * 4 * rows * share * share, bytes_accessed=17 << 20, transcendentals=0
        ),
        name="begin",
    )(cols, lows, panel, w_own, w_other)


def more(cols, lows, p2, p3, before, mine, coulomb, w_own, w_other):
    rows, share = p2.shape[1:]
    whole = w_own.shape[2]
    total = pl.BlockSpec((1, 2, rows, share), lambda q, *_: (q, 0, 0, 0))
    return pl.pallas_call(
        more_kernel,
        grid_spec=pltpu.PrefetchScalarGridSpec(
            num_scalar_prefetch=2,
            grid=(4,),
            in_specs=[
                fixed((4, rows, share)),
                fixed((4, rows, share)),
                total,
                fixed((2, rows, share)),
                fixed((1, share)),
            ]
            + transfer_specs(share, whole),
            out_specs=total,
        ),
        out_shape=jax.ShapeDtypeStruct((4, 2, rows, share), jnp.float32),
        compiler_params=pltpu.CompilerParams(vmem_limit_bytes=VMEM),
        cost_estimate=pl.CostEstimate(
            flops=2 * 4 * 8 * rows * share * share, bytes_accessed=17 << 20, transcendentals=0
        ),
        name="more",
    )(cols, lows, p2, p3, before, mine, coulomb, w_own, w_other)


def finish_kernel(starts, places, lows, panel, before, kept, mine, other, out, left_rows, total, u):
    rows, share = mine.shape[1:]
    for low in range(2):
        left_rows[pl.ds(low * rows, rows), :] = mine[low]
        left_rows[pl.ds((2 + low) * rows, rows), :] = other[low]
    for q in range(4):
        total[...] = before[q]
        for half in range(2):
            left = jnp.concatenate([panel[2 * half], panel[2 * half + 1]], axis=1)
            right = kept[q, :, 2 * half * share : (2 * half + 2) * share]
            total[lows[4 + 2 * half]] -= contract(left, right)
        u[q] = total[...].astype(u.dtype)
    lane = lax.broadcasted_iota(jnp.int32, (16, 128), 1) // 16
    for target in range(8):
        for two in range(2):
            left, right = [], []
            for q in (2 * two, 2 * two + 1):
                for i in range(4):
                    start = pl.multiple_of(starts[(q * 8 + target) * 4 + i], 16)
                    left.append(left_rows[pl.ds(start, 16), :])
                for i in range(2):
                    place = pl.multiple_of(places[(2 * target + i) % NZ] * 32, 32)
                    right.append(u[q, target // 4, pl.ds(place, 32), :])
            met = contract(jnp.concatenate(left, axis=0), jnp.concatenate(right, axis=0))
            block = jnp.zeros((16, 128), jnp.float32)
            for i in range(8):
                block = jnp.where(lane == i, met[16 * i : 16 * i + 16], block)
            out[target, two] = block


def finish(starts, places, lows, panel, before, kept, mine, other):
    rows, share = mine.shape[1:]
    smem = pl.BlockSpec(memory_space=pltpu.SMEM)
    vmem = pl.BlockSpec(memory_space=pltpu.VMEM)
    return pl.pallas_call(
        finish_kernel,
        in_specs=[smem] * 3 + [vmem] * 5,
        out_specs=vmem,
        out_shape=jax.ShapeDtypeStruct((8, 2, 16, 128), jnp.float32),
        scratch_shapes=[
            pltpu.VMEM((4 * rows, share), jnp.bfloat16),
            pltpu.VMEM((2, rows, share), jnp.float32),
            pltpu.VMEM((4, 2, rows, share), jnp.bfloat16),
        ],
        compiler_params=pltpu.CompilerParams(vmem_limit_bytes=VMEM),
        cost_estimate=pl.CostEstimate(
            flops=2 * 4 * 4 * rows * share * share, bytes_accessed=9 << 20, transcendentals=0
        ),
        name="finish",
    )(starts, places, lows, panel, before, kept, mine, other)


def spread_kernel(mask, terms, out):
    lane = lax.broadcasted_iota(jnp.int32, (16, 128), 1)
    blocks = []
    for two in range(2):
        full = terms[0, two]
        for j in range(1, 8):
            full = full + terms[j, two]
        turned = pltpu.roll(full, 64, 1)
        blocks.append(jnp.where(lane < 64, full, turned))
        blocks.append(jnp.where(lane < 64, turned, full))
    for target in range(out.shape[0]):
        block = jnp.zeros((16, 128), jnp.float32)
        for q in range(4):
            block = jnp.where(mask[target, q : q + 1, :] > 0, blocks[q], block)
        out[target] = block.astype(out.dtype)


def spread(mask, terms):
    vmem = pl.BlockSpec(memory_space=pltpu.VMEM)
    return pl.pallas_call(
        spread_kernel,
        in_specs=[vmem, vmem],
        out_specs=vmem,
        out_shape=jax.ShapeDtypeStruct((32, 16, 128), jnp.float32),
        name="spread",
    )(mask, terms)


def settle_kernel(arrived, out):
    lane = lax.broadcasted_iota(jnp.int32, (16, 128), 1) // 32
    sums = []
    for c in range(2):
        full = arrived[c].astype(jnp.float32)
        for r in range(2 + c, arrived.shape[0], 2):
            full = full + arrived[r].astype(jnp.float32)
        sums.append(full)
    for k in range(2):
        block = jnp.zeros((16, 128), jnp.float32)
        for z in range(2):
            for c in range(2):
                move = (z * 64 + c * 32 - k * 64 - z * 32) % 128
                turned = pltpu.roll(sums[c], move, 1) if move else sums[c]
                block = jnp.where(lane == 2 * z + c, turned, block)
        out[16 * k : 16 * k + 16, :] = block


def settle(arrived):
    vmem = pl.BlockSpec(memory_space=pltpu.VMEM)
    return pl.pallas_call(
        settle_kernel,
        in_specs=[vmem],
        out_specs=vmem,
        out_shape=jax.ShapeDtypeStruct((32, 128), jnp.float32),
        name="settle",
    )(arrived)


def local(pair_matrix, screened, coulomb, q_index):
    bands, share = pair_matrix.shape[1:]
    r, j = lax.axis_index("row"), lax.axis_index("col")
    w_other = send(screened, SWAP)
    own = pair_matrix.reshape(1, 2 * bands, share)
    even = jnp.concatenate([own] + [send(own, along_z(s)) for s in ZSHIFTS[1:]], axis=0)
    stack = jnp.concatenate([even, send(even, ZPAIR)], axis=0).reshape(1, NZ * 32, share)
    parts = [send(stack, first_plane(s)) for s in SHIFTS[1:]]
    r, j, q_index, _ = lax.optimization_barrier((r, j, q_index, stack))
    c, z, y_lo = r % 2, (r // 2) % NZ, r // 16
    x, y = j % NX, 2 * (j // NX) + y_lo

    shifts = jnp.array(SHIFTS, jnp.int32)
    first, second = shifts[None, :], shifts[:, None]
    xs = jnp.mod(x - jnp.where(c == 0, first, second), NX)
    ys = jnp.mod(y - jnp.where(c == 0, second, first), NY)
    cols = ((ys // 2) * NX + xs).reshape(-1).astype(jnp.int32)
    lows = jnp.broadcast_to(ys % 2, (4, 4)).reshape(-1).astype(jnp.int32)

    z_from = jnp.mod(
        jnp.stack([z, z ^ 1])[:, None] - jnp.array(ZSHIFTS, jnp.int32)[None, :], NZ
    ).reshape(-1)
    order = lax.iota(jnp.int32, NZ)
    places = jnp.sum(jnp.where(z_from[None, :] == order[:, None], order[None, :], 0), axis=1)

    q_mine = jnp.stack([2 * r, 2 * r + 1, 2 * (r ^ 1), 2 * (r ^ 1) + 1])
    slot = lax.iota(jnp.int32, 4)
    k_cols = 2 * (4 * lax.iota(jnp.int32, 8)[:, None] + 2 * (slot // 2) + c) + slot % 2
    chosen = jnp.take(q_index, k_cols.reshape(-1), axis=1)
    ks = lax.iota(jnp.int32, q_index.shape[0])
    partner = jnp.sum(
        jnp.where(chosen[None] == q_mine[:, None, None], ks[None, :, None], 0), axis=1
    )
    k_row = partner // 2
    z_place = jnp.sum(
        jnp.where((k_row // 2 % NZ)[..., None] == order, places, 0), axis=-1
    )
    starts = (
        (((k_row % 2) ^ c) * 2 + k_row // 16) * (NZ * 32) + z_place * 32 + (partner % 2) * 16
    )
    starts = starts.reshape(-1).astype(jnp.int32)

    my_cols = 2 * (4 * j + 2 * (slot // 2) + c) + slot % 2
    seen = jnp.take(q_index, my_cols, axis=1).reshape(32, 2, 4)
    mask = (seen[:, None] == q_mine[None, :, None, None]).astype(jnp.int32)
    mask = jnp.broadcast_to(mask[..., None], (32, 4, 2, 4, 16)).reshape(32, 4, 128)

    panel = jnp.concatenate([stack] + parts, axis=0)
    panels = [panel] + [send(panel, second_plane(s)) for s in SHIFTS[1:]]

    total, kept = begin(cols, lows, panel, screened, w_other)
    total, panels[2], panels[3] = lax.optimization_barrier((total, panels[2], panels[3]))
    up = jnp.where(c == 0, panels[3][0], parts[2][0])
    down = jnp.where(c == 0, panels[2][0], parts[1][0])
    across = jnp.where(y_lo == 0, up, down)
    mine = jnp.stack(
        [jnp.where(y_lo == 0, stack[0], across), jnp.where(y_lo == 0, across, stack[0])]
    )
    other = send(mine, SWAP)

    total = more(
        cols, lows, panels[2], panels[3], total, mine, coulomb.reshape(1, share), screened, w_other
    )
    terms = finish(
        starts, places.astype(jnp.int32), lows, panels[1], total, kept, mine, other
    )
    terms = lax.all_to_all(terms, "col", split_axis=0, concat_axis=0, tiled=True)
    placed = spread(mask, terms)
    arrived = lax.all_to_all(placed, "row", split_axis=0, concat_axis=0, tiled=True)
    return settle(arrived)


def solution(mesh):
    placed = (P("row", None, "col"), P("row", "col", None), P("col"), P())
    return jax.shard_map(
        local, mesh=mesh, in_specs=placed, out_specs=P("row", "col"), check_vma=False
    )
```

```python
import jax
import jax.numpy as jnp
from jax import lax
from jax.experimental import pallas as pl
from jax.experimental.pallas import tpu as pltpu
from jax.sharding import PartitionSpec as P

AXES = ("row", "col")
NX, NY, NZ, NCORE = 4, 4, 8, 2
SHIFTS = (0, 2, 1, -1)
ZSHIFTS = (0, 2, 4, -2)
VMEM = 48 * 1024 * 1024


def device_index(x, y, z, c):
    y_hi, y_lo = divmod(y % NY, 2)
    row = (y_lo * NZ + z % NZ) * NCORE + c
    return row * 8 + y_hi * NX + x % NX


def pairs(move):
    found = []
    for x in range(NX):
        for y in range(NY):
            for z in range(NZ):
                for c in range(NCORE):
                    found.append((device_index(x, y, z, c), device_index(*move(x, y, z, c))))
    return found


SWAP = pairs(lambda x, y, z, c: (x, y, z, 1 - c))
ZPAIR = pairs(lambda x, y, z, c: (x, y, z ^ 1, c))


def along_z(s):
    return pairs(lambda x, y, z, c: (x, y, z + s, c))


def first_plane(s):
    return pairs(lambda x, y, z, c: (x + s, y, z, c) if c == 0 else (x, y + s, z, c))


def second_plane(s):
    return pairs(lambda x, y, z, c: (x, y + s, z, c) if c == 0 else (x + s, y, z, c))


def send(value, perm):
    return lax.ppermute(value, AXES, perm)


def contract(a, b):
    return lax.dot_general(a, b, (((1,), (1,)), ((), ())), preferred_element_type=jnp.float32)


def where_am_i():
    r, j = lax.axis_index("row"), lax.axis_index("col")
    return r, j, r & 1, (r >> 1) & 7, r >> 4


def spot(k, i):
    r, j, c, _, y_lo = where_am_i()
    first, second = SHIFTS[i], SHIFTS[k]
    x = ((j & 3) - first - c * (second - first)) & 3
    y = (2 * (j >> 2) + y_lo - second - c * (first - second)) & 3
    return (y >> 1) * NX + x, y & 1


def place_of(z_wanted):
    z = where_am_i()[3]
    side = (z ^ z_wanted) & 1
    return side * 4 + ((((z ^ side) - z_wanted) & 7) >> 1)


def product(pieces, w, share, k, pair):
    right = []
    for i in (2 * pair, 2 * pair + 1):
        start = pl.multiple_of(spot(k, i)[0] * share, share)
        right.append(w[0, :, pl.ds(start, share)])
    left = jnp.concatenate([pieces[0], pieces[1]], axis=1)
    return spot(k, 2 * pair)[1], contract(left, jnp.concatenate(right, axis=1))


def for_each_w(run, w_own, w_other):
    @pl.when(pl.program_id(0) < 2)
    def _():
        run(w_own)

    @pl.when(pl.program_id(0) >= 2)
    def _():
        run(w_other)


def begin_kernel(p01, p23, w_own, w_other, out, kept):
    share = p01.shape[2]

    def run(w):
        out[...] = jnp.zeros_like(out)
        for pair, pieces in enumerate((p01, p23)):
            low, term = product(pieces, w, share, 0, pair)
            out[0, low] -= term
        for i in range(4):
            start = pl.multiple_of(spot(1, i)[0] * share, share)
            kept[0, :, i * share : (i + 1) * share] = w[0, :, pl.ds(start, share)]

    for_each_w(run, w_own, w_other)


def more_kernel(f0, f1, g0, g1, before, mine, coulomb, w_own, w_other, out):
    share = f0.shape[2]

    def run(w):
        for low in range(2):
            bare = (2.0 * coulomb[...]) * mine[low].astype(jnp.float32)
            out[0, low] = before[0, low] + bare
        for k, pair, pieces in ((2, 0, f0), (2, 1, f1), (3, 0, g0), (3, 1, g1)):
            low, term = product(pieces, w, share, k, pair)
            out[0, low] -= term

    for_each_w(run, w_own, w_other)


def fixed(shape):
    return pl.BlockSpec(shape, lambda q: (0,) * len(shape))


def w_specs(share, whole):
    return [
        pl.BlockSpec((1, share, whole), lambda q: (jnp.minimum(q, 1), 0, 0)),
        pl.BlockSpec((1, share, whole), lambda q: (jnp.maximum(q - 2, 0), 0, 0)),
    ]


def cost(pieces, rows, share, reads):
    return pl.CostEstimate(
        flops=2 * 4 * pieces * rows * share * share, bytes_accessed=reads << 20, transcendentals=0
    )


def begin(p01, p23, w_own, w_other):
    rows, share = p01.shape[1:]
    return pl.pallas_call(
        begin_kernel,
        grid=(4,),
        in_specs=[fixed((2, rows, share))] * 2 + w_specs(share, w_own.shape[2]),
        out_specs=[
            pl.BlockSpec((1, 2, rows, share), lambda q: (q, 0, 0, 0)),
            pl.BlockSpec((1, share, 4 * share), lambda q: (q, 0, 0)),
        ],
        out_shape=[
            jax.ShapeDtypeStruct((4, 2, rows, share), jnp.float32),
            jax.ShapeDtypeStruct((4, share, 4 * share), jnp.bfloat16),
        ],
        compiler_params=pltpu.CompilerParams(vmem_limit_bytes=VMEM),
        cost_estimate=cost(4, rows, share, 17),
        name="begin",
    )(p01, p23, w_own, w_other)


def more(f0, f1, g0, g1, before, mine, coulomb, w_own, w_other):
    rows, share = f0.shape[1:]
    total = pl.BlockSpec((1, 2, rows, share), lambda q: (q, 0, 0, 0))
    return pl.pallas_call(
        more_kernel,
        grid=(4,),
        in_specs=[fixed((2, rows, share))] * 4
        + [total, fixed((2, rows, share)), fixed((1, share))]
        + w_specs(share, w_own.shape[2]),
        out_specs=total,
        out_shape=jax.ShapeDtypeStruct((4, 2, rows, share), jnp.float32),
        compiler_params=pltpu.CompilerParams(vmem_limit_bytes=VMEM),
        cost_estimate=cost(8, rows, share, 17),
        name="more",
    )(f0, f1, g0, g1, before, mine, coulomb, w_own, w_other)


def finish_kernel(partner, p01, p23, before, kept, mine, other, out, left_rows, total, u):
    rows, share = mine.shape[1:]
    c = where_am_i()[2]
    for low in range(2):
        left_rows[pl.ds(low * rows, rows), :] = mine[low]
        left_rows[pl.ds((2 + low) * rows, rows), :] = other[low]
    for q in range(4):
        total[...] = before[q]
        for pair, pieces in enumerate((p01, p23)):
            left = jnp.concatenate([pieces[0], pieces[1]], axis=1)
            right = kept[q, :, 2 * pair * share : (2 * pair + 2) * share]
            total[spot(1, 2 * pair)[1]] -= contract(left, right)
        u[q] = total[...].astype(u.dtype)
    lane = lax.broadcasted_iota(jnp.int32, (16, 128), 1) // 16
    for target in range(8):
        places = [place_of((2 * target + i) % NZ) for i in range(2)]
        for two in range(2):
            left, right = [], []
            for q in (2 * two, 2 * two + 1):
                for i in range(4):
                    k = partner[q, 8 * target + 4 * (i // 2) + 2 * c + i % 2]
                    block = ((((k >> 1) & 1) ^ c) * 2 + (k >> 5)) * NZ + place_of((k >> 2) & 7)
                    start = pl.multiple_of(block * 32 + (k & 1) * 16, 16)
                    left.append(left_rows[pl.ds(start, 16), :])
                for place in places:
                    right.append(u[q, target // 4, pl.ds(pl.multiple_of(place * 32, 32), 32), :])
            met = contract(jnp.concatenate(left, axis=0), jnp.concatenate(right, axis=0))
            block = jnp.zeros((16, 128), jnp.float32)
            for i in range(8):
                block = jnp.where(lane == i, met[16 * i : 16 * i + 16], block)
            out[target, two] = block


def finish(partner, p01, p23, before, kept, mine, other):
    rows, share = mine.shape[1:]
    vmem = pl.BlockSpec(memory_space=pltpu.VMEM)
    return pl.pallas_call(
        finish_kernel,
        in_specs=[pl.BlockSpec(memory_space=pltpu.SMEM)] + [vmem] * 6,
        out_specs=vmem,
        out_shape=jax.ShapeDtypeStruct((8, 2, 16, 128), jnp.float32),
        scratch_shapes=[
            pltpu.VMEM((4 * rows, share), jnp.bfloat16),
            pltpu.VMEM((2, rows, share), jnp.float32),
            pltpu.VMEM((4, 2, rows, share), jnp.bfloat16),
        ],
        compiler_params=pltpu.CompilerParams(vmem_limit_bytes=VMEM),
        cost_estimate=cost(4, rows, share, 9),
        name="finish",
    )(partner, p01, p23, before, kept, mine, other)


def spread_kernel(q_index, terms, out):
    r, j, c, _, _ = where_am_i()
    ks = q_index.shape[0]
    row = lax.broadcasted_iota(jnp.int32, (ks, 128), 0)
    col = lax.broadcasted_iota(jnp.int32, (ks, 128), 1)
    slot = (col & 63) >> 4
    hit = row == 8 * j + 4 * (slot >> 1) + 2 * c + (slot & 1)
    seen = jnp.zeros((ks // 2, 128), jnp.float32)
    for k in range(2):
        rows = q_index[pl.ds(k, ks // 2, stride=2), :].astype(jnp.float32).astype(jnp.bfloat16)
        pick = jnp.where(hit & (col >> 6 == k), 1.0, 0.0).astype(jnp.bfloat16)
        seen = seen + jnp.dot(rows, pick, preferred_element_type=jnp.float32)
    seen = seen.astype(jnp.int32)
    lane = lax.broadcasted_iota(jnp.int32, (16, 128), 1)
    blocks = []
    for two in range(2):
        full = terms[0, two]
        for i in range(1, 8):
            full = full + terms[i, two]
        turned = pltpu.roll(full, 64, 1)
        blocks.append(jnp.where(lane < 64, full, turned))
        blocks.append(jnp.where(lane < 64, turned, full))
    mine = (2 * r, 2 * r + 1, 2 * (r ^ 1), 2 * (r ^ 1) + 1)
    for target in range(out.shape[0]):
        wanted = jnp.broadcast_to(seen[target : target + 1, :], (16, 128))
        block = jnp.zeros((16, 128), jnp.float32)
        for q in range(4):
            block = jnp.where(wanted == mine[q], blocks[q], block)
        out[target] = block.astype(out.dtype)


def spread(q_index, terms):
    vmem = pl.BlockSpec(memory_space=pltpu.VMEM)
    return pl.pallas_call(
        spread_kernel,
        in_specs=[vmem, vmem],
        out_specs=vmem,
        out_shape=jax.ShapeDtypeStruct((32, 16, 128), jnp.float32),
        name="spread",
    )(q_index, terms)


def settle_kernel(arrived, out):
    lane = lax.broadcasted_iota(jnp.int32, (16, 128), 1) // 32
    sums = []
    for c in range(2):
        full = arrived[c].astype(jnp.float32)
        for r in range(2 + c, arrived.shape[0], 2):
            full = full + arrived[r].astype(jnp.float32)
        sums.append(full)
    for k in range(2):
        block = jnp.zeros((16, 128), jnp.float32)
        for z in range(2):
            for c in range(2):
                move = (z * 64 + c * 32 - k * 64 - z * 32) % 128
                turned = pltpu.roll(sums[c], move, 1) if move else sums[c]
                block = jnp.where(lane == 2 * z + c, turned, block)
        out[16 * k : 16 * k + 16, :] = block


def settle(arrived):
    vmem = pl.BlockSpec(memory_space=pltpu.VMEM)
    return pl.pallas_call(
        settle_kernel,
        in_specs=[vmem],
        out_specs=vmem,
        out_shape=jax.ShapeDtypeStruct((32, 128), jnp.float32),
        name="settle",
    )(arrived)


def local(pair_matrix, screened, coulomb, q_index):
    bands, share = pair_matrix.shape[1:]
    r, _, c, _, y_lo = where_am_i()
    w_other = send(screened, SWAP)
    own = pair_matrix.reshape(1, 2 * bands, share)
    even = jnp.concatenate([own] + [send(own, along_z(s)) for s in ZSHIFTS[1:]], axis=0)
    stack = jnp.concatenate([even, send(even, ZPAIR)], axis=0).reshape(1, NZ * 32, share)
    parts = [send(stack, first_plane(s)) for s in SHIFTS[1:]]
    p01 = jnp.concatenate([stack, parts[0]], axis=0)
    p23 = jnp.concatenate([parts[1], parts[2]], axis=0)

    f0 = send(p01, second_plane(1))
    g1 = send(p23, second_plane(-1))
    f1 = send(p23, second_plane(1))
    g0 = send(p01, second_plane(-1))
    ff0 = send(f0, second_plane(1))
    gg1 = send(g1, second_plane(-1))

    q_mine = jnp.stack([2 * r, 2 * r + 1, 2 * (r ^ 1), 2 * (r ^ 1) + 1])
    ks = lax.iota(jnp.int32, q_index.shape[0])
    partner = jnp.sum(
        jnp.where(q_index[None] == q_mine[:, None, None], ks[None, :, None], 0), axis=1
    )

    total, kept = begin(p01, p23, screened, w_other)
    total, f1, g0 = lax.optimization_barrier((total, f1, g0))
    up = jnp.where(c == 0, g0[0], parts[2][0])
    down = jnp.where(c == 0, f0[0], parts[1][0])
    across = jnp.where(y_lo == 0, up, down)
    mine = jnp.stack(
        [jnp.where(y_lo == 0, stack[0], across), jnp.where(y_lo == 0, across, stack[0])]
    )
    other = send(mine, SWAP)

    total = more(f0, f1, g0, g1, total, mine, coulomb.reshape(1, share), screened, w_other)
    terms = finish(partner.astype(jnp.int32), ff0, gg1, total, kept, mine, other)
    terms = lax.all_to_all(terms, "col", split_axis=0, concat_axis=0, tiled=True)
    placed = spread(q_index, terms)
    arrived = lax.all_to_all(placed, "row", split_axis=0, concat_axis=0, tiled=True)
    return settle(arrived)


def solution(mesh):
    placed = (P("row", None, "col"), P("row", "col", None), P("col"), P())
    return jax.shard_map(
        local, mesh=mesh, in_specs=placed, out_specs=P("row", "col"), check_vma=False
    )
```

```python
import jax
import jax.numpy as jnp
from jax import lax
from jax.experimental import pallas as pl
from jax.experimental.pallas import tpu as pltpu
from jax.sharding import PartitionSpec as P

AXES = ("row", "col")
NX, NY, NZ, NCORE = 4, 4, 8, 2
SHIFTS = (0, 2, 1, -1)
ZSHIFTS = (0, 2, 4, -2)
VMEM = 24 * 1024 * 1024


def device_index(x, y, z, c):
    y_hi, y_lo = divmod(y % NY, 2)
    row = (y_lo * NZ + z % NZ) * NCORE + c
    return row * 8 + y_hi * NX + x % NX


def pairs(move):
    found = []
    for x in range(NX):
        for y in range(NY):
            for z in range(NZ):
                for c in range(NCORE):
                    found.append((device_index(x, y, z, c), device_index(*move(x, y, z, c))))
    return found


SWAP = pairs(lambda x, y, z, c: (x, y, z, 1 - c))
ZPAIR = pairs(lambda x, y, z, c: (x, y, z ^ 1, c))


def along_z(s):
    return pairs(lambda x, y, z, c: (x, y, z + s, c))


def first_plane(s):
    return pairs(lambda x, y, z, c: (x + s, y, z, c) if c == 0 else (x, y + s, z, c))


def second_plane(s):
    return pairs(lambda x, y, z, c: (x, y + s, z, c) if c == 0 else (x + s, y, z, c))


def send(value, perm):
    return lax.ppermute(value, AXES, perm)


def contract(a, b):
    return lax.dot_general(a, b, (((1,), (1,)), ((), ())), preferred_element_type=jnp.float32)


def where_am_i():
    r, j = lax.axis_index("row"), lax.axis_index("col")
    return r, j, r & 1, (r >> 1) & 7, r >> 4


def spot(k, i):
    r, j, c, _, y_lo = where_am_i()
    first, second = SHIFTS[i], SHIFTS[k]
    x = ((j & 3) - first - c * (second - first)) & 3
    y = (2 * (j >> 2) + y_lo - second - c * (first - second)) & 3
    return (y >> 1) * NX + x, y & 1


def place_of(z_wanted):
    z = where_am_i()[3]
    side = (z ^ z_wanted) & 1
    return side * 4 + ((((z ^ side) - z_wanted) & 7) >> 1)


def load_kernel(own, other, out, sems):
    copies = [
        pltpu.make_async_copy(own, out.at[pl.ds(0, 2)], sems.at[0]),
        pltpu.make_async_copy(other, out.at[pl.ds(2, 2)], sems.at[1]),
    ]
    for copy in copies:
        copy.start()
    for copy in copies:
        copy.wait()


def load(own, other):
    _, share, whole = own.shape
    return pl.pallas_call(
        load_kernel,
        in_specs=[pl.BlockSpec(memory_space=pl.ANY)] * 2,
        out_specs=pl.BlockSpec(memory_space=pltpu.VMEM),
        out_shape=jax.ShapeDtypeStruct((4, share, whole), own.dtype),
        scratch_shapes=[pltpu.SemaphoreType.DMA((2,))],
        compiler_params=pltpu.CompilerParams(vmem_limit_bytes=VMEM),
        cost_estimate=pl.CostEstimate(
            flops=0, bytes_accessed=8 * share * whole * 2, transcendentals=0
        ),
        name="load",
    )(own, other)


def solve_kernel(
    partner, coulomb, w, p01, p23, f0, f1, g0, g1, ff0, gg1, other, out, panel, left_rows, image
):
    rows, share = p01.shape[1:]
    r, j, c, _, _ = where_am_i()
    starts = [pl.multiple_of(place_of(z) * 32, 32) for z in range(NZ)]
    arrays = ((p01, p23), (ff0, gg1), (f0, f1), (g0, g1))
    for k in range(4):
        for i in range(4):
            col, low = spot(k, i)
            for z in range(NZ):
                to = pl.multiple_of(low * rows + z * 32, 32)
                piece = arrays[k][i // 2][i % 2, pl.ds(starts[z], 32), :]
                panel[pl.ds(to, 32), pl.ds(pl.multiple_of(col * share, share), share)] = piece
    left_rows[: 2 * rows, :] = panel[:, pl.ds(pl.multiple_of(j * share, share), share)]
    for low in range(2):
        for z in range(NZ):
            to = (2 + low) * rows + z * 32
            left_rows[to : to + 32, :] = other[low, pl.ds(starts[z], 32), :]
    for q in range(4):
        image[q] = contract(w[q], panel[...]).astype(image.dtype)

    lane = lax.broadcasted_iota(jnp.int32, (16, 128), 1)
    twice = 2.0 * coulomb[...]
    for pair in range(4):
        columns = left_rows[128 * pair : 128 * pair + 128, :]
        blocks = []
        for q in range(4):
            left = []
            for i in range(8):
                k = partner[q, 16 * pair + 8 * (i // 4) + 4 * (i // 2 % 2) + 2 * c + i % 2]
                block = ((((k >> 1) & 1) ^ c) * 2 + (k >> 5)) * NZ + ((k >> 2) & 7)
                start = pl.multiple_of(block * 32 + (k & 1) * 16, 16)
                left.append(left_rows[pl.ds(start, 16), :])
            left = jnp.concatenate(left, axis=0)
            weighted = (left.astype(jnp.float32) * twice).astype(left.dtype)
            met = contract(weighted, columns) - jnp.dot(
                left,
                image[q, :, 128 * pair : 128 * pair + 128],
                preferred_element_type=jnp.float32,
            )
            block = jnp.zeros((16, 128), jnp.float32)
            for i in range(8):
                block = jnp.where(lane // 16 == i, met[16 * i : 16 * i + 16], block)
            blocks.append(block)
        for two in range(2):
            even, odd = blocks[2 * two], blocks[2 * two + 1]
            out[2 * pair, two] = jnp.where(lane < 64, even, pltpu.roll(odd, 64, 1))
            out[2 * pair + 1, two] = jnp.where(lane < 64, pltpu.roll(even, 64, 1), odd)


def solve(partner, coulomb, w, panels, other):
    rows, share = panels[0].shape[1:]
    whole = w.shape[2]
    vmem = pl.BlockSpec(memory_space=pltpu.VMEM)
    return pl.pallas_call(
        solve_kernel,
        in_specs=[pl.BlockSpec(memory_space=pltpu.SMEM)] + [vmem] * 11,
        out_specs=vmem,
        out_shape=jax.ShapeDtypeStruct((8, 2, 16, 128), jnp.float32),
        scratch_shapes=[
            pltpu.VMEM((2 * rows, whole), jnp.bfloat16),
            pltpu.VMEM((4 * rows, share), jnp.bfloat16),
            pltpu.VMEM((4, share, 2 * rows), jnp.bfloat16),
        ],
        compiler_params=pltpu.CompilerParams(vmem_limit_bytes=VMEM),
        cost_estimate=pl.CostEstimate(
            flops=2 * 4 * share * whole * 2 * rows,
            bytes_accessed=4 * share * whole * 2,
            transcendentals=0,
        ),
        name="solve",
    )(partner, coulomb, w, *panels, other)


def spread_kernel(q_index, terms, out):
    r, j, c, _, _ = where_am_i()
    ks = q_index.shape[0]
    row = lax.broadcasted_iota(jnp.int32, (ks, 128), 0)
    col = lax.broadcasted_iota(jnp.int32, (ks, 128), 1)
    slot = (col & 63) >> 4
    hit = row == 8 * j + 4 * (slot >> 1) + 2 * c + (slot & 1)
    seen = jnp.zeros((ks // 2, 128), jnp.float32)
    for k in range(2):
        rows = q_index[pl.ds(k, ks // 2, stride=2), :].astype(jnp.float32).astype(jnp.bfloat16)
        pick = jnp.where(hit & (col >> 6 == k), 1.0, 0.0).astype(jnp.bfloat16)
        seen = seen + jnp.dot(rows, pick, preferred_element_type=jnp.float32)
    seen = seen.astype(jnp.int32)
    lane = lax.broadcasted_iota(jnp.int32, (16, 128), 1)
    blocks = []
    for two in range(2):
        full = terms[0, two]
        for i in range(1, 8):
            full = full + terms[i, two]
        turned = pltpu.roll(full, 64, 1)
        blocks.append(jnp.where(lane < 64, full, turned))
        blocks.append(jnp.where(lane < 64, turned, full))
    mine = (2 * r, 2 * r + 1, 2 * (r ^ 1), 2 * (r ^ 1) + 1)
    for target in range(out.shape[0]):
        wanted = jnp.broadcast_to(seen[target : target + 1, :], (16, 128))
        block = jnp.zeros((16, 128), jnp.float32)
        for q in range(4):
            block = jnp.where(wanted == mine[q], blocks[q], block)
        out[target] = block.astype(out.dtype)


def spread(q_index, terms):
    vmem = pl.BlockSpec(memory_space=pltpu.VMEM)
    return pl.pallas_call(
        spread_kernel,
        in_specs=[vmem, vmem],
        out_specs=vmem,
        out_shape=jax.ShapeDtypeStruct((32, 16, 128), jnp.float32),
        name="spread",
    )(q_index, terms)


def settle_kernel(arrived, out):
    lane = lax.broadcasted_iota(jnp.int32, (16, 128), 1) // 32
    sums = []
    for c in range(2):
        full = arrived[c].astype(jnp.float32)
        for r in range(2 + c, arrived.shape[0], 2):
            full = full + arrived[r].astype(jnp.float32)
        sums.append(full)
    for k in range(2):
        block = jnp.zeros((16, 128), jnp.float32)
        for z in range(2):
            for c in range(2):
                move = (z * 64 + c * 32 - k * 64 - z * 32) % 128
                turned = pltpu.roll(sums[c], move, 1) if move else sums[c]
                block = jnp.where(lane == 2 * z + c, turned, block)
        out[16 * k : 16 * k + 16, :] = block


def settle(arrived):
    vmem = pl.BlockSpec(memory_space=pltpu.VMEM)
    return pl.pallas_call(
        settle_kernel,
        in_specs=[vmem],
        out_specs=vmem,
        out_shape=jax.ShapeDtypeStruct((32, 128), jnp.float32),
        name="settle",
    )(arrived)


def local(pair_matrix, screened, coulomb, q_index):
    bands, share = pair_matrix.shape[1:]
    r, _, c, _, y_lo = where_am_i()
    w_other = send(screened, SWAP)
    own = pair_matrix.reshape(1, 2 * bands, share)
    even = jnp.concatenate([own] + [send(own, along_z(s)) for s in ZSHIFTS[1:]], axis=0)
    stack = jnp.concatenate([even, send(even, ZPAIR)], axis=0).reshape(1, NZ * 32, share)
    parts = [send(stack, first_plane(s)) for s in SHIFTS[1:]]
    p01 = jnp.concatenate([stack, parts[0]], axis=0)
    p23 = jnp.concatenate([parts[1], parts[2]], axis=0)

    f0 = send(p01, second_plane(1))
    g1 = send(p23, second_plane(-1))
    f1 = send(p23, second_plane(1))
    g0 = send(p01, second_plane(-1))
    ff0 = send(f0, second_plane(1))
    gg1 = send(g1, second_plane(-1))

    q_mine = jnp.stack([2 * r, 2 * r + 1, 2 * (r ^ 1), 2 * (r ^ 1) + 1])
    ks = lax.iota(jnp.int32, q_index.shape[0])
    partner = jnp.sum(
        jnp.where(q_index[None] == q_mine[:, None, None], ks[None, :, None], 0), axis=1
    )

    w = load(screened, w_other)
    w, f1, g0 = lax.optimization_barrier((w, f1, g0))
    up = jnp.where(c == 0, g0[0], parts[2][0])
    down = jnp.where(c == 0, f0[0], parts[1][0])
    across = jnp.where(y_lo == 0, up, down)
    mine = jnp.stack(
        [jnp.where(y_lo == 0, stack[0], across), jnp.where(y_lo == 0, across, stack[0])]
    )
    other = send(mine, SWAP)

    panels = (p01, p23, f0, f1, g0, g1, ff0, gg1)
    terms = solve(partner.astype(jnp.int32), coulomb.reshape(1, share), w, panels, other)
    terms = lax.all_to_all(terms, "col", split_axis=0, concat_axis=0, tiled=True)
    placed = spread(q_index, terms)
    arrived = lax.all_to_all(placed, "row", split_axis=0, concat_axis=0, tiled=True)
    return settle(arrived)


def solution(mesh):
    placed = (P("row", None, "col"), P("row", "col", None), P("col"), P())
    return jax.shard_map(
        local, mesh=mesh, in_specs=placed, out_specs=P("row", "col"), check_vma=False
    )
```

```python
import jax
import jax.numpy as jnp
from jax import lax
from jax.experimental import pallas as pl
from jax.experimental.pallas import tpu as pltpu
from jax.sharding import PartitionSpec as P

AXES = ("row", "col")
NX, NY, NZ, NCORE = 4, 4, 8, 2
SHIFTS = (0, 2, 1, -1)
ZSHIFTS = (0, 2, 4, -2)
VMEM = 58 * 1024 * 1024


def device_index(x, y, z, c):
    y_hi, y_lo = divmod(y % NY, 2)
    row = (y_lo * NZ + z % NZ) * NCORE + c
    return row * 8 + y_hi * NX + x % NX


def pairs(move):
    found = []
    for x in range(NX):
        for y in range(NY):
            for z in range(NZ):
                for c in range(NCORE):
                    found.append((device_index(x, y, z, c), device_index(*move(x, y, z, c))))
    return found


SWAP = pairs(lambda x, y, z, c: (x, y, z, 1 - c))
ZPAIR = pairs(lambda x, y, z, c: (x, y, z ^ 1, c))


def along_z(s):
    return pairs(lambda x, y, z, c: (x, y, z + s, c))


def first_plane(s):
    return pairs(lambda x, y, z, c: (x + s, y, z, c) if c == 0 else (x, y + s, z, c))


def second_plane(s):
    return pairs(lambda x, y, z, c: (x, y + s, z, c) if c == 0 else (x + s, y, z, c))


def send(value, perm):
    return lax.ppermute(value, AXES, perm)


def contract(a, b):
    return lax.dot_general(a, b, (((1,), (1,)), ((), ())), preferred_element_type=jnp.float32)


def where_am_i():
    r, j = lax.axis_index("row"), lax.axis_index("col")
    return r, j, r & 1, (r >> 1) & 7, r >> 4


def spot(k, i):
    r, j, c, _, y_lo = where_am_i()
    first, second = SHIFTS[i], SHIFTS[k]
    x = ((j & 3) - first - c * (second - first)) & 3
    y = (2 * (j >> 2) + y_lo - second - c * (first - second)) & 3
    return (y >> 1) * NX + x, y & 1


def place_of(z_wanted):
    z = where_am_i()[3]
    side = (z ^ z_wanted) & 1
    return side * 4 + ((((z ^ side) - z_wanted) & 7) >> 1)


def solve_kernel(
    partner, coulomb, w_own, w_other, p01, p23, f0, f1, g0, g1, ff0, gg1, other, out,
    panel, left_rows, image, w, sems,
):
    copies = [
        pltpu.make_async_copy((w_own, w_other)[q // 2].at[q % 2], w.at[q], sems.at[q])
        for q in range(4)
    ]
    copies[0].start()
    copies[1].start()
    rows, share = p01.shape[1:]
    r, j, c, _, _ = where_am_i()
    starts = [pl.multiple_of(place_of(z) * 32, 32) for z in range(NZ)]
    arrays = ((p01, p23), (ff0, gg1), (f0, f1), (g0, g1))
    for k in range(4):
        for i in range(4):
            col, low = spot(k, i)
            for z in range(NZ):
                to = pl.multiple_of(low * rows + z * 32, 32)
                piece = arrays[k][i // 2][i % 2, pl.ds(starts[z], 32), :]
                panel[pl.ds(to, 32), pl.ds(pl.multiple_of(col * share, share), share)] = piece
    left_rows[: 2 * rows, :] = panel[:, pl.ds(pl.multiple_of(j * share, share), share)]
    for low in range(2):
        for z in range(NZ):
            to = (2 + low) * rows + z * 32
            left_rows[to : to + 32, :] = other[low, pl.ds(starts[z], 32), :]
    for q in range(4):
        copies[q].wait()
        if q < 2:
            copies[q + 2].start()
        image[q] = contract(w[q], panel[...]).astype(image.dtype)

    lane = lax.broadcasted_iota(jnp.int32, (16, 128), 1)
    twice = 2.0 * coulomb[...]
    for pair in range(4):
        columns = left_rows[128 * pair : 128 * pair + 128, :]
        blocks = []
        for q in range(4):
            left = []
            for i in range(8):
                k = partner[q, 16 * pair + 8 * (i // 4) + 4 * (i // 2 % 2) + 2 * c + i % 2]
                block = ((((k >> 1) & 1) ^ c) * 2 + (k >> 5)) * NZ + ((k >> 2) & 7)
                start = pl.multiple_of(block * 32 + (k & 1) * 16, 16)
                left.append(left_rows[pl.ds(start, 16), :])
            left = jnp.concatenate(left, axis=0)
            weighted = (left.astype(jnp.float32) * twice).astype(left.dtype)
            met = contract(weighted, columns) - jnp.dot(
                left,
                image[q, :, 128 * pair : 128 * pair + 128],
                preferred_element_type=jnp.float32,
            )
            block = jnp.zeros((16, 128), jnp.float32)
            for i in range(8):
                block = jnp.where(lane // 16 == i, met[16 * i : 16 * i + 16], block)
            blocks.append(block)
        for two in range(2):
            even, odd = blocks[2 * two], blocks[2 * two + 1]
            out[2 * pair, two] = jnp.where(lane < 64, even, pltpu.roll(odd, 64, 1))
            out[2 * pair + 1, two] = jnp.where(lane < 64, pltpu.roll(even, 64, 1), odd)


def solve(partner, coulomb, w_own, w_other, panels, other):
    rows, share = panels[0].shape[1:]
    whole = w_own.shape[2]
    vmem = pl.BlockSpec(memory_space=pltpu.VMEM)
    return pl.pallas_call(
        solve_kernel,
        in_specs=[pl.BlockSpec(memory_space=pltpu.SMEM), vmem]
        + [pl.BlockSpec(memory_space=pl.ANY)] * 2
        + [vmem] * 9,
        out_specs=vmem,
        out_shape=jax.ShapeDtypeStruct((8, 2, 16, 128), jnp.float32),
        scratch_shapes=[
            pltpu.VMEM((2 * rows, whole), jnp.bfloat16),
            pltpu.VMEM((4 * rows, share), jnp.bfloat16),
            pltpu.VMEM((4, share, 2 * rows), jnp.bfloat16),
            pltpu.VMEM((4, share, whole), jnp.bfloat16),
            pltpu.SemaphoreType.DMA((4,)),
        ],
        compiler_params=pltpu.CompilerParams(vmem_limit_bytes=VMEM),
        cost_estimate=pl.CostEstimate(
            flops=2 * 4 * share * whole * 2 * rows,
            bytes_accessed=4 * share * whole * 2,
            transcendentals=0,
        ),
        name="solve",
    )(partner, coulomb, w_own, w_other, *panels, other)


def spread_kernel(q_index, terms, out):
    r, j, c, _, _ = where_am_i()
    ks = q_index.shape[0]
    row = lax.broadcasted_iota(jnp.int32, (ks, 128), 0)
    col = lax.broadcasted_iota(jnp.int32, (ks, 128), 1)
    slot = (col & 63) >> 4
    hit = row == 8 * j + 4 * (slot >> 1) + 2 * c + (slot & 1)
    seen = jnp.zeros((ks // 2, 128), jnp.float32)
    for k in range(2):
        rows = q_index[pl.ds(k, ks // 2, stride=2), :].astype(jnp.float32).astype(jnp.bfloat16)
        pick = jnp.where(hit & (col >> 6 == k), 1.0, 0.0).astype(jnp.bfloat16)
        seen = seen + jnp.dot(rows, pick, preferred_element_type=jnp.float32)
    seen = seen.astype(jnp.int32)
    lane = lax.broadcasted_iota(jnp.int32, (16, 128), 1)
    blocks = []
    for two in range(2):
        full = terms[0, two]
        for i in range(1, 8):
            full = full + terms[i, two]
        turned = pltpu.roll(full, 64, 1)
        blocks.append(jnp.where(lane < 64, full, turned))
        blocks.append(jnp.where(lane < 64, turned, full))
    mine = (2 * r, 2 * r + 1, 2 * (r ^ 1), 2 * (r ^ 1) + 1)
    for target in range(out.shape[0]):
        wanted = jnp.broadcast_to(seen[target : target + 1, :], (16, 128))
        block = jnp.zeros((16, 128), jnp.float32)
        for q in range(4):
            block = jnp.where(wanted == mine[q], blocks[q], block)
        out[target] = block.astype(out.dtype)


def spread(q_index, terms):
    vmem = pl.BlockSpec(memory_space=pltpu.VMEM)
    return pl.pallas_call(
        spread_kernel,
        in_specs=[vmem, vmem],
        out_specs=vmem,
        out_shape=jax.ShapeDtypeStruct((32, 16, 128), jnp.float32),
        name="spread",
    )(q_index, terms)


def settle_kernel(arrived, out):
    lane = lax.broadcasted_iota(jnp.int32, (16, 128), 1) // 32
    sums = []
    for c in range(2):
        full = arrived[c].astype(jnp.float32)
        for r in range(2 + c, arrived.shape[0], 2):
            full = full + arrived[r].astype(jnp.float32)
        sums.append(full)
    for k in range(2):
        block = jnp.zeros((16, 128), jnp.float32)
        for z in range(2):
            for c in range(2):
                move = (z * 64 + c * 32 - k * 64 - z * 32) % 128
                turned = pltpu.roll(sums[c], move, 1) if move else sums[c]
                block = jnp.where(lane == 2 * z + c, turned, block)
        out[16 * k : 16 * k + 16, :] = block


def settle(arrived):
    vmem = pl.BlockSpec(memory_space=pltpu.VMEM)
    return pl.pallas_call(
        settle_kernel,
        in_specs=[vmem],
        out_specs=vmem,
        out_shape=jax.ShapeDtypeStruct((32, 128), jnp.float32),
        name="settle",
    )(arrived)


def local(pair_matrix, screened, coulomb, q_index):
    bands, share = pair_matrix.shape[1:]
    r, _, c, _, y_lo = where_am_i()
    w_other = send(screened, SWAP)
    own = pair_matrix.reshape(1, 2 * bands, share)
    even = jnp.concatenate([own] + [send(own, along_z(s)) for s in ZSHIFTS[1:]], axis=0)
    stack = jnp.concatenate([even, send(even, ZPAIR)], axis=0).reshape(1, NZ * 32, share)
    parts = [send(stack, first_plane(s)) for s in SHIFTS[1:]]
    p01 = jnp.concatenate([stack, parts[0]], axis=0)
    p23 = jnp.concatenate([parts[1], parts[2]], axis=0)

    f0 = send(p01, second_plane(1))
    g1 = send(p23, second_plane(-1))
    g0 = send(p01, second_plane(-1))
    f1 = send(p23, second_plane(1))
    ff0 = send(f0, second_plane(1))
    gg1 = send(g1, second_plane(-1))

    q_mine = jnp.stack([2 * r, 2 * r + 1, 2 * (r ^ 1), 2 * (r ^ 1) + 1])
    ks = lax.iota(jnp.int32, q_index.shape[0])
    partner = jnp.sum(
        jnp.where(q_index[None] == q_mine[:, None, None], ks[None, :, None], 0), axis=1
    )

    up = jnp.where(c == 0, g0[0], parts[2][0])
    down = jnp.where(c == 0, f0[0], parts[1][0])
    across = jnp.where(y_lo == 0, up, down)
    mine = jnp.stack(
        [jnp.where(y_lo == 0, stack[0], across), jnp.where(y_lo == 0, across, stack[0])]
    )
    other = send(mine, SWAP)

    panels = (p01, p23, f0, f1, g0, g1, ff0, gg1)
    terms = solve(
        partner.astype(jnp.int32), coulomb.reshape(1, share), screened, w_other, panels, other
    )
    terms = lax.all_to_all(terms, "col", split_axis=0, concat_axis=0, tiled=True)
    placed = spread(q_index, terms)
    arrived = lax.all_to_all(placed, "row", split_axis=0, concat_axis=0, tiled=True)
    return settle(arrived)


def solution(mesh):
    placed = (P("row", None, "col"), P("row", "col", None), P("col"), P())
    return jax.shard_map(
        local, mesh=mesh, in_specs=placed, out_specs=P("row", "col"), check_vma=False
    )
```

```python
import jax
import jax.numpy as jnp
from jax import lax
from jax.experimental import pallas as pl
from jax.experimental.pallas import tpu as pltpu
from jax.sharding import PartitionSpec as P

AXES = ("row", "col")
NX, NY, NZ, NCORE = 4, 4, 8, 2
SHIFTS = (0, 2, 1, -1)
ZSHIFTS = (0, 2, 4, -2)
VMEM = 48 * 1024 * 1024


def device_index(x, y, z, c):
    y_hi, y_lo = divmod(y % NY, 2)
    row = (y_lo * NZ + z % NZ) * NCORE + c
    return row * 8 + y_hi * NX + x % NX


def pairs(move):
    found = []
    for x in range(NX):
        for y in range(NY):
            for z in range(NZ):
                for c in range(NCORE):
                    found.append((device_index(x, y, z, c), device_index(*move(x, y, z, c))))
    return found


SWAP = pairs(lambda x, y, z, c: (x, y, z, 1 - c))
ACROSS = pairs(lambda x, y, z, c: (x, y ^ 1, z, 1 - c))
ZPAIR = pairs(lambda x, y, z, c: (x, y, z ^ 1, c))


def along_z(s):
    return pairs(lambda x, y, z, c: (x, y, z + s, c))


def first_plane(s):
    return pairs(lambda x, y, z, c: (x + s, y, z, c) if c == 0 else (x, y + s, z, c))


def second_plane(s):
    return pairs(lambda x, y, z, c: (x, y + s, z, c) if c == 0 else (x + s, y, z, c))


def send(value, perm):
    return lax.ppermute(value, AXES, perm)


def contract(a, b):
    return lax.dot_general(a, b, (((1,), (1,)), ((), ())), preferred_element_type=jnp.float32)


def where_am_i():
    r, j = lax.axis_index("row"), lax.axis_index("col")
    return r, j, r & 1, (r >> 1) & 7, r >> 4


def spot(k, i):
    r, j, c, _, y_lo = where_am_i()
    first, second = SHIFTS[i], SHIFTS[k]
    x = ((j & 3) - first - c * (second - first)) & 3
    y = (2 * (j >> 2) + y_lo - second - c * (first - second)) & 3
    return (y >> 1) * NX + x, y & 1


def place_of(z_wanted):
    z = where_am_i()[3]
    side = (z ^ z_wanted) & 1
    return side * 4 + ((((z ^ side) - z_wanted) & 7) >> 1)


def solve_kernel(
    partner, coulomb, w_own, w_other, p01, p23, f0, f1, g0, g1, ff0, gg1, near, far, out,
    panel, left_rows, image, w, sems,
):
    copies = [
        pltpu.make_async_copy((w_own, w_other)[q // 2].at[q % 2], w.at[q], sems.at[q])
        for q in range(4)
    ]
    copies[0].start()
    copies[1].start()
    rows, share = p01.shape[1:]
    _, j, c, _, y_lo = where_am_i()
    starts = [pl.multiple_of(place_of(z) * 32, 32) for z in range(NZ)]
    arrays = ((p01, p23), (ff0, gg1), (f0, f1), (g0, g1))
    for k in range(4):
        for i in range(4):
            col, low = spot(k, i)
            for z in range(NZ):
                to = pl.multiple_of(low * rows + z * 32, 32)
                piece = arrays[k][i // 2][i % 2, pl.ds(starts[z], 32), :]
                panel[pl.ds(to, 32), pl.ds(pl.multiple_of(col * share, share), share)] = piece
    left_rows[: 2 * rows, :] = panel[:, pl.ds(pl.multiple_of(j * share, share), share)]
    for low, stack in ((y_lo, near), (1 - y_lo, far)):
        for z in range(NZ):
            to = pl.multiple_of((2 + low) * rows + z * 32, 32)
            left_rows[pl.ds(to, 32), :] = stack[0, pl.ds(starts[z], 32), :]
    for q in range(4):
        copies[q].wait()
        if q < 2:
            copies[q + 2].start()
        image[q] = contract(w[q], panel[...]).astype(image.dtype)

    lane = lax.broadcasted_iota(jnp.int32, (16, 128), 1)
    twice = 2.0 * coulomb[...]
    for pair in range(4):
        columns = left_rows[128 * pair : 128 * pair + 128, :]
        blocks = []
        for q in range(4):
            left = []
            for i in range(8):
                k = partner[q, 16 * pair + 8 * (i // 4) + 4 * (i // 2 % 2) + 2 * c + i % 2]
                block = ((((k >> 1) & 1) ^ c) * 2 + (k >> 5)) * NZ + ((k >> 2) & 7)
                start = pl.multiple_of(block * 32 + (k & 1) * 16, 16)
                left.append(left_rows[pl.ds(start, 16), :])
            left = jnp.concatenate(left, axis=0)
            weighted = (left.astype(jnp.float32) * twice).astype(left.dtype)
            met = contract(weighted, columns) - jnp.dot(
                left,
                image[q, :, 128 * pair : 128 * pair + 128],
                preferred_element_type=jnp.float32,
            )
            block = jnp.zeros((16, 128), jnp.float32)
            for i in range(8):
                block = jnp.where(lane // 16 == i, met[16 * i : 16 * i + 16], block)
            blocks.append(block)
        for two in range(2):
            even, odd = blocks[2 * two], blocks[2 * two + 1]
            out[2 * pair, two] = jnp.where(lane < 64, even, pltpu.roll(odd, 64, 1))
            out[2 * pair + 1, two] = jnp.where(lane < 64, pltpu.roll(even, 64, 1), odd)


def solve(partner, coulomb, w_own, w_other, panels, near, far):
    rows, share = panels[0].shape[1:]
    whole = w_own.shape[2]
    vmem = pl.BlockSpec(memory_space=pltpu.VMEM)
    return pl.pallas_call(
        solve_kernel,
        in_specs=[pl.BlockSpec(memory_space=pltpu.SMEM), vmem]
        + [pl.BlockSpec(memory_space=pl.ANY)] * 2
        + [vmem] * 10,
        out_specs=vmem,
        out_shape=jax.ShapeDtypeStruct((8, 2, 16, 128), jnp.float32),
        scratch_shapes=[
            pltpu.VMEM((2 * rows, whole), jnp.bfloat16),
            pltpu.VMEM((4 * rows, share), jnp.bfloat16),
            pltpu.VMEM((4, share, 2 * rows), jnp.bfloat16),
            pltpu.VMEM((4, share, whole), jnp.bfloat16),
            pltpu.SemaphoreType.DMA((4,)),
        ],
        compiler_params=pltpu.CompilerParams(vmem_limit_bytes=VMEM),
        cost_estimate=pl.CostEstimate(
            flops=2 * 4 * share * whole * 2 * rows,
            bytes_accessed=4 * share * whole * 2,
            transcendentals=0,
        ),
        name="solve",
    )(partner, coulomb, w_own, w_other, *panels, near, far)


def spread_kernel(q_index, terms, out):
    r, j, c, _, _ = where_am_i()
    ks = q_index.shape[0]
    row = lax.broadcasted_iota(jnp.int32, (ks, 128), 0)
    col = lax.broadcasted_iota(jnp.int32, (ks, 128), 1)
    slot = (col & 63) >> 4
    hit = row == 8 * j + 4 * (slot >> 1) + 2 * c + (slot & 1)
    seen = jnp.zeros((ks // 2, 128), jnp.float32)
    for k in range(2):
        rows = q_index[pl.ds(k, ks // 2, stride=2), :].astype(jnp.float32).astype(jnp.bfloat16)
        pick = jnp.where(hit & (col >> 6 == k), 1.0, 0.0).astype(jnp.bfloat16)
        seen = seen + jnp.dot(rows, pick, preferred_element_type=jnp.float32)
    seen = seen.astype(jnp.int32)
    lane = lax.broadcasted_iota(jnp.int32, (16, 128), 1)
    blocks = []
    for two in range(2):
        full = terms[0, two]
        for i in range(1, 8):
            full = full + terms[i, two]
        turned = pltpu.roll(full, 64, 1)
        blocks.append(jnp.where(lane < 64, full, turned))
        blocks.append(jnp.where(lane < 64, turned, full))
    mine = (2 * r, 2 * r + 1, 2 * (r ^ 1), 2 * (r ^ 1) + 1)
    for target in range(out.shape[0]):
        wanted = jnp.broadcast_to(seen[target : target + 1, :], (16, 128))
        block = jnp.zeros((16, 128), jnp.float32)
        for q in range(4):
            block = jnp.where(wanted == mine[q], blocks[q], block)
        out[target] = block.astype(out.dtype)


def spread(q_index, terms):
    vmem = pl.BlockSpec(memory_space=pltpu.VMEM)
    return pl.pallas_call(
        spread_kernel,
        in_specs=[vmem, vmem],
        out_specs=vmem,
        out_shape=jax.ShapeDtypeStruct((32, 16, 128), jnp.float32),
        name="spread",
    )(q_index, terms)


def settle_kernel(arrived, out):
    lane = lax.broadcasted_iota(jnp.int32, (16, 128), 1) // 32
    sums = []
    for c in range(2):
        full = arrived[c].astype(jnp.float32)
        for r in range(2 + c, arrived.shape[0], 2):
            full = full + arrived[r].astype(jnp.float32)
        sums.append(full)
    for k in range(2):
        block = jnp.zeros((16, 128), jnp.float32)
        for z in range(2):
            for c in range(2):
                move = (z * 64 + c * 32 - k * 64 - z * 32) % 128
                turned = pltpu.roll(sums[c], move, 1) if move else sums[c]
                block = jnp.where(lane == 2 * z + c, turned, block)
        out[16 * k : 16 * k + 16, :] = block


def settle(arrived):
    vmem = pl.BlockSpec(memory_space=pltpu.VMEM)
    return pl.pallas_call(
        settle_kernel,
        in_specs=[vmem],
        out_specs=vmem,
        out_shape=jax.ShapeDtypeStruct((32, 128), jnp.float32),
        name="settle",
    )(arrived)


def local(pair_matrix, screened, coulomb, q_index):
    bands, share = pair_matrix.shape[1:]
    r = lax.axis_index("row")
    w_other = send(screened, SWAP)
    own = pair_matrix.reshape(1, 2 * bands, share)
    even = jnp.concatenate([own] + [send(own, along_z(s)) for s in ZSHIFTS[1:]], axis=0)
    paired = send(even, ZPAIR)
    q_mine = jnp.stack([2 * r, 2 * r + 1, 2 * (r ^ 1), 2 * (r ^ 1) + 1])
    ks = lax.iota(jnp.int32, q_index.shape[0])
    partner = jnp.sum(
        jnp.where(q_index[None] == q_mine[:, None, None], ks[None, :, None], 0), axis=1
    ).astype(jnp.int32)
    paired, partner, coulomb = lax.optimization_barrier(
        (paired, partner, coulomb.reshape(1, share))
    )
    stack = jnp.concatenate([even, paired], axis=0).reshape(1, NZ * 32, share)
    near = send(stack, SWAP)
    far = send(stack, ACROSS)
    parts = lax.optimization_barrier([send(stack, first_plane(s)) for s in SHIFTS[1:]])
    p01 = jnp.concatenate([stack, parts[0]], axis=0)
    p23 = jnp.concatenate([parts[1], parts[2]], axis=0)

    f0 = send(p01, second_plane(1))
    g1 = send(p23, second_plane(-1))
    g0 = send(p01, second_plane(-1))
    f1 = send(p23, second_plane(1))
    ff0 = send(f0, second_plane(1))
    gg1 = send(g1, second_plane(-1))

    panels = (p01, p23, f0, f1, g0, g1, ff0, gg1)
    terms = solve(partner, coulomb, screened, w_other, panels, near, far)
    terms = lax.all_to_all(terms, "col", split_axis=0, concat_axis=0, tiled=True)
    placed = spread(q_index, terms)
    arrived = lax.all_to_all(placed, "row", split_axis=0, concat_axis=0, tiled=True)
    return settle(arrived)


def solution(mesh):
    placed = (P("row", None, "col"), P("row", "col", None), P("col"), P())
    return jax.shard_map(
        local, mesh=mesh, in_specs=placed, out_specs=P("row", "col"), check_vma=False
    )
```

```python
import jax
import jax.numpy as jnp
from jax import lax
from jax.experimental import pallas as pl
from jax.experimental.pallas import tpu as pltpu
from jax.sharding import PartitionSpec as P

AXES = ("row", "col")
NX, NY, NZ, NCORE = 4, 4, 8, 2
SHIFTS = (0, 2, 1, -1)
ZSHIFTS = (0, 2, 4, -2)
VMEM = 48 * 1024 * 1024


def device_index(x, y, z, c):
    y_hi, y_lo = divmod(y % NY, 2)
    row = (y_lo * NZ + z % NZ) * NCORE + c
    return row * 8 + y_hi * NX + x % NX


def pairs(move):
    found = []
    for x in range(NX):
        for y in range(NY):
            for z in range(NZ):
                for c in range(NCORE):
                    found.append((device_index(x, y, z, c), device_index(*move(x, y, z, c))))
    return found


SWAP = pairs(lambda x, y, z, c: (x, y, z, 1 - c))
ACROSS = pairs(lambda x, y, z, c: (x, y ^ 1, z, 1 - c))
ZPAIR = pairs(lambda x, y, z, c: (x, y, z ^ 1, c))


def along_z(s):
    return pairs(lambda x, y, z, c: (x, y, z + s, c))


def first_plane(s):
    return pairs(lambda x, y, z, c: (x + s, y, z, c) if c == 0 else (x, y + s, z, c))


def second_plane(s):
    return pairs(lambda x, y, z, c: (x, y + s, z, c) if c == 0 else (x + s, y, z, c))


def send(value, perm):
    return lax.ppermute(value, AXES, perm)


def contract(a, b):
    return lax.dot_general(a, b, (((1,), (1,)), ((), ())), preferred_element_type=jnp.float32)


def where_am_i():
    r, j = lax.axis_index("row"), lax.axis_index("col")
    return r, j, r & 1, (r >> 1) & 7, r >> 4


def spot(k, i):
    r, j, c, _, y_lo = where_am_i()
    first, second = SHIFTS[i], SHIFTS[k]
    x = ((j & 3) - first - c * (second - first)) & 3
    y = (2 * (j >> 2) + y_lo - second - c * (first - second)) & 3
    return (y >> 1) * NX + x, y & 1


def place_of(z_wanted):
    z = where_am_i()[3]
    side = (z ^ z_wanted) & 1
    return side * 4 + ((((z ^ side) - z_wanted) & 7) >> 1)


def solve_kernel(
    partner, coulomb, w_own, w_other, p01, p23, f0, f1, g0, g1, ff0, gg1, near, far, out,
    panel, left_rows, image, w, sems,
):
    copies = [
        pltpu.make_async_copy((w_own, w_other)[q // 2].at[q % 2], w.at[q], sems.at[q])
        for q in range(4)
    ]
    copies[0].start()
    copies[1].start()
    rows, share = p01.shape[1:]
    _, j, c, _, y_lo = where_am_i()
    starts = [pl.multiple_of(place_of(z) * 32, 32) for z in range(NZ)]
    arrays = ((p01, p23), (ff0, gg1), (f0, f1), (g0, g1))
    for k in range(4):
        for i in range(4):
            col, low = spot(k, i)
            for z in range(NZ):
                to = pl.multiple_of(low * rows + z * 32, 32)
                piece = arrays[k][i // 2][i % 2, pl.ds(starts[z], 32), :]
                panel[pl.ds(to, 32), pl.ds(pl.multiple_of(col * share, share), share)] = piece
    left_rows[: 2 * rows, :] = panel[:, pl.ds(pl.multiple_of(j * share, share), share)]
    for low, stack in ((y_lo, near), (1 - y_lo, far)):
        for z in range(NZ):
            to = pl.multiple_of((2 + low) * rows + z * 32, 32)
            left_rows[pl.ds(to, 32), :] = stack[0, pl.ds(starts[z], 32), :]
    for q in range(4):
        copies[q].wait()
        if q < 2:
            copies[q + 2].start()
        image[q] = contract(w[q], panel[...]).astype(image.dtype)

    lane = lax.broadcasted_iota(jnp.int32, (16, 128), 1)
    twice = 2.0 * coulomb[...]
    for pair in range(4):
        columns = left_rows[128 * pair : 128 * pair + 128, :]
        blocks = []
        for q in range(4):
            left = []
            for i in range(8):
                k = partner[q, 16 * pair + 8 * (i // 4) + 4 * (i // 2 % 2) + 2 * c + i % 2]
                block = ((((k >> 1) & 1) ^ c) * 2 + (k >> 5)) * NZ + ((k >> 2) & 7)
                start = pl.multiple_of(block * 32 + (k & 1) * 16, 16)
                left.append(left_rows[pl.ds(start, 16), :])
            left = jnp.concatenate(left, axis=0)
            weighted = (left.astype(jnp.float32) * twice).astype(left.dtype)
            met = contract(weighted, columns) - jnp.dot(
                left,
                image[q, :, 128 * pair : 128 * pair + 128],
                preferred_element_type=jnp.float32,
            )
            block = jnp.zeros((16, 128), jnp.float32)
            for i in range(8):
                block = jnp.where(lane // 16 == i, met[16 * i : 16 * i + 16], block)
            blocks.append(block)
        for two in range(2):
            even, odd = blocks[2 * two], blocks[2 * two + 1]
            out[2 * pair, two] = jnp.where(lane < 64, even, pltpu.roll(odd, 64, 1))
            out[2 * pair + 1, two] = jnp.where(lane < 64, pltpu.roll(even, 64, 1), odd)


def solve(partner, coulomb, w_own, w_other, panels, near, far):
    rows, share = panels[0].shape[1:]
    whole = w_own.shape[2]
    vmem = pl.BlockSpec(memory_space=pltpu.VMEM)
    return pl.pallas_call(
        solve_kernel,
        in_specs=[pl.BlockSpec(memory_space=pltpu.SMEM), vmem]
        + [pl.BlockSpec(memory_space=pl.ANY)] * 2
        + [vmem] * 10,
        out_specs=vmem,
        out_shape=jax.ShapeDtypeStruct((8, 2, 16, 128), jnp.float32),
        scratch_shapes=[
            pltpu.VMEM((2 * rows, whole), jnp.bfloat16),
            pltpu.VMEM((4 * rows, share), jnp.bfloat16),
            pltpu.VMEM((4, share, 2 * rows), jnp.bfloat16),
            pltpu.VMEM((4, share, whole), jnp.bfloat16),
            pltpu.SemaphoreType.DMA((4,)),
        ],
        compiler_params=pltpu.CompilerParams(vmem_limit_bytes=VMEM),
        cost_estimate=pl.CostEstimate(
            flops=2 * 4 * share * whole * 2 * rows,
            bytes_accessed=4 * share * whole * 2,
            transcendentals=0,
        ),
        name="solve",
    )(partner, coulomb, w_own, w_other, *panels, near, far)


def spread_kernel(q_index, terms, out):
    r, j, c, _, _ = where_am_i()
    ks = q_index.shape[0]
    row = lax.broadcasted_iota(jnp.int32, (ks, 128), 0)
    col = lax.broadcasted_iota(jnp.int32, (ks, 128), 1)
    slot = (col & 63) >> 4
    hit = row == 8 * j + 4 * (slot >> 1) + 2 * c + (slot & 1)
    seen = jnp.zeros((ks // 2, 128), jnp.float32)
    for k in range(2):
        rows = q_index[pl.ds(k, ks // 2, stride=2), :].astype(jnp.float32).astype(jnp.bfloat16)
        pick = jnp.where(hit & (col >> 6 == k), 1.0, 0.0).astype(jnp.bfloat16)
        seen = seen + jnp.dot(rows, pick, preferred_element_type=jnp.float32)
    seen = seen.astype(jnp.int32)
    lane = lax.broadcasted_iota(jnp.int32, (16, 128), 1)
    blocks = []
    for two in range(2):
        full = terms[0, two]
        for i in range(1, 8):
            full = full + terms[i, two]
        turned = pltpu.roll(full, 64, 1)
        blocks.append(jnp.where(lane < 64, full, turned))
        blocks.append(jnp.where(lane < 64, turned, full))
    mine = (2 * r, 2 * r + 1, 2 * (r ^ 1), 2 * (r ^ 1) + 1)
    for target in range(out.shape[0]):
        wanted = jnp.broadcast_to(seen[target : target + 1, :], (16, 128))
        block = jnp.zeros((16, 128), jnp.float32)
        for q in range(4):
            block = jnp.where(wanted == mine[q], blocks[q], block)
        out[target] = block.astype(out.dtype)


def spread(q_index, terms):
    vmem = pl.BlockSpec(memory_space=pltpu.VMEM)
    return pl.pallas_call(
        spread_kernel,
        in_specs=[vmem, vmem],
        out_specs=vmem,
        out_shape=jax.ShapeDtypeStruct((32, 16, 128), jnp.float32),
        name="spread",
    )(q_index, terms)


def settle_kernel(arrived, out):
    lane = lax.broadcasted_iota(jnp.int32, (16, 128), 1) // 32
    sums = []
    for c in range(2):
        full = arrived[c].astype(jnp.float32)
        for r in range(2 + c, arrived.shape[0], 2):
            full = full + arrived[r].astype(jnp.float32)
        sums.append(full)
    for k in range(2):
        block = jnp.zeros((16, 128), jnp.float32)
        for z in range(2):
            for c in range(2):
                move = (z * 64 + c * 32 - k * 64 - z * 32) % 128
                turned = pltpu.roll(sums[c], move, 1) if move else sums[c]
                block = jnp.where(lane == 2 * z + c, turned, block)
        out[16 * k : 16 * k + 16, :] = block


def settle(arrived):
    vmem = pl.BlockSpec(memory_space=pltpu.VMEM)
    return pl.pallas_call(
        settle_kernel,
        in_specs=[vmem],
        out_specs=vmem,
        out_shape=jax.ShapeDtypeStruct((32, 128), jnp.float32),
        name="settle",
    )(arrived)


def local(pair_matrix, screened, coulomb, q_index):
    bands, share = pair_matrix.shape[1:]
    r = lax.axis_index("row")
    w_other = send(screened, SWAP)
    own = pair_matrix.reshape(1, 2 * bands, share)
    even = jnp.concatenate([own] + [send(own, along_z(s)) for s in ZSHIFTS[1:]], axis=0)
    paired = send(even, ZPAIR)
    q_mine = jnp.stack([2 * r, 2 * r + 1, 2 * (r ^ 1), 2 * (r ^ 1) + 1])
    ks = lax.iota(jnp.int32, q_index.shape[0])
    partner = jnp.sum(
        jnp.where(q_index[None] == q_mine[:, None, None], ks[None, :, None], 0), axis=1
    ).astype(jnp.int32)
    paired, partner, coulomb, w_other = lax.optimization_barrier(
        (paired, partner, coulomb.reshape(1, share), w_other)
    )
    stack = jnp.concatenate([even, paired], axis=0).reshape(1, NZ * 32, share)
    near = send(stack, SWAP)
    far = send(stack, ACROSS)
    parts = lax.optimization_barrier([send(stack, first_plane(s)) for s in SHIFTS[1:]])
    p01 = jnp.concatenate([stack, parts[0]], axis=0)
    p23 = jnp.concatenate([parts[1], parts[2]], axis=0)

    f0 = send(p01, second_plane(1))
    g1 = send(p23, second_plane(-1))
    g0 = send(p01, second_plane(-1))
    f1 = send(p23, second_plane(1))
    ff0 = send(f0, second_plane(1))
    gg1 = send(g1, second_plane(-1))

    panels = (p01, p23, f0, f1, g0, g1, ff0, gg1)
    terms = solve(partner, coulomb, screened, w_other, panels, near, far)
    terms = lax.all_to_all(terms, "col", split_axis=0, concat_axis=0, tiled=True)
    placed = spread(q_index, terms)
    arrived = lax.all_to_all(placed, "row", split_axis=0, concat_axis=0, tiled=True)
    return settle(arrived)


def solution(mesh):
    placed = (P("row", None, "col"), P("row", "col", None), P("col"), P())
    return jax.shard_map(
        local, mesh=mesh, in_specs=placed, out_specs=P("row", "col"), check_vma=False
    )
```

```python
import jax
import jax.numpy as jnp
from jax import lax
from jax.experimental import pallas as pl
from jax.experimental.pallas import tpu as pltpu
from jax.sharding import PartitionSpec as P

AXES = ("row", "col")
NX, NY, NZ, NCORE = 4, 4, 8, 2
FIRST = (0, 1, 2, -1)
SECOND = (0, 2, 1, -1)
ZSHIFTS = (0, 2, 4, -2)
VMEM = 48 * 1024 * 1024


def device_index(x, y, z, c):
    y_hi, y_lo = divmod(y % NY, 2)
    row = (y_lo * NZ + z % NZ) * NCORE + c
    return row * 8 + y_hi * NX + x % NX


def pairs(move):
    found = []
    for x in range(NX):
        for y in range(NY):
            for z in range(NZ):
                for c in range(NCORE):
                    found.append((device_index(x, y, z, c), device_index(*move(x, y, z, c))))
    return found


SWAP = pairs(lambda x, y, z, c: (x, y, z, 1 - c))
ACROSS = pairs(lambda x, y, z, c: (x, y ^ 1, z, 1 - c))
ZPAIR = pairs(lambda x, y, z, c: (x, y, z ^ 1, c))


def along_z(s):
    return pairs(lambda x, y, z, c: (x, y, z + s, c))


def first_plane(s):
    return pairs(lambda x, y, z, c: (x + s, y, z, c) if c == 0 else (x, y + s, z, c))


def second_plane(s):
    return pairs(lambda x, y, z, c: (x, y + s, z, c) if c == 0 else (x + s, y, z, c))


def send(value, perm):
    return lax.ppermute(value, AXES, perm)


def contract(a, b):
    return lax.dot_general(a, b, (((1,), (1,)), ((), ())), preferred_element_type=jnp.float32)


def where_am_i():
    r, j = lax.axis_index("row"), lax.axis_index("col")
    return r, j, r & 1, (r >> 1) & 7, r >> 4


def spot(k, i):
    r, j, c, _, y_lo = where_am_i()
    first, second = FIRST[i], SECOND[k]
    x = ((j & 3) - first - c * (second - first)) & 3
    y = (2 * (j >> 2) + y_lo - second - c * (first - second)) & 3
    return (y >> 1) * NX + x, y & 1


def place_of(z_wanted):
    z = where_am_i()[3]
    side = (z ^ z_wanted) & 1
    return side * 4 + ((((z ^ side) - z_wanted) & 7) >> 1)


def solve_kernel(
    partner, coulomb, w_own, w_other, p01, p23, f0, f1, g0, g1, ff0, gg1, near, far, out,
    panel, left_rows, image, w, sems,
):
    copies = [
        pltpu.make_async_copy((w_own, w_other)[q // 2].at[q % 2], w.at[q], sems.at[q])
        for q in range(4)
    ]
    copies[0].start()
    rows, share = p01.shape[1:]
    _, j, c, _, y_lo = where_am_i()
    starts = [pl.multiple_of(place_of(z) * 32, 32) for z in range(NZ)]
    arrays = ((p01, p23), (ff0, gg1), (f0, f1), (g0, g1))
    for k in range(4):
        for i in range(4):
            col, low = spot(k, i)
            for z in range(NZ):
                to = pl.multiple_of(low * rows + z * 32, 32)
                piece = arrays[k][i // 2][i % 2, pl.ds(starts[z], 32), :]
                panel[pl.ds(to, 32), pl.ds(pl.multiple_of(col * share, share), share)] = piece
    left_rows[: 2 * rows, :] = panel[:, pl.ds(pl.multiple_of(j * share, share), share)]
    for low, stack in ((y_lo, near), (1 - y_lo, far)):
        for z in range(NZ):
            to = pl.multiple_of((2 + low) * rows + z * 32, 32)
            left_rows[pl.ds(to, 32), :] = stack[0, pl.ds(starts[z], 32), :]
    for q in range(4):
        copies[q].wait()
        if q < 3:
            copies[q + 1].start()
        image[q] = contract(w[q], panel[...]).astype(image.dtype)

    lane = lax.broadcasted_iota(jnp.int32, (16, 128), 1)
    twice = 2.0 * coulomb[...]
    for pair in range(4):
        columns = left_rows[128 * pair : 128 * pair + 128, :]
        blocks = []
        for q in range(4):
            left = []
            for i in range(8):
                k = partner[q, 16 * pair + 8 * (i // 4) + 4 * (i // 2 % 2) + 2 * c + i % 2]
                block = ((((k >> 1) & 1) ^ c) * 2 + (k >> 5)) * NZ + ((k >> 2) & 7)
                start = pl.multiple_of(block * 32 + (k & 1) * 16, 16)
                left.append(left_rows[pl.ds(start, 16), :])
            left = jnp.concatenate(left, axis=0)
            weighted = (left.astype(jnp.float32) * twice).astype(left.dtype)
            met = contract(weighted, columns) - jnp.dot(
                left,
                image[q, :, 128 * pair : 128 * pair + 128],
                preferred_element_type=jnp.float32,
            )
            block = jnp.zeros((16, 128), jnp.float32)
            for i in range(8):
                block = jnp.where(lane // 16 == i, met[16 * i : 16 * i + 16], block)
            blocks.append(block)
        for two in range(2):
            even, odd = blocks[2 * two], blocks[2 * two + 1]
            out[2 * pair, two] = jnp.where(lane < 64, even, pltpu.roll(odd, 64, 1))
            out[2 * pair + 1, two] = jnp.where(lane < 64, pltpu.roll(even, 64, 1), odd)


def solve(partner, coulomb, w_own, w_other, panels, near, far):
    rows, share = panels[0].shape[1:]
    whole = w_own.shape[2]
    vmem = pl.BlockSpec(memory_space=pltpu.VMEM)
    return pl.pallas_call(
        solve_kernel,
        in_specs=[pl.BlockSpec(memory_space=pltpu.SMEM), vmem]
        + [pl.BlockSpec(memory_space=pl.ANY)] * 2
        + [vmem] * 10,
        out_specs=vmem,
        out_shape=jax.ShapeDtypeStruct((8, 2, 16, 128), jnp.float32),
        scratch_shapes=[
            pltpu.VMEM((2 * rows, whole), jnp.bfloat16),
            pltpu.VMEM((4 * rows, share), jnp.bfloat16),
            pltpu.VMEM((4, share, 2 * rows), jnp.bfloat16),
            pltpu.VMEM((4, share, whole), jnp.bfloat16),
            pltpu.SemaphoreType.DMA((4,)),
        ],
        compiler_params=pltpu.CompilerParams(vmem_limit_bytes=VMEM),
        cost_estimate=pl.CostEstimate(
            flops=2 * 4 * share * whole * 2 * rows,
            bytes_accessed=4 * share * whole * 2,
            transcendentals=0,
        ),
        name="solve",
    )(partner, coulomb, w_own, w_other, *panels, near, far)


def spread_kernel(q_index, terms, out):
    r, j, c, _, _ = where_am_i()
    ks = q_index.shape[0]
    row = lax.broadcasted_iota(jnp.int32, (ks, 128), 0)
    col = lax.broadcasted_iota(jnp.int32, (ks, 128), 1)
    slot = (col & 63) >> 4
    hit = row == 8 * j + 4 * (slot >> 1) + 2 * c + (slot & 1)
    seen = jnp.zeros((ks // 2, 128), jnp.float32)
    for k in range(2):
        rows = q_index[pl.ds(k, ks // 2, stride=2), :].astype(jnp.float32).astype(jnp.bfloat16)
        pick = jnp.where(hit & (col >> 6 == k), 1.0, 0.0).astype(jnp.bfloat16)
        seen = seen + jnp.dot(rows, pick, preferred_element_type=jnp.float32)
    seen = seen.astype(jnp.int32)
    lane = lax.broadcasted_iota(jnp.int32, (16, 128), 1)
    blocks = []
    for two in range(2):
        full = terms[0, two]
        for i in range(1, 8):
            full = full + terms[i, two]
        turned = pltpu.roll(full, 64, 1)
        blocks.append(jnp.where(lane < 64, full, turned))
        blocks.append(jnp.where(lane < 64, turned, full))
    mine = (2 * r, 2 * r + 1, 2 * (r ^ 1), 2 * (r ^ 1) + 1)
    for target in range(out.shape[0]):
        wanted = jnp.broadcast_to(seen[target : target + 1, :], (16, 128))
        block = jnp.zeros((16, 128), jnp.float32)
        for q in range(4):
            block = jnp.where(wanted == mine[q], blocks[q], block)
        out[target] = block.astype(out.dtype)


def spread(q_index, terms):
    vmem = pl.BlockSpec(memory_space=pltpu.VMEM)
    return pl.pallas_call(
        spread_kernel,
        in_specs=[vmem, vmem],
        out_specs=vmem,
        out_shape=jax.ShapeDtypeStruct((32, 16, 128), jnp.float32),
        name="spread",
    )(q_index, terms)


def settle_kernel(arrived, out):
    lane = lax.broadcasted_iota(jnp.int32, (16, 128), 1) // 32
    sums = []
    for c in range(2):
        full = arrived[c].astype(jnp.float32)
        for r in range(2 + c, arrived.shape[0], 2):
            full = full + arrived[r].astype(jnp.float32)
        sums.append(full)
    for k in range(2):
        block = jnp.zeros((16, 128), jnp.float32)
        for z in range(2):
            for c in range(2):
                move = (z * 64 + c * 32 - k * 64 - z * 32) % 128
                turned = pltpu.roll(sums[c], move, 1) if move else sums[c]
                block = jnp.where(lane == 2 * z + c, turned, block)
        out[16 * k : 16 * k + 16, :] = block


def settle(arrived):
    vmem = pl.BlockSpec(memory_space=pltpu.VMEM)
    return pl.pallas_call(
        settle_kernel,
        in_specs=[vmem],
        out_specs=vmem,
        out_shape=jax.ShapeDtypeStruct((32, 128), jnp.float32),
        name="settle",
    )(arrived)


def local(pair_matrix, screened, coulomb, q_index):
    bands, share = pair_matrix.shape[1:]
    r = lax.axis_index("row")
    w_other = send(screened, SWAP)
    own = pair_matrix.reshape(1, 2 * bands, share)
    even = jnp.concatenate([own] + [send(own, along_z(s)) for s in ZSHIFTS[1:]], axis=0)
    paired = send(even, ZPAIR)
    q_mine = jnp.stack([2 * r, 2 * r + 1, 2 * (r ^ 1), 2 * (r ^ 1) + 1])
    ks = lax.iota(jnp.int32, q_index.shape[0])
    partner = jnp.sum(
        jnp.where(q_index[None] == q_mine[:, None, None], ks[None, :, None], 0), axis=1
    ).astype(jnp.int32)
    paired, partner, coulomb, w_other = lax.optimization_barrier(
        (paired, partner, coulomb.reshape(1, share), w_other)
    )
    stack = jnp.concatenate([even, paired], axis=0).reshape(1, NZ * 32, share)
    near = send(stack, SWAP)
    far = send(stack, ACROSS)
    parts = [send(stack, first_plane(s)) for s in FIRST[1:]]
    p01 = jnp.concatenate([stack, parts[0]], axis=0)
    p23 = jnp.concatenate([parts[1], parts[2]], axis=0)

    f0 = send(p01, second_plane(1))
    g1 = send(p23, second_plane(-1))
    late01, late23, near, far = lax.optimization_barrier((p01, p23, near, far))
    g0 = send(late01, second_plane(-1))
    f1 = send(late23, second_plane(1))
    ff0 = send(f0, second_plane(1))
    gg1 = send(g1, second_plane(-1))

    panels = (p01, p23, f0, f1, g0, g1, ff0, gg1)
    terms = solve(partner, coulomb, screened, w_other, panels, near, far)
    terms = lax.all_to_all(terms, "col", split_axis=0, concat_axis=0, tiled=True)
    placed = spread(q_index, terms)
    arrived = lax.all_to_all(placed, "row", split_axis=0, concat_axis=0, tiled=True)
    return settle(arrived)


def solution(mesh):
    placed = (P("row", None, "col"), P("row", "col", None), P("col"), P())
    return jax.shard_map(
        local, mesh=mesh, in_specs=placed, out_specs=P("row", "col"), check_vma=False
    )
```

```python
import jax
import jax.numpy as jnp
from jax import lax
from jax.experimental import pallas as pl
from jax.experimental.pallas import tpu as pltpu
from jax.sharding import PartitionSpec as P

AXES = ("row", "col")
NX, NY, NZ, NCORE = 4, 4, 8, 2
FIRST = (0, 1, 2, -1)
SECOND = (0, 2, 1, -1)
ZSHIFTS = (0, 2, 4, -2)
MIB = 1024 * 1024


def device_index(x, y, z, c):
    y_hi, y_lo = divmod(y % NY, 2)
    row = (y_lo * NZ + z % NZ) * NCORE + c
    return row * 8 + y_hi * NX + x % NX


def pairs(move):
    found = []
    for x in range(NX):
        for y in range(NY):
            for z in range(NZ):
                for c in range(NCORE):
                    found.append((device_index(x, y, z, c), device_index(*move(x, y, z, c))))
    return found


SWAP = pairs(lambda x, y, z, c: (x, y, z, 1 - c))
ACROSS = pairs(lambda x, y, z, c: (x, y ^ 1, z, 1 - c))
ZPAIR = pairs(lambda x, y, z, c: (x, y, z ^ 1, c))


def along_z(s):
    return pairs(lambda x, y, z, c: (x, y, z + s, c))


def first_plane(s):
    return pairs(lambda x, y, z, c: (x + s, y, z, c) if c == 0 else (x, y + s, z, c))


def second_plane(s):
    return pairs(lambda x, y, z, c: (x, y + s, z, c) if c == 0 else (x + s, y, z, c))


def send(value, perm):
    return lax.ppermute(value, AXES, perm)


def contract(a, b):
    return lax.dot_general(a, b, (((1,), (1,)), ((), ())), preferred_element_type=jnp.float32)


def where_am_i():
    r, j = lax.axis_index("row"), lax.axis_index("col")
    return r, j, r & 1, (r >> 1) & 7, r >> 4


def spot(k, i):
    r, j, c, _, y_lo = where_am_i()
    first, second = FIRST[i], SECOND[k]
    x = ((j & 3) - first - c * (second - first)) & 3
    y = (2 * (j >> 2) + y_lo - second - c * (first - second)) & 3
    return (y >> 1) * NX + x, y & 1


def place_of(z_wanted):
    z = where_am_i()[3]
    side = (z ^ z_wanted) & 1
    return side * 4 + ((((z ^ side) - z_wanted) & 7) >> 1)


def load_kernel(own, other, out, sems):
    copies = [
        pltpu.make_async_copy(w.at[q], out.at[2 * i + q], sems.at[2 * i + q])
        for i, w in enumerate((own, other))
        for q in range(2)
    ]
    for copy in copies:
        copy.start()
    for copy in copies:
        copy.wait()


def load(own, other):
    _, share, whole = own.shape
    return pl.pallas_call(
        load_kernel,
        in_specs=[pl.BlockSpec(memory_space=pl.ANY)] * 2,
        out_specs=pl.BlockSpec(memory_space=pltpu.VMEM),
        out_shape=jax.ShapeDtypeStruct((4, share, whole), own.dtype),
        scratch_shapes=[pltpu.SemaphoreType.DMA((4,))],
        compiler_params=pltpu.CompilerParams(vmem_limit_bytes=16 * MIB),
        cost_estimate=pl.CostEstimate(
            flops=0, bytes_accessed=8 * share * whole * 2, transcendentals=0
        ),
        name="load",
    )(own, other)


def solve_kernel(
    partner, coulomb, w, p01, p23, f0, f1, g0, g1, ff0, gg1, near, far, out,
    panel, left_rows, image,
):
    rows, share = p01.shape[1:]
    _, j, c, _, y_lo = where_am_i()
    starts = [pl.multiple_of(place_of(z) * 32, 32) for z in range(NZ)]
    arrays = ((p01, p23), (ff0, gg1), (f0, f1), (g0, g1))
    for k in range(4):
        for i in range(4):
            col, low = spot(k, i)
            for z in range(NZ):
                to = pl.multiple_of(low * rows + z * 32, 32)
                piece = arrays[k][i // 2][i % 2, pl.ds(starts[z], 32), :]
                panel[pl.ds(to, 32), pl.ds(pl.multiple_of(col * share, share), share)] = piece
    left_rows[: 2 * rows, :] = panel[:, pl.ds(pl.multiple_of(j * share, share), share)]
    for low, stack in ((y_lo, near), (1 - y_lo, far)):
        for z in range(NZ):
            to = pl.multiple_of((2 + low) * rows + z * 32, 32)
            left_rows[pl.ds(to, 32), :] = stack[0, pl.ds(starts[z], 32), :]
    for q in range(4):
        image[q] = contract(w[q], panel[...]).astype(image.dtype)

    lane = lax.broadcasted_iota(jnp.int32, (16, 128), 1)
    twice = 2.0 * coulomb[...]
    for pair in range(4):
        columns = left_rows[128 * pair : 128 * pair + 128, :]
        blocks = []
        for q in range(4):
            left = []
            for i in range(8):
                k = partner[q, 16 * pair + 8 * (i // 4) + 4 * (i // 2 % 2) + 2 * c + i % 2]
                block = ((((k >> 1) & 1) ^ c) * 2 + (k >> 5)) * NZ + ((k >> 2) & 7)
                start = pl.multiple_of(block * 32 + (k & 1) * 16, 16)
                left.append(left_rows[pl.ds(start, 16), :])
            left = jnp.concatenate(left, axis=0)
            weighted = (left.astype(jnp.float32) * twice).astype(left.dtype)
            met = contract(weighted, columns) - jnp.dot(
                left,
                image[q, :, 128 * pair : 128 * pair + 128],
                preferred_element_type=jnp.float32,
            )
            block = jnp.zeros((16, 128), jnp.float32)
            for i in range(8):
                block = jnp.where(lane // 16 == i, met[16 * i : 16 * i + 16], block)
            blocks.append(block)
        for two in range(2):
            even, odd = blocks[2 * two], blocks[2 * two + 1]
            out[2 * pair, two] = jnp.where(lane < 64, even, pltpu.roll(odd, 64, 1))
            out[2 * pair + 1, two] = jnp.where(lane < 64, pltpu.roll(even, 64, 1), odd)


def solve(partner, coulomb, w, panels, near, far):
    rows, share = panels[0].shape[1:]
    whole = w.shape[2]
    vmem = pl.BlockSpec(memory_space=pltpu.VMEM)
    return pl.pallas_call(
        solve_kernel,
        in_specs=[pl.BlockSpec(memory_space=pltpu.SMEM)] + [vmem] * 12,
        out_specs=vmem,
        out_shape=jax.ShapeDtypeStruct((8, 2, 16, 128), jnp.float32),
        scratch_shapes=[
            pltpu.VMEM((2 * rows, whole), jnp.bfloat16),
            pltpu.VMEM((4 * rows, share), jnp.bfloat16),
            pltpu.VMEM((4, share, 2 * rows), jnp.bfloat16),
        ],
        compiler_params=pltpu.CompilerParams(vmem_limit_bytes=24 * MIB),
        cost_estimate=pl.CostEstimate(
            flops=2 * 4 * share * whole * 2 * rows,
            bytes_accessed=4 * share * whole * 2,
            transcendentals=0,
        ),
        name="solve",
    )(partner, coulomb, w, *panels, near, far)


def spread_kernel(q_index, terms, out):
    r, j, c, _, _ = where_am_i()
    ks = q_index.shape[0]
    row = lax.broadcasted_iota(jnp.int32, (ks, 128), 0)
    col = lax.broadcasted_iota(jnp.int32, (ks, 128), 1)
    slot = (col & 63) >> 4
    hit = row == 8 * j + 4 * (slot >> 1) + 2 * c + (slot & 1)
    seen = jnp.zeros((ks // 2, 128), jnp.float32)
    for k in range(2):
        rows = q_index[pl.ds(k, ks // 2, stride=2), :].astype(jnp.float32).astype(jnp.bfloat16)
        pick = jnp.where(hit & (col >> 6 == k), 1.0, 0.0).astype(jnp.bfloat16)
        seen = seen + jnp.dot(rows, pick, preferred_element_type=jnp.float32)
    seen = seen.astype(jnp.int32)
    lane = lax.broadcasted_iota(jnp.int32, (16, 128), 1)
    blocks = []
    for two in range(2):
        full = terms[0, two]
        for i in range(1, 8):
            full = full + terms[i, two]
        turned = pltpu.roll(full, 64, 1)
        blocks.append(jnp.where(lane < 64, full, turned))
        blocks.append(jnp.where(lane < 64, turned, full))
    mine = (2 * r, 2 * r + 1, 2 * (r ^ 1), 2 * (r ^ 1) + 1)
    for target in range(out.shape[0]):
        wanted = jnp.broadcast_to(seen[target : target + 1, :], (16, 128))
        block = jnp.zeros((16, 128), jnp.float32)
        for q in range(4):
            block = jnp.where(wanted == mine[q], blocks[q], block)
        out[target] = block.astype(out.dtype)


def spread(q_index, terms):
    vmem = pl.BlockSpec(memory_space=pltpu.VMEM)
    return pl.pallas_call(
        spread_kernel,
        in_specs=[vmem, vmem],
        out_specs=vmem,
        out_shape=jax.ShapeDtypeStruct((32, 16, 128), jnp.float32),
        name="spread",
    )(q_index, terms)


def settle_kernel(arrived, out):
    lane = lax.broadcasted_iota(jnp.int32, (16, 128), 1) // 32
    sums = []
    for c in range(2):
        full = arrived[c].astype(jnp.float32)
        for r in range(2 + c, arrived.shape[0], 2):
            full = full + arrived[r].astype(jnp.float32)
        sums.append(full)
    for k in range(2):
        block = jnp.zeros((16, 128), jnp.float32)
        for z in range(2):
            for c in range(2):
                move = (z * 64 + c * 32 - k * 64 - z * 32) % 128
                turned = pltpu.roll(sums[c], move, 1) if move else sums[c]
                block = jnp.where(lane == 2 * z + c, turned, block)
        out[16 * k : 16 * k + 16, :] = block


def settle(arrived):
    vmem = pl.BlockSpec(memory_space=pltpu.VMEM)
    return pl.pallas_call(
        settle_kernel,
        in_specs=[vmem],
        out_specs=vmem,
        out_shape=jax.ShapeDtypeStruct((32, 128), jnp.float32),
        name="settle",
    )(arrived)


def local(pair_matrix, screened, coulomb, q_index):
    bands, share = pair_matrix.shape[1:]
    r = lax.axis_index("row")
    w_other = send(screened, SWAP)
    own = pair_matrix.reshape(1, 2 * bands, share)
    even = jnp.concatenate([own] + [send(own, along_z(s)) for s in ZSHIFTS[1:]], axis=0)
    paired = send(even, ZPAIR)
    q_mine = jnp.stack([2 * r, 2 * r + 1, 2 * (r ^ 1), 2 * (r ^ 1) + 1])
    ks = lax.iota(jnp.int32, q_index.shape[0])
    partner = jnp.sum(
        jnp.where(q_index[None] == q_mine[:, None, None], ks[None, :, None], 0), axis=1
    ).astype(jnp.int32)
    paired, partner, coulomb, w_other = lax.optimization_barrier(
        (paired, partner, coulomb.reshape(1, share), w_other)
    )
    stack = jnp.concatenate([even, paired], axis=0).reshape(1, NZ * 32, share)
    near = send(stack, SWAP)
    far = send(stack, ACROSS)
    parts = [send(stack, first_plane(s)) for s in FIRST[1:]]
    parts, near, far = lax.optimization_barrier((parts, near, far))
    p01 = jnp.concatenate([stack, parts[0]], axis=0)
    p23 = jnp.concatenate([parts[1], parts[2]], axis=0)

    f0 = send(p01, second_plane(1))
    g1 = send(p23, second_plane(-1))
    g0 = send(p01, second_plane(-1))
    f1 = send(p23, second_plane(1))
    ff0 = send(f0, second_plane(1))
    gg1 = send(g1, second_plane(-1))

    w_own, w_other, f0, g1 = lax.optimization_barrier((screened, w_other, f0, g1))
    w = load(w_own, w_other)
    panels = (p01, p23, f0, f1, g0, g1, ff0, gg1)
    terms = solve(partner, coulomb, w, panels, near, far)
    terms = lax.all_to_all(terms, "col", split_axis=0, concat_axis=0, tiled=True)
    placed = spread(q_index, terms)
    arrived = lax.all_to_all(placed, "row", split_axis=0, concat_axis=0, tiled=True)
    return settle(arrived)


def solution(mesh):
    placed = (P("row", None, "col"), P("row", "col", None), P("col"), P())
    return jax.shard_map(
        local, mesh=mesh, in_specs=placed, out_specs=P("row", "col"), check_vma=False
    )
```

```python
import jax
import jax.numpy as jnp
from jax import lax
from jax.experimental import pallas as pl
from jax.experimental.pallas import tpu as pltpu
from jax.sharding import PartitionSpec as P

AXES = ("row", "col")
NX, NY, NZ, NCORE = 4, 4, 8, 2
FIRST = (0, 1, 2, -1)
SECOND = (0, 2, 1, -1)
ZSHIFTS = (0, 2, 4, -2)
MIB = 1024 * 1024


def device_index(x, y, z, c):
    y_hi, y_lo = divmod(y % NY, 2)
    row = (y_lo * NZ + z % NZ) * NCORE + c
    return row * 8 + y_hi * NX + x % NX


def pairs(move):
    found = []
    for x in range(NX):
        for y in range(NY):
            for z in range(NZ):
                for c in range(NCORE):
                    found.append((device_index(x, y, z, c), device_index(*move(x, y, z, c))))
    return found


SWAP = pairs(lambda x, y, z, c: (x, y, z, 1 - c))
ACROSS = pairs(lambda x, y, z, c: (x, y ^ 1, z, 1 - c))
ZPAIR = pairs(lambda x, y, z, c: (x, y, z ^ 1, c))


def along_z(s):
    return pairs(lambda x, y, z, c: (x, y, z + s, c))


def first_plane(s):
    return pairs(lambda x, y, z, c: (x + s, y, z, c) if c == 0 else (x, y + s, z, c))


def second_plane(s):
    return pairs(lambda x, y, z, c: (x, y + s, z, c) if c == 0 else (x + s, y, z, c))


def send(value, perm):
    return lax.ppermute(value, AXES, perm)


def contract(a, b):
    return lax.dot_general(a, b, (((1,), (1,)), ((), ())), preferred_element_type=jnp.float32)


def where_am_i():
    r, j = lax.axis_index("row"), lax.axis_index("col")
    return r, j, r & 1, (r >> 1) & 7, r >> 4


def spot(k, i):
    r, j, c, _, y_lo = where_am_i()
    first, second = FIRST[i], SECOND[k]
    x = ((j & 3) - first - c * (second - first)) & 3
    y = (2 * (j >> 2) + y_lo - second - c * (first - second)) & 3
    return (y >> 1) * NX + x, y & 1


def place_of(z_wanted):
    z = where_am_i()[3]
    side = (z ^ z_wanted) & 1
    return side * 4 + ((((z ^ side) - z_wanted) & 7) >> 1)


def load_kernel(own, other, out, sems):
    copies = [
        pltpu.make_async_copy(w.at[q], out.at[2 * i + q], sems.at[2 * i + q])
        for i, w in enumerate((own, other))
        for q in range(2)
    ]
    for copy in copies:
        copy.start()
    for copy in copies:
        copy.wait()


def load(own, other):
    _, share, whole = own.shape
    return pl.pallas_call(
        load_kernel,
        in_specs=[pl.BlockSpec(memory_space=pl.ANY)] * 2,
        out_specs=pl.BlockSpec(memory_space=pltpu.VMEM),
        out_shape=jax.ShapeDtypeStruct((4, share, whole), own.dtype),
        scratch_shapes=[pltpu.SemaphoreType.DMA((4,))],
        compiler_params=pltpu.CompilerParams(vmem_limit_bytes=16 * MIB),
        cost_estimate=pl.CostEstimate(
            flops=0, bytes_accessed=8 * share * whole * 2, transcendentals=0
        ),
        name="load",
    )(own, other)


def solve_kernel(
    partner, coulomb, w, p01, p23, f0, f1, g0, g1, ff0, gg1, near, far, out,
    panel, left_rows, image,
):
    rows, share = p01.shape[1:]
    _, j, c, _, y_lo = where_am_i()
    starts = [pl.multiple_of(place_of(z) * 32, 32) for z in range(NZ)]
    arrays = ((p01, p23), (ff0, gg1), (f0, f1), (g0, g1))
    for k in range(4):
        for i in range(4):
            col, low = spot(k, i)
            for z in range(NZ):
                to = pl.multiple_of(low * rows + z * 32, 32)
                piece = arrays[k][i // 2][i % 2, pl.ds(starts[z], 32), :]
                panel[pl.ds(to, 32), pl.ds(pl.multiple_of(col * share, share), share)] = piece
    left_rows[: 2 * rows, :] = panel[:, pl.ds(pl.multiple_of(j * share, share), share)]
    for low, stack in ((y_lo, near), (1 - y_lo, far)):
        for z in range(NZ):
            to = pl.multiple_of((2 + low) * rows + z * 32, 32)
            left_rows[pl.ds(to, 32), :] = stack[0, pl.ds(starts[z], 32), :]
    for q in range(4):
        image[q] = contract(w[q], panel[...]).astype(image.dtype)

    lane = lax.broadcasted_iota(jnp.int32, (16, 128), 1)
    twice = 2.0 * coulomb[...]
    for pair in range(4):
        columns = left_rows[128 * pair : 128 * pair + 128, :]
        blocks = []
        for q in range(4):
            left = []
            for i in range(8):
                k = partner[q, 16 * pair + 8 * (i // 4) + 4 * (i // 2 % 2) + 2 * c + i % 2]
                block = ((((k >> 1) & 1) ^ c) * 2 + (k >> 5)) * NZ + ((k >> 2) & 7)
                start = pl.multiple_of(block * 32 + (k & 1) * 16, 16)
                left.append(left_rows[pl.ds(start, 16), :])
            left = jnp.concatenate(left, axis=0)
            weighted = (left.astype(jnp.float32) * twice).astype(left.dtype)
            met = contract(weighted, columns) - jnp.dot(
                left,
                image[q, :, 128 * pair : 128 * pair + 128],
                preferred_element_type=jnp.float32,
            )
            block = jnp.zeros((16, 128), jnp.float32)
            for i in range(8):
                block = jnp.where(lane // 16 == i, met[16 * i : 16 * i + 16], block)
            blocks.append(block)
        for two in range(2):
            even, odd = blocks[2 * two], blocks[2 * two + 1]
            out[2 * pair, two] = jnp.where(lane < 64, even, pltpu.roll(odd, 64, 1))
            out[2 * pair + 1, two] = jnp.where(lane < 64, pltpu.roll(even, 64, 1), odd)


def solve(partner, coulomb, w, panels, near, far):
    rows, share = panels[0].shape[1:]
    whole = w.shape[2]
    vmem = pl.BlockSpec(memory_space=pltpu.VMEM)
    return pl.pallas_call(
        solve_kernel,
        in_specs=[pl.BlockSpec(memory_space=pltpu.SMEM)] + [vmem] * 12,
        out_specs=vmem,
        out_shape=jax.ShapeDtypeStruct((8, 2, 16, 128), jnp.float32),
        scratch_shapes=[
            pltpu.VMEM((2 * rows, whole), jnp.bfloat16),
            pltpu.VMEM((4 * rows, share), jnp.bfloat16),
            pltpu.VMEM((4, share, 2 * rows), jnp.bfloat16),
        ],
        compiler_params=pltpu.CompilerParams(vmem_limit_bytes=24 * MIB),
        cost_estimate=pl.CostEstimate(
            flops=2 * 4 * share * whole * 2 * rows,
            bytes_accessed=4 * share * whole * 2,
            transcendentals=0,
        ),
        name="solve",
    )(partner, coulomb, w, *panels, near, far)


def spread_kernel(q_index, terms, out):
    r, j, c, _, _ = where_am_i()
    ks = q_index.shape[0]
    row = lax.broadcasted_iota(jnp.int32, (ks, 128), 0)
    col = lax.broadcasted_iota(jnp.int32, (ks, 128), 1)
    slot = (col & 63) >> 4
    hit = row == 8 * j + 4 * (slot >> 1) + 2 * c + (slot & 1)
    seen = jnp.zeros((ks // 2, 128), jnp.float32)
    for k in range(2):
        rows = q_index[pl.ds(k, ks // 2, stride=2), :].astype(jnp.float32).astype(jnp.bfloat16)
        pick = jnp.where(hit & (col >> 6 == k), 1.0, 0.0).astype(jnp.bfloat16)
        seen = seen + jnp.dot(rows, pick, preferred_element_type=jnp.float32)
    seen = seen.astype(jnp.int32)
    lane = lax.broadcasted_iota(jnp.int32, (16, 128), 1)
    blocks = []
    for two in range(2):
        full = terms[0, two]
        for i in range(1, 8):
            full = full + terms[i, two]
        turned = pltpu.roll(full, 64, 1)
        blocks.append(jnp.where(lane < 64, full, turned))
        blocks.append(jnp.where(lane < 64, turned, full))
    mine = (2 * r, 2 * r + 1, 2 * (r ^ 1), 2 * (r ^ 1) + 1)
    for target in range(out.shape[0]):
        wanted = jnp.broadcast_to(seen[target : target + 1, :], (16, 128))
        block = jnp.zeros((16, 128), jnp.float32)
        for q in range(4):
            block = jnp.where(wanted == mine[q], blocks[q], block)
        out[target] = block.astype(out.dtype)


def spread(q_index, terms):
    vmem = pl.BlockSpec(memory_space=pltpu.VMEM)
    return pl.pallas_call(
        spread_kernel,
        in_specs=[vmem, vmem],
        out_specs=vmem,
        out_shape=jax.ShapeDtypeStruct((32, 16, 128), jnp.bfloat16),
        compiler_params=pltpu.CompilerParams(vmem_limit_bytes=4 * MIB),
        name="spread",
    )(q_index, terms)


def settle_kernel(arrived, out):
    lane = lax.broadcasted_iota(jnp.int32, (16, 128), 1) // 32
    sums = []
    for c in range(2):
        full = arrived[c].astype(jnp.float32)
        for r in range(2 + c, arrived.shape[0], 2):
            full = full + arrived[r].astype(jnp.float32)
        sums.append(full)
    for k in range(2):
        block = jnp.zeros((16, 128), jnp.float32)
        for z in range(2):
            for c in range(2):
                move = (z * 64 + c * 32 - k * 64 - z * 32) % 128
                turned = pltpu.roll(sums[c], move, 1) if move else sums[c]
                block = jnp.where(lane == 2 * z + c, turned, block)
        out[16 * k : 16 * k + 16, :] = block


def settle(arrived):
    vmem = pl.BlockSpec(memory_space=pltpu.VMEM)
    return pl.pallas_call(
        settle_kernel,
        in_specs=[vmem],
        out_specs=vmem,
        out_shape=jax.ShapeDtypeStruct((32, 128), jnp.float32),
        compiler_params=pltpu.CompilerParams(vmem_limit_bytes=4 * MIB),
        name="settle",
    )(arrived)


def local(pair_matrix, screened, coulomb, q_index):
    bands, share = pair_matrix.shape[1:]
    r = lax.axis_index("row")
    w_other = send(screened, SWAP)
    own = pair_matrix.reshape(1, 2 * bands, share)
    even = jnp.concatenate([own] + [send(own, along_z(s)) for s in ZSHIFTS[1:]], axis=0)
    paired = send(even, ZPAIR)
    q_mine = jnp.stack([2 * r, 2 * r + 1, 2 * (r ^ 1), 2 * (r ^ 1) + 1])
    ks = lax.iota(jnp.int32, q_index.shape[0])
    partner = jnp.sum(
        jnp.where(q_index[None] == q_mine[:, None, None], ks[None, :, None], 0), axis=1
    ).astype(jnp.int32)
    paired, partner, coulomb, w_other = lax.optimization_barrier(
        (paired, partner, coulomb.reshape(1, share), w_other)
    )
    stack = jnp.concatenate([even, paired], axis=0).reshape(1, NZ * 32, share)
    near = send(stack, SWAP)
    far = send(stack, ACROSS)
    parts = [send(stack, first_plane(s)) for s in FIRST[1:]]
    parts, near, far = lax.optimization_barrier((parts, near, far))
    p01 = jnp.concatenate([stack, parts[0]], axis=0)
    p23 = jnp.concatenate([parts[1], parts[2]], axis=0)

    f0 = send(p01, second_plane(1))
    g1 = send(p23, second_plane(-1))
    g0 = send(p01, second_plane(-1))
    f1 = send(p23, second_plane(1))
    ff0 = send(f0, second_plane(1))
    gg1 = send(g1, second_plane(-1))

    w_own, w_other, f0, g1 = lax.optimization_barrier((screened, w_other, f0, g1))
    w = load(w_own, w_other)
    panels = (p01, p23, f0, f1, g0, g1, ff0, gg1)
    terms = solve(partner, coulomb, w, panels, near, far)
    terms = lax.all_to_all(terms, "col", split_axis=0, concat_axis=0, tiled=True)
    placed = spread(q_index, terms)
    arrived = lax.all_to_all(placed, "row", split_axis=0, concat_axis=0, tiled=True)
    return settle(arrived)


def solution(mesh):
    placed = (P("row", None, "col"), P("row", "col", None), P("col"), P())
    return jax.shard_map(
        local, mesh=mesh, in_specs=placed, out_specs=P("row", "col"), check_vma=False
    )
```

```python
import jax
import jax.numpy as jnp
from jax import lax
from jax.experimental import pallas as pl
from jax.experimental.pallas import tpu as pltpu
from jax.sharding import PartitionSpec as P

AXES = ("row", "col")
NX, NY, NZ, NCORE = 4, 4, 8, 2
FIRST = (0, 1, 2, -1)
SECOND = (0, 2, 1, -1)
ZSHIFTS = (0, 2, 4, -2)
MIB = 1024 * 1024


def device_index(x, y, z, c):
    y_hi, y_lo = divmod(y % NY, 2)
    row = (y_lo * NZ + z % NZ) * NCORE + c
    return row * 8 + y_hi * NX + x % NX


def pairs(move):
    found = []
    for x in range(NX):
        for y in range(NY):
            for z in range(NZ):
                for c in range(NCORE):
                    found.append((device_index(x, y, z, c), device_index(*move(x, y, z, c))))
    return found


SWAP = pairs(lambda x, y, z, c: (x, y, z, 1 - c))
ACROSS = pairs(lambda x, y, z, c: (x, y ^ 1, z, 1) if c == 0 else (x, y, z, 0))
ZPAIR = pairs(lambda x, y, z, c: (x, y, z ^ 1, c))


def along_z(s):
    return pairs(lambda x, y, z, c: (x, y, z + s, c))


def first_plane(s):
    return pairs(lambda x, y, z, c: (x + s, y, z, c) if c == 0 else (x, y + s, z, c))


def second_plane(s):
    return pairs(lambda x, y, z, c: (x, y + s, z, c) if c == 0 else (x + s, y, z, c))


def send(value, perm):
    return lax.ppermute(value, AXES, perm)


def contract(a, b):
    return lax.dot_general(a, b, (((1,), (1,)), ((), ())), preferred_element_type=jnp.float32)


def where_am_i():
    r, j = lax.axis_index("row"), lax.axis_index("col")
    return r, j, r & 1, (r >> 1) & 7, r >> 4


def spot(k, i):
    r, j, c, _, y_lo = where_am_i()
    first, second = FIRST[i], SECOND[k]
    x = ((j & 3) - first - c * (second - first)) & 3
    y = (2 * (j >> 2) + y_lo - second - c * (first - second)) & 3
    return (y >> 1) * NX + x, y & 1


def place_of(z_wanted):
    z = where_am_i()[3]
    side = (z ^ z_wanted) & 1
    return side * 4 + ((((z ^ side) - z_wanted) & 7) >> 1)


def load_kernel(own, other, out, sems):
    copies = [
        pltpu.make_async_copy(w.at[q], out.at[2 * i + q], sems.at[2 * i + q])
        for i, w in enumerate((own, other))
        for q in range(2)
    ]
    for copy in copies:
        copy.start()
    for copy in copies:
        copy.wait()


def load(own, other):
    _, share, whole = own.shape
    return pl.pallas_call(
        load_kernel,
        in_specs=[pl.BlockSpec(memory_space=pl.ANY)] * 2,
        out_specs=pl.BlockSpec(memory_space=pltpu.VMEM),
        out_shape=jax.ShapeDtypeStruct((4, share, whole), own.dtype),
        scratch_shapes=[pltpu.SemaphoreType.DMA((4,))],
        compiler_params=pltpu.CompilerParams(vmem_limit_bytes=16 * MIB),
        cost_estimate=pl.CostEstimate(
            flops=0, bytes_accessed=8 * share * whole * 2, transcendentals=0
        ),
        name="load",
    )(own, other)


def solve_kernel(
    partner, coulomb, w, p01, p23, f0, f1, g0, g1, ff0, gg1, near, far, out,
    panel, left_rows, image,
):
    rows, share = p01.shape[1:]
    _, j, c, _, y_lo = where_am_i()
    starts = [pl.multiple_of(place_of(z) * 32, 32) for z in range(NZ)]
    arrays = ((p01, p23), (ff0, gg1), (f0, f1), (g0, g1))
    for k in range(4):
        for i in range(4):
            col, low = spot(k, i)
            for z in range(NZ):
                to = pl.multiple_of(low * rows + z * 32, 32)
                piece = arrays[k][i // 2][i % 2, pl.ds(starts[z], 32), :]
                panel[pl.ds(to, 32), pl.ds(pl.multiple_of(col * share, share), share)] = piece
    left_rows[: 2 * rows, :] = panel[:, pl.ds(pl.multiple_of(j * share, share), share)]
    for low, stack in ((y_lo, near), (1 - y_lo, far)):
        for z in range(NZ):
            to = pl.multiple_of((2 + low) * rows + z * 32, 32)
            left_rows[pl.ds(to, 32), :] = stack[0, pl.ds(starts[z], 32), :]
    for q in range(4):
        image[q] = contract(w[q], panel[...]).astype(image.dtype)

    lane = lax.broadcasted_iota(jnp.int32, (16, 128), 1)
    twice = 2.0 * coulomb[...]
    for pair in range(4):
        columns = left_rows[128 * pair : 128 * pair + 128, :]
        blocks = []
        for q in range(4):
            left = []
            for i in range(8):
                k = partner[q, 16 * pair + 8 * (i // 4) + 4 * (i // 2 % 2) + 2 * c + i % 2]
                block = ((((k >> 1) & 1) ^ c) * 2 + (k >> 5)) * NZ + ((k >> 2) & 7)
                start = pl.multiple_of(block * 32 + (k & 1) * 16, 16)
                left.append(left_rows[pl.ds(start, 16), :])
            left = jnp.concatenate(left, axis=0)
            weighted = (left.astype(jnp.float32) * twice).astype(left.dtype)
            met = contract(weighted, columns) - jnp.dot(
                left,
                image[q, :, 128 * pair : 128 * pair + 128],
                preferred_element_type=jnp.float32,
            )
            block = jnp.zeros((16, 128), jnp.float32)
            for i in range(8):
                block = jnp.where(lane // 16 == i, met[16 * i : 16 * i + 16], block)
            blocks.append(block)
        for two in range(2):
            even, odd = blocks[2 * two], blocks[2 * two + 1]
            out[2 * pair, two] = jnp.where(lane < 64, even, pltpu.roll(odd, 64, 1))
            out[2 * pair + 1, two] = jnp.where(lane < 64, pltpu.roll(even, 64, 1), odd)


def solve(partner, coulomb, w, panels, near, far):
    rows, share = panels[0].shape[1:]
    whole = w.shape[2]
    vmem = pl.BlockSpec(memory_space=pltpu.VMEM)
    return pl.pallas_call(
        solve_kernel,
        in_specs=[pl.BlockSpec(memory_space=pltpu.SMEM)] + [vmem] * 12,
        out_specs=vmem,
        out_shape=jax.ShapeDtypeStruct((8, 2, 16, 128), jnp.float32),
        scratch_shapes=[
            pltpu.VMEM((2 * rows, whole), jnp.bfloat16),
            pltpu.VMEM((4 * rows, share), jnp.bfloat16),
            pltpu.VMEM((4, share, 2 * rows), jnp.bfloat16),
        ],
        compiler_params=pltpu.CompilerParams(vmem_limit_bytes=24 * MIB),
        cost_estimate=pl.CostEstimate(
            flops=2 * 4 * share * whole * 2 * rows,
            bytes_accessed=4 * share * whole * 2,
            transcendentals=0,
        ),
        name="solve",
    )(partner, coulomb, w, *panels, near, far)


def spread_kernel(q_index, terms, out):
    r, j, c, _, _ = where_am_i()
    ks = q_index.shape[0]
    row = lax.broadcasted_iota(jnp.int32, (ks, 128), 0)
    col = lax.broadcasted_iota(jnp.int32, (ks, 128), 1)
    slot = (col & 63) >> 4
    hit = row == 8 * j + 4 * (slot >> 1) + 2 * c + (slot & 1)
    seen = jnp.zeros((ks // 2, 128), jnp.float32)
    for k in range(2):
        rows = q_index[pl.ds(k, ks // 2, stride=2), :].astype(jnp.float32).astype(jnp.bfloat16)
        pick = jnp.where(hit & (col >> 6 == k), 1.0, 0.0).astype(jnp.bfloat16)
        seen = seen + jnp.dot(rows, pick, preferred_element_type=jnp.float32)
    seen = seen.astype(jnp.int32)
    lane = lax.broadcasted_iota(jnp.int32, (16, 128), 1)
    blocks = []
    for two in range(2):
        full = terms[0, two]
        for i in range(1, 8):
            full = full + terms[i, two]
        turned = pltpu.roll(full, 64, 1)
        blocks.append(jnp.where(lane < 64, full, turned))
        blocks.append(jnp.where(lane < 64, turned, full))
    mine = (2 * r, 2 * r + 1, 2 * (r ^ 1), 2 * (r ^ 1) + 1)
    for target in range(out.shape[0]):
        wanted = jnp.broadcast_to(seen[target : target + 1, :], (16, 128))
        block = jnp.zeros((16, 128), jnp.float32)
        for q in range(4):
            block = jnp.where(wanted == mine[q], blocks[q], block)
        out[target] = block.astype(out.dtype)


def spread(q_index, terms):
    vmem = pl.BlockSpec(memory_space=pltpu.VMEM)
    return pl.pallas_call(
        spread_kernel,
        in_specs=[vmem, vmem],
        out_specs=vmem,
        out_shape=jax.ShapeDtypeStruct((32, 16, 128), jnp.bfloat16),
        compiler_params=pltpu.CompilerParams(vmem_limit_bytes=4 * MIB),
        name="spread",
    )(q_index, terms)


def settle_kernel(arrived, out):
    lane = lax.broadcasted_iota(jnp.int32, (16, 128), 1) // 32
    sums = []
    for c in range(2):
        full = arrived[c].astype(jnp.float32)
        for r in range(2 + c, arrived.shape[0], 2):
            full = full + arrived[r].astype(jnp.float32)
        sums.append(full)
    for k in range(2):
        block = jnp.zeros((16, 128), jnp.float32)
        for z in range(2):
            for c in range(2):
                move = (z * 64 + c * 32 - k * 64 - z * 32) % 128
                turned = pltpu.roll(sums[c], move, 1) if move else sums[c]
                block = jnp.where(lane == 2 * z + c, turned, block)
        out[16 * k : 16 * k + 16, :] = block


def settle(arrived):
    vmem = pl.BlockSpec(memory_space=pltpu.VMEM)
    return pl.pallas_call(
        settle_kernel,
        in_specs=[vmem],
        out_specs=vmem,
        out_shape=jax.ShapeDtypeStruct((32, 128), jnp.float32),
        compiler_params=pltpu.CompilerParams(vmem_limit_bytes=4 * MIB),
        name="settle",
    )(arrived)


def local(pair_matrix, screened, coulomb, q_index):
    bands, share = pair_matrix.shape[1:]
    r = lax.axis_index("row")
    w_other = send(screened, SWAP)
    own = pair_matrix.reshape(1, 2 * bands, share)
    even = jnp.concatenate([own] + [send(own, along_z(s)) for s in ZSHIFTS[1:]], axis=0)
    paired = send(even, ZPAIR)
    q_mine = jnp.stack([2 * r, 2 * r + 1, 2 * (r ^ 1), 2 * (r ^ 1) + 1])
    ks = lax.iota(jnp.int32, q_index.shape[0])
    partner = jnp.sum(
        jnp.where(q_index[None] == q_mine[:, None, None], ks[None, :, None], 0), axis=1
    ).astype(jnp.int32)
    paired, partner, coulomb, w_other = lax.optimization_barrier(
        (paired, partner, coulomb.reshape(1, share), w_other)
    )
    stack = jnp.concatenate([even, paired], axis=0).reshape(1, NZ * 32, share)
    parts = [send(stack, first_plane(s)) for s in FIRST[1:]]
    parts[0], near = lax.optimization_barrier((parts[0], send(stack, SWAP)))
    p01 = jnp.concatenate([stack, parts[0]], axis=0)
    p23 = jnp.concatenate([parts[1], parts[2]], axis=0)

    f0 = send(p01, second_plane(1))
    g1 = send(p23, second_plane(-1))
    g0 = send(p01, second_plane(-1))
    f1 = send(p23, second_plane(1))
    ff0 = send(f0, second_plane(1))
    gg1 = send(g1, second_plane(-1))

    core, low = r & 1, r >> 4
    passed = jnp.where(core == 0, stack, jnp.where(low == 0, parts[2], parts[0]))
    w_own, w_other, f0, g1, passed = lax.optimization_barrier(
        (screened, w_other, f0, g1, passed)
    )
    far = send(passed, ACROSS)
    w = load(w_own, w_other)
    panels = (p01, p23, f0, f1, g0, g1, ff0, gg1)
    terms = solve(partner, coulomb, w, panels, near, far)
    terms = lax.all_to_all(terms, "col", split_axis=0, concat_axis=0, tiled=True)
    placed = spread(q_index, terms)
    arrived = lax.all_to_all(placed, "row", split_axis=0, concat_axis=0, tiled=True)
    return settle(arrived)


def solution(mesh):
    placed = (P("row", None, "col"), P("row", "col", None), P("col"), P())
    return jax.shard_map(
        local, mesh=mesh, in_specs=placed, out_specs=P("row", "col"), check_vma=False
    )
```

```python
import jax
import jax.numpy as jnp
from jax import lax
from jax.experimental import pallas as pl
from jax.experimental.pallas import tpu as pltpu
from jax.sharding import PartitionSpec as P

AXES = ("row", "col")
NX, NY, NZ, NCORE = 4, 4, 8, 2
FIRST = (0, 1, 2, -1)
SECOND = (0, 2, 1, -1)
ZSHIFTS = (0, 2, 4, -2)
MIB = 1024 * 1024


def device_index(x, y, z, c):
    y_hi, y_lo = divmod(y % NY, 2)
    row = (y_lo * NZ + z % NZ) * NCORE + c
    return row * 8 + y_hi * NX + x % NX


def pairs(move):
    found = []
    for x in range(NX):
        for y in range(NY):
            for z in range(NZ):
                for c in range(NCORE):
                    found.append((device_index(x, y, z, c), device_index(*move(x, y, z, c))))
    return found


SWAP = pairs(lambda x, y, z, c: (x, y, z, 1 - c))
ACROSS = pairs(lambda x, y, z, c: (x, y ^ 1, z, 1) if c == 0 else (x, y, z, 0))
ZPAIR = pairs(lambda x, y, z, c: (x, y, z ^ 1, c))


def along_z(s):
    return pairs(lambda x, y, z, c: (x, y, z + s, c))


def first_plane(s):
    return pairs(lambda x, y, z, c: (x + s, y, z, c) if c == 0 else (x, y + s, z, c))


def second_plane(s):
    return pairs(lambda x, y, z, c: (x, y + s, z, c) if c == 0 else (x + s, y, z, c))


def send(value, perm):
    return lax.ppermute(value, AXES, perm)


def contract(a, b):
    return lax.dot_general(a, b, (((1,), (1,)), ((), ())), preferred_element_type=jnp.float32)


def where_am_i():
    r, j = lax.axis_index("row"), lax.axis_index("col")
    return r, j, r & 1, (r >> 1) & 7, r >> 4


def spot(k, i):
    r, j, c, _, y_lo = where_am_i()
    first, second = FIRST[i], SECOND[k]
    x = ((j & 3) - first - c * (second - first)) & 3
    y = (2 * (j >> 2) + y_lo - second - c * (first - second)) & 3
    return (y >> 1) * NX + x, y & 1


def place_of(z_wanted):
    z = where_am_i()[3]
    side = (z ^ z_wanted) & 1
    return side * 4 + ((((z ^ side) - z_wanted) & 7) >> 1)


def load_kernel(own, other, out, sems):
    copies = [
        pltpu.make_async_copy(w.at[q], out.at[2 * i + q], sems.at[2 * i + q])
        for i, w in enumerate((own, other))
        for q in range(2)
    ]
    for copy in copies:
        copy.start()
    for copy in copies:
        copy.wait()


def load(own, other):
    _, share, whole = own.shape
    return pl.pallas_call(
        load_kernel,
        in_specs=[pl.BlockSpec(memory_space=pl.ANY)] * 2,
        out_specs=pl.BlockSpec(memory_space=pltpu.VMEM),
        out_shape=jax.ShapeDtypeStruct((4, share, whole), own.dtype),
        scratch_shapes=[pltpu.SemaphoreType.DMA((4,))],
        compiler_params=pltpu.CompilerParams(vmem_limit_bytes=16 * MIB),
        cost_estimate=pl.CostEstimate(
            flops=0, bytes_accessed=8 * share * whole * 2, transcendentals=0
        ),
        name="load",
    )(own, other)


def solve_kernel(
    partner, coulomb, w, p01, p23, f0, f1, g0, g1, ff0, gg1, near, far, out,
    panel, left_rows, image,
):
    rows, share = p01.shape[1:]
    _, j, c, _, y_lo = where_am_i()
    starts = [pl.multiple_of(place_of(z) * 32, 32) for z in range(NZ)]
    arrays = ((p01, p23), (ff0, gg1), (f0, f1), (g0, g1))
    for k in range(4):
        for i in range(4):
            col, low = spot(k, i)
            for z in range(NZ):
                to = pl.multiple_of(low * rows + z * 32, 32)
                piece = arrays[k][i // 2][i % 2, pl.ds(starts[z], 32), :]
                panel[pl.ds(to, 32), pl.ds(pl.multiple_of(col * share, share), share)] = piece
    left_rows[: 2 * rows, :] = panel[:, pl.ds(pl.multiple_of(j * share, share), share)]
    for low, stack in ((y_lo, near), (1 - y_lo, far)):
        for z in range(NZ):
            to = pl.multiple_of((2 + low) * rows + z * 32, 32)
            left_rows[pl.ds(to, 32), :] = stack[0, pl.ds(starts[z], 32), :]
    for q in range(4):
        image[q] = contract(w[q], panel[...]).astype(image.dtype)

    lane = lax.broadcasted_iota(jnp.int32, (16, 128), 1)
    twice = 2.0 * coulomb[...]
    for pair in range(4):
        columns = left_rows[128 * pair : 128 * pair + 128, :]
        blocks = []
        for q in range(4):
            left = []
            for i in range(8):
                k = partner[q, 16 * pair + 8 * (i // 4) + 4 * (i // 2 % 2) + 2 * c + i % 2]
                block = ((((k >> 1) & 1) ^ c) * 2 + (k >> 5)) * NZ + ((k >> 2) & 7)
                start = pl.multiple_of(block * 32 + (k & 1) * 16, 16)
                left.append(left_rows[pl.ds(start, 16), :])
            left = jnp.concatenate(left, axis=0)
            weighted = (left.astype(jnp.float32) * twice).astype(left.dtype)
            met = contract(weighted, columns) - jnp.dot(
                left,
                image[q, :, 128 * pair : 128 * pair + 128],
                preferred_element_type=jnp.float32,
            )
            block = jnp.zeros((16, 128), jnp.float32)
            for i in range(8):
                block = jnp.where(lane // 16 == i, met[16 * i : 16 * i + 16], block)
            blocks.append(block)
        for two in range(2):
            even, odd = blocks[2 * two], blocks[2 * two + 1]
            out[2 * pair, two] = jnp.where(lane < 64, even, pltpu.roll(odd, 64, 1))
            out[2 * pair + 1, two] = jnp.where(lane < 64, pltpu.roll(even, 64, 1), odd)


def solve(partner, coulomb, w, panels, near, far):
    rows, share = panels[0].shape[1:]
    whole = w.shape[2]
    vmem = pl.BlockSpec(memory_space=pltpu.VMEM)
    return pl.pallas_call(
        solve_kernel,
        in_specs=[pl.BlockSpec(memory_space=pltpu.SMEM)] + [vmem] * 12,
        out_specs=vmem,
        out_shape=jax.ShapeDtypeStruct((8, 2, 16, 128), jnp.float32),
        scratch_shapes=[
            pltpu.VMEM((2 * rows, whole), jnp.bfloat16),
            pltpu.VMEM((4 * rows, share), jnp.bfloat16),
            pltpu.VMEM((4, share, 2 * rows), jnp.bfloat16),
        ],
        compiler_params=pltpu.CompilerParams(vmem_limit_bytes=24 * MIB),
        cost_estimate=pl.CostEstimate(
            flops=2 * 4 * share * whole * 2 * rows,
            bytes_accessed=4 * share * whole * 2,
            transcendentals=0,
        ),
        name="solve",
    )(partner, coulomb, w, *panels, near, far)


def spread_kernel(q_index, terms, out):
    r, j, c, _, _ = where_am_i()
    ks = q_index.shape[0]
    row = lax.broadcasted_iota(jnp.int32, (ks, 128), 0)
    col = lax.broadcasted_iota(jnp.int32, (ks, 128), 1)
    slot = (col & 63) >> 4
    hit = row == 8 * j + 4 * (slot >> 1) + 2 * c + (slot & 1)
    seen = jnp.zeros((ks // 2, 128), jnp.float32)
    for k in range(2):
        rows = q_index[pl.ds(k, ks // 2, stride=2), :].astype(jnp.float32).astype(jnp.bfloat16)
        pick = jnp.where(hit & (col >> 6 == k), 1.0, 0.0).astype(jnp.bfloat16)
        seen = seen + jnp.dot(rows, pick, preferred_element_type=jnp.float32)
    seen = seen.astype(jnp.int32)
    lane = lax.broadcasted_iota(jnp.int32, (16, 128), 1)
    blocks = []
    for two in range(2):
        full = terms[0, two]
        for i in range(1, 8):
            full = full + terms[i, two]
        turned = pltpu.roll(full, 64, 1)
        blocks.append(jnp.where(lane < 64, full, turned))
        blocks.append(jnp.where(lane < 64, turned, full))
    mine = (2 * r, 2 * r + 1, 2 * (r ^ 1), 2 * (r ^ 1) + 1)
    for target in range(out.shape[0]):
        wanted = jnp.broadcast_to(seen[target : target + 1, :], (16, 128))
        block = jnp.zeros((16, 128), jnp.float32)
        for q in range(4):
            block = jnp.where(wanted == mine[q], blocks[q], block)
        out[target] = block.astype(out.dtype)


def spread(q_index, terms):
    vmem = pl.BlockSpec(memory_space=pltpu.VMEM)
    return pl.pallas_call(
        spread_kernel,
        in_specs=[vmem, vmem],
        out_specs=vmem,
        out_shape=jax.ShapeDtypeStruct((32, 16, 128), jnp.bfloat16),
        compiler_params=pltpu.CompilerParams(vmem_limit_bytes=4 * MIB),
        name="spread",
    )(q_index, terms)


def settle_kernel(arrived, out):
    lane = lax.broadcasted_iota(jnp.int32, (16, 128), 1) // 32
    sums = []
    for c in range(2):
        full = arrived[c].astype(jnp.float32)
        for r in range(2 + c, arrived.shape[0], 2):
            full = full + arrived[r].astype(jnp.float32)
        sums.append(full)
    for k in range(2):
        block = jnp.zeros((16, 128), jnp.float32)
        for z in range(2):
            for c in range(2):
                move = (z * 64 + c * 32 - k * 64 - z * 32) % 128
                turned = pltpu.roll(sums[c], move, 1) if move else sums[c]
                block = jnp.where(lane == 2 * z + c, turned, block)
        out[16 * k : 16 * k + 16, :] = block


def settle(arrived):
    vmem = pl.BlockSpec(memory_space=pltpu.VMEM)
    return pl.pallas_call(
        settle_kernel,
        in_specs=[vmem],
        out_specs=vmem,
        out_shape=jax.ShapeDtypeStruct((32, 128), jnp.float32),
        compiler_params=pltpu.CompilerParams(vmem_limit_bytes=4 * MIB),
        name="settle",
    )(arrived)


def local(pair_matrix, screened, coulomb, q_index):
    bands, share = pair_matrix.shape[1:]
    r = lax.axis_index("row")
    own = pair_matrix.reshape(1, 2 * bands, share)
    even = jnp.concatenate([own] + [send(own, along_z(s)) for s in ZSHIFTS[1:]], axis=0)
    paired = send(even, ZPAIR)
    q_mine = jnp.stack([2 * r, 2 * r + 1, 2 * (r ^ 1), 2 * (r ^ 1) + 1])
    ks = lax.iota(jnp.int32, q_index.shape[0])
    partner = jnp.sum(
        jnp.where(q_index[None] == q_mine[:, None, None], ks[None, :, None], 0), axis=1
    ).astype(jnp.int32)
    paired, partner, coulomb, screened = lax.optimization_barrier(
        (paired, partner, coulomb.reshape(1, share), screened)
    )
    w_other = send(screened, SWAP)
    stack = jnp.concatenate([even, paired], axis=0).reshape(1, NZ * 32, share)
    parts = [send(stack, first_plane(s)) for s in FIRST[1:]]
    p01 = jnp.concatenate([stack, parts[0]], axis=0)
    p23 = jnp.concatenate([parts[1], parts[2]], axis=0)

    f0 = send(p01, second_plane(1))
    g1 = send(p23, second_plane(-1))
    g0 = send(p01, second_plane(-1))
    f1 = send(p23, second_plane(1))
    ff0 = send(f0, second_plane(1))
    gg1 = send(g1, second_plane(-1))

    core, low = r & 1, r >> 4
    passed = jnp.where(core == 0, stack, jnp.where(low == 0, parts[2], parts[0]))
    w_own, w_other, f0, g1, passed, kept = lax.optimization_barrier(
        (screened, w_other, f0, g1, passed, stack)
    )
    near = send(kept, SWAP)
    far = send(passed, ACROSS)
    w = load(w_own, w_other)
    panels = (p01, p23, f0, f1, g0, g1, ff0, gg1)
    terms = solve(partner, coulomb, w, panels, near, far)
    terms = lax.all_to_all(terms, "col", split_axis=0, concat_axis=0, tiled=True)
    placed = spread(q_index, terms)
    arrived = lax.all_to_all(placed, "row", split_axis=0, concat_axis=0, tiled=True)
    return settle(arrived)


def solution(mesh):
    placed = (P("row", None, "col"), P("row", "col", None), P("col"), P())
    return jax.shard_map(
        local, mesh=mesh, in_specs=placed, out_specs=P("row", "col"), check_vma=False
    )
```

```python
import jax
import jax.numpy as jnp
from jax import lax
from jax.experimental import pallas as pl
from jax.experimental.pallas import tpu as pltpu
from jax.sharding import PartitionSpec as P

AXES = ("row", "col")
NX, NY, NZ, NCORE = 4, 4, 8, 2
FIRST = (0, 1, 2, -1)
SECOND = (0, 2, 1, -1)
ZSHIFTS = (0, 2, 4, -2)
MIB = 1024 * 1024


def device_index(x, y, z, c):
    y_hi, y_lo = divmod(y % NY, 2)
    row = (y_lo * NZ + z % NZ) * NCORE + c
    return row * 8 + y_hi * NX + x % NX


def pairs(move):
    found = []
    for x in range(NX):
        for y in range(NY):
            for z in range(NZ):
                for c in range(NCORE):
                    found.append((device_index(x, y, z, c), device_index(*move(x, y, z, c))))
    return found


SWAP = pairs(lambda x, y, z, c: (x, y, z, 1 - c))
ACROSS = pairs(lambda x, y, z, c: (x, y ^ 1, z, 1) if c == 0 else (x, y, z, 0))
ZPAIR = pairs(lambda x, y, z, c: (x, y, z ^ 1, c))


def along_z(s):
    return pairs(lambda x, y, z, c: (x, y, z + s, c))


def first_plane(s):
    return pairs(lambda x, y, z, c: (x + s, y, z, c) if c == 0 else (x, y + s, z, c))


def second_plane(s):
    return pairs(lambda x, y, z, c: (x, y + s, z, c) if c == 0 else (x + s, y, z, c))


def send(value, perm):
    return lax.ppermute(value, AXES, perm)


def contract(a, b):
    return lax.dot_general(a, b, (((1,), (1,)), ((), ())), preferred_element_type=jnp.float32)


def where_am_i():
    r, j = lax.axis_index("row"), lax.axis_index("col")
    return r, j, r & 1, (r >> 1) & 7, r >> 4


def spot(k, i):
    r, j, c, _, y_lo = where_am_i()
    first, second = FIRST[i], SECOND[k]
    x = ((j & 3) - first - c * (second - first)) & 3
    y = (2 * (j >> 2) + y_lo - second - c * (first - second)) & 3
    return (y >> 1) * NX + x, y & 1


def place_of(z_wanted):
    z = where_am_i()[3]
    side = (z ^ z_wanted) & 1
    return side * 4 + ((((z ^ side) - z_wanted) & 7) >> 1)


def load_kernel(own, other, out, sems):
    copies = [
        pltpu.make_async_copy(w.at[q], out.at[2 * i + q], sems.at[2 * i + q])
        for i, w in enumerate((own, other))
        for q in range(2)
    ]
    for copy in copies:
        copy.start()
    for copy in copies:
        copy.wait()


def load(own, other):
    _, share, whole = own.shape
    return pl.pallas_call(
        load_kernel,
        in_specs=[pl.BlockSpec(memory_space=pl.ANY)] * 2,
        out_specs=pl.BlockSpec(memory_space=pltpu.VMEM),
        out_shape=jax.ShapeDtypeStruct((4, share, whole), own.dtype),
        scratch_shapes=[pltpu.SemaphoreType.DMA((4,))],
        compiler_params=pltpu.CompilerParams(vmem_limit_bytes=16 * MIB),
        cost_estimate=pl.CostEstimate(
            flops=0, bytes_accessed=8 * share * whole * 2, transcendentals=0
        ),
        name="load",
    )(own, other)


def solve_kernel(
    partner, coulomb, w, p01, p23, two01, two2, two3, up01, up23, down012, down3, near, far, out,
    panel, left_rows, image,
):
    rows, share = p01.shape[1:]
    _, j, c, _, y_lo = where_am_i()
    starts = [pl.multiple_of(place_of(z) * 32, 32) for z in range(NZ)]
    pieces = (
        ((p01, 0), (p01, 1), (p23, 0), (p23, 1)),
        ((two01, 0), (two01, 1), (two2, 0), (two3, 0)),
        ((up01, 0), (up01, 1), (up23, 0), (up23, 1)),
        ((down012, 0), (down012, 1), (down012, 2), (down3, 0)),
    )
    for k in range(4):
        for i in range(4):
            col, low = spot(k, i)
            array, at = pieces[k][i]
            for z in range(NZ):
                to = pl.multiple_of(low * rows + z * 32, 32)
                piece = array[at, pl.ds(starts[z], 32), :]
                panel[pl.ds(to, 32), pl.ds(pl.multiple_of(col * share, share), share)] = piece
    left_rows[: 2 * rows, :] = panel[:, pl.ds(pl.multiple_of(j * share, share), share)]
    for low, stack in ((y_lo, near), (1 - y_lo, far)):
        for z in range(NZ):
            to = pl.multiple_of((2 + low) * rows + z * 32, 32)
            left_rows[pl.ds(to, 32), :] = stack[0, pl.ds(starts[z], 32), :]
    for q in range(4):
        image[q] = contract(w[q], panel[...]).astype(image.dtype)

    lane = lax.broadcasted_iota(jnp.int32, (16, 128), 1)
    twice = 2.0 * coulomb[...]
    for pair in range(4):
        columns = left_rows[128 * pair : 128 * pair + 128, :]
        blocks = []
        for q in range(4):
            left = []
            for i in range(8):
                k = partner[q, 16 * pair + 8 * (i // 4) + 4 * (i // 2 % 2) + 2 * c + i % 2]
                block = ((((k >> 1) & 1) ^ c) * 2 + (k >> 5)) * NZ + ((k >> 2) & 7)
                start = pl.multiple_of(block * 32 + (k & 1) * 16, 16)
                left.append(left_rows[pl.ds(start, 16), :])
            left = jnp.concatenate(left, axis=0)
            weighted = (left.astype(jnp.float32) * twice).astype(left.dtype)
            met = contract(weighted, columns) - jnp.dot(
                left,
                image[q, :, 128 * pair : 128 * pair + 128],
                preferred_element_type=jnp.float32,
            )
            block = jnp.zeros((16, 128), jnp.float32)
            for i in range(8):
                block = jnp.where(lane // 16 == i, met[16 * i : 16 * i + 16], block)
            blocks.append(block)
        for two in range(2):
            even, odd = blocks[2 * two], blocks[2 * two + 1]
            out[2 * pair, two] = jnp.where(lane < 64, even, pltpu.roll(odd, 64, 1))
            out[2 * pair + 1, two] = jnp.where(lane < 64, pltpu.roll(even, 64, 1), odd)


def solve(partner, coulomb, w, panels, near, far):
    rows, share = panels[0].shape[1:]
    whole = w.shape[2]
    vmem = pl.BlockSpec(memory_space=pltpu.VMEM)
    return pl.pallas_call(
        solve_kernel,
        in_specs=[pl.BlockSpec(memory_space=pltpu.SMEM)] + [vmem] * 13,
        out_specs=vmem,
        out_shape=jax.ShapeDtypeStruct((8, 2, 16, 128), jnp.float32),
        scratch_shapes=[
            pltpu.VMEM((2 * rows, whole), jnp.bfloat16),
            pltpu.VMEM((4 * rows, share), jnp.bfloat16),
            pltpu.VMEM((4, share, 2 * rows), jnp.bfloat16),
        ],
        compiler_params=pltpu.CompilerParams(vmem_limit_bytes=24 * MIB),
        cost_estimate=pl.CostEstimate(
            flops=2 * 4 * share * whole * 2 * rows,
            bytes_accessed=4 * share * whole * 2,
            transcendentals=0,
        ),
        name="solve",
    )(partner, coulomb, w, *panels, near, far)


def spread_kernel(q_index, terms, out):
    r, j, c, _, _ = where_am_i()
    ks = q_index.shape[0]
    row = lax.broadcasted_iota(jnp.int32, (ks, 128), 0)
    col = lax.broadcasted_iota(jnp.int32, (ks, 128), 1)
    slot = (col & 63) >> 4
    hit = row == 8 * j + 4 * (slot >> 1) + 2 * c + (slot & 1)
    seen = jnp.zeros((ks // 2, 128), jnp.float32)
    for k in range(2):
        rows = q_index[pl.ds(k, ks // 2, stride=2), :].astype(jnp.float32).astype(jnp.bfloat16)
        pick = jnp.where(hit & (col >> 6 == k), 1.0, 0.0).astype(jnp.bfloat16)
        seen = seen + jnp.dot(rows, pick, preferred_element_type=jnp.float32)
    seen = seen.astype(jnp.int32)
    lane = lax.broadcasted_iota(jnp.int32, (16, 128), 1)
    blocks = []
    for two in range(2):
        full = terms[0, two]
        for i in range(1, 8):
            full = full + terms[i, two]
        turned = pltpu.roll(full, 64, 1)
        blocks.append(jnp.where(lane < 64, full, turned))
        blocks.append(jnp.where(lane < 64, turned, full))
    mine = (2 * r, 2 * r + 1, 2 * (r ^ 1), 2 * (r ^ 1) + 1)
    for target in range(out.shape[0]):
        wanted = jnp.broadcast_to(seen[target : target + 1, :], (16, 128))
        block = jnp.zeros((16, 128), jnp.float32)
        for q in range(4):
            block = jnp.where(wanted == mine[q], blocks[q], block)
        out[target] = block.astype(out.dtype)


def spread(q_index, terms):
    vmem = pl.BlockSpec(memory_space=pltpu.VMEM)
    return pl.pallas_call(
        spread_kernel,
        in_specs=[vmem, vmem],
        out_specs=vmem,
        out_shape=jax.ShapeDtypeStruct((32, 16, 128), jnp.bfloat16),
        compiler_params=pltpu.CompilerParams(vmem_limit_bytes=4 * MIB),
        name="spread",
    )(q_index, terms)


def settle_kernel(arrived, out):
    lane = lax.broadcasted_iota(jnp.int32, (16, 128), 1) // 32
    sums = []
    for c in range(2):
        full = arrived[c].astype(jnp.float32)
        for r in range(2 + c, arrived.shape[0], 2):
            full = full + arrived[r].astype(jnp.float32)
        sums.append(full)
    for k in range(2):
        block = jnp.zeros((16, 128), jnp.float32)
        for z in range(2):
            for c in range(2):
                move = (z * 64 + c * 32 - k * 64 - z * 32) % 128
                turned = pltpu.roll(sums[c], move, 1) if move else sums[c]
                block = jnp.where(lane == 2 * z + c, turned, block)
        out[16 * k : 16 * k + 16, :] = block


def settle(arrived):
    vmem = pl.BlockSpec(memory_space=pltpu.VMEM)
    return pl.pallas_call(
        settle_kernel,
        in_specs=[vmem],
        out_specs=vmem,
        out_shape=jax.ShapeDtypeStruct((32, 128), jnp.float32),
        compiler_params=pltpu.CompilerParams(vmem_limit_bytes=4 * MIB),
        name="settle",
    )(arrived)


def local(pair_matrix, screened, coulomb, q_index):
    bands, share = pair_matrix.shape[1:]
    r = lax.axis_index("row")
    w_other = send(screened, SWAP)
    own = pair_matrix.reshape(1, 2 * bands, share)
    even = jnp.concatenate([own] + [send(own, along_z(s)) for s in ZSHIFTS[1:]], axis=0)
    paired = send(even, ZPAIR)
    q_mine = jnp.stack([2 * r, 2 * r + 1, 2 * (r ^ 1), 2 * (r ^ 1) + 1])
    ks = lax.iota(jnp.int32, q_index.shape[0])
    partner = jnp.sum(
        jnp.where(q_index[None] == q_mine[:, None, None], ks[None, :, None], 0), axis=1
    ).astype(jnp.int32)
    paired, partner, coulomb, w_other = lax.optimization_barrier(
        (paired, partner, coulomb.reshape(1, share), w_other)
    )
    stack = jnp.concatenate([even, paired], axis=0).reshape(1, NZ * 32, share)
    parts = [send(stack, first_plane(s)) for s in FIRST[1:]]
    p01 = jnp.concatenate([stack, parts[0]], axis=0)
    p23 = jnp.concatenate([parts[1], parts[2]], axis=0)

    up01 = send(p01, second_plane(1))
    down3 = send(parts[2], second_plane(-1))
    opposite, _ = lax.optimization_barrier((parts[1], parts[2]))
    up23 = send(p23, second_plane(1))
    down012 = send(jnp.concatenate([stack, parts[0], opposite], axis=0), second_plane(-1))
    two2 = send(opposite, second_plane(2))
    two01 = send(up01, second_plane(1))
    two3 = send(down3, second_plane(-1))

    core, low = r & 1, r >> 4
    passed = jnp.where(core == 0, stack, jnp.where(low == 0, parts[2], parts[0]))
    w_own, w_other, up01, down3, passed, kept = lax.optimization_barrier(
        (screened, w_other, up01, down3, passed, stack)
    )
    near = send(kept, SWAP)
    far = send(passed, ACROSS)
    w = load(w_own, w_other)
    panels = (p01, p23, two01, two2, two3, up01, up23, down012, down3)
    terms = solve(partner, coulomb, w, panels, near, far)
    terms = lax.all_to_all(terms, "col", split_axis=0, concat_axis=0, tiled=True)
    placed = spread(q_index, terms)
    arrived = lax.all_to_all(placed, "row", split_axis=0, concat_axis=0, tiled=True)
    return settle(arrived)


def solution(mesh):
    placed = (P("row", None, "col"), P("row", "col", None), P("col"), P())
    return jax.shard_map(
        local, mesh=mesh, in_specs=placed, out_specs=P("row", "col"), check_vma=False
    )
```

```python
import jax
import jax.numpy as jnp
from jax import lax
from jax.experimental import pallas as pl
from jax.experimental.pallas import tpu as pltpu
from jax.sharding import PartitionSpec as P

AXES = ("row", "col")
NX, NY, NZ, NCORE = 4, 4, 8, 2
FIRST = (0, 1, 2, -1)
SECOND = (0, 2, 1, -1)
ZSHIFTS = (0, 2, 4, -2)
MIB = 1024 * 1024


def device_index(x, y, z, c):
    y_hi, y_lo = divmod(y % NY, 2)
    row = (y_lo * NZ + z % NZ) * NCORE + c
    return row * 8 + y_hi * NX + x % NX


def pairs(move):
    found = []
    for x in range(NX):
        for y in range(NY):
            for z in range(NZ):
                for c in range(NCORE):
                    found.append((device_index(x, y, z, c), device_index(*move(x, y, z, c))))
    return found


SWAP = pairs(lambda x, y, z, c: (x, y, z, 1 - c))
ACROSS = pairs(lambda x, y, z, c: (x, y ^ 1, z, 1) if c == 0 else (x, y, z, 0))
ZPAIR = pairs(lambda x, y, z, c: (x, y, z ^ 1, c))


def along_z(s):
    return pairs(lambda x, y, z, c: (x, y, z + s, c))


def first_plane(s):
    return pairs(lambda x, y, z, c: (x + s, y, z, c) if c == 0 else (x, y + s, z, c))


def second_plane(s):
    return pairs(lambda x, y, z, c: (x, y + s, z, c) if c == 0 else (x + s, y, z, c))


def send(value, perm):
    return lax.ppermute(value, AXES, perm)


def contract(a, b):
    return lax.dot_general(a, b, (((1,), (1,)), ((), ())), preferred_element_type=jnp.float32)


def where_am_i():
    r, j = lax.axis_index("row"), lax.axis_index("col")
    return r, j, r & 1, (r >> 1) & 7, r >> 4


def spot(k, i):
    r, j, c, _, y_lo = where_am_i()
    first, second = FIRST[i], SECOND[k]
    x = ((j & 3) - first - c * (second - first)) & 3
    y = (2 * (j >> 2) + y_lo - second - c * (first - second)) & 3
    return (y >> 1) * NX + x, y & 1


def place_of(z_wanted):
    z = where_am_i()[3]
    side = (z ^ z_wanted) & 1
    return (((z ^ side) - z_wanted) & 7) + side


def load_kernel(own, other, out, sems):
    copies = [
        pltpu.make_async_copy(w.at[q], out.at[2 * i + q], sems.at[2 * i + q])
        for i, w in enumerate((own, other))
        for q in range(2)
    ]
    for copy in copies:
        copy.start()
    for copy in copies:
        copy.wait()


def load(own, other):
    _, share, whole = own.shape
    return pl.pallas_call(
        load_kernel,
        in_specs=[pl.BlockSpec(memory_space=pl.ANY)] * 2,
        out_specs=pl.BlockSpec(memory_space=pltpu.VMEM),
        out_shape=jax.ShapeDtypeStruct((4, share, whole), own.dtype),
        scratch_shapes=[pltpu.SemaphoreType.DMA((4,))],
        compiler_params=pltpu.CompilerParams(vmem_limit_bytes=16 * MIB),
        cost_estimate=pl.CostEstimate(
            flops=0, bytes_accessed=8 * share * whole * 2, transcendentals=0
        ),
        name="load",
    )(own, other)


def solve_kernel(
    partner, coulomb, w, p01, p23, f0, f1, g0, g1, ff0, gg1, near, far, out,
    panel, left_rows, image,
):
    rows, share = p01.shape[1:]
    _, j, c, _, y_lo = where_am_i()
    starts = [pl.multiple_of(place_of(z) * 32, 32) for z in range(NZ)]
    arrays = ((p01, p23), (ff0, gg1), (f0, f1), (g0, g1))
    for k in range(4):
        for i in range(4):
            col, low = spot(k, i)
            for z in range(NZ):
                to = pl.multiple_of(low * rows + z * 32, 32)
                piece = arrays[k][i // 2][i % 2, pl.ds(starts[z], 32), :]
                panel[pl.ds(to, 32), pl.ds(pl.multiple_of(col * share, share), share)] = piece
    left_rows[: 2 * rows, :] = panel[:, pl.ds(pl.multiple_of(j * share, share), share)]
    for low, stack in ((y_lo, near), (1 - y_lo, far)):
        for z in range(NZ):
            to = pl.multiple_of((2 + low) * rows + z * 32, 32)
            left_rows[pl.ds(to, 32), :] = stack[0, pl.ds(starts[z], 32), :]
    for q in range(4):
        image[q] = contract(w[q], panel[...]).astype(image.dtype)

    lane = lax.broadcasted_iota(jnp.int32, (16, 128), 1)
    twice = 2.0 * coulomb[...]
    for pair in range(4):
        columns = left_rows[128 * pair : 128 * pair + 128, :]
        blocks = []
        for q in range(4):
            left = []
            for i in range(8):
                k = partner[q, 16 * pair + 8 * (i // 4) + 4 * (i // 2 % 2) + 2 * c + i % 2]
                block = ((((k >> 1) & 1) ^ c) * 2 + (k >> 5)) * NZ + ((k >> 2) & 7)
                start = pl.multiple_of(block * 32 + (k & 1) * 16, 16)
                left.append(left_rows[pl.ds(start, 16), :])
            left = jnp.concatenate(left, axis=0)
            weighted = (left.astype(jnp.float32) * twice).astype(left.dtype)
            met = contract(weighted, columns) - jnp.dot(
                left,
                image[q, :, 128 * pair : 128 * pair + 128],
                preferred_element_type=jnp.float32,
            )
            block = jnp.zeros((16, 128), jnp.float32)
            for i in range(8):
                block = jnp.where(lane // 16 == i, met[16 * i : 16 * i + 16], block)
            blocks.append(block)
        for two in range(2):
            even, odd = blocks[2 * two], blocks[2 * two + 1]
            out[2 * pair, two] = jnp.where(lane < 64, even, pltpu.roll(odd, 64, 1))
            out[2 * pair + 1, two] = jnp.where(lane < 64, pltpu.roll(even, 64, 1), odd)


def solve(partner, coulomb, w, panels, near, far):
    rows, share = panels[0].shape[1:]
    whole = w.shape[2]
    vmem = pl.BlockSpec(memory_space=pltpu.VMEM)
    return pl.pallas_call(
        solve_kernel,
        in_specs=[pl.BlockSpec(memory_space=pltpu.SMEM)] + [vmem] * 12,
        out_specs=vmem,
        out_shape=jax.ShapeDtypeStruct((8, 2, 16, 128), jnp.float32),
        scratch_shapes=[
            pltpu.VMEM((2 * rows, whole), jnp.bfloat16),
            pltpu.VMEM((4 * rows, share), jnp.bfloat16),
            pltpu.VMEM((4, share, 2 * rows), jnp.bfloat16),
        ],
        compiler_params=pltpu.CompilerParams(vmem_limit_bytes=24 * MIB),
        cost_estimate=pl.CostEstimate(
            flops=2 * 4 * share * whole * 2 * rows,
            bytes_accessed=4 * share * whole * 2,
            transcendentals=0,
        ),
        name="solve",
    )(partner, coulomb, w, *panels, near, far)


def spread_kernel(q_index, terms, out):
    r, j, c, _, _ = where_am_i()
    ks = q_index.shape[0]
    row = lax.broadcasted_iota(jnp.int32, (ks, 128), 0)
    col = lax.broadcasted_iota(jnp.int32, (ks, 128), 1)
    slot = (col & 63) >> 4
    hit = row == 8 * j + 4 * (slot >> 1) + 2 * c + (slot & 1)
    seen = jnp.zeros((ks // 2, 128), jnp.float32)
    for k in range(2):
        rows = q_index[pl.ds(k, ks // 2, stride=2), :].astype(jnp.float32).astype(jnp.bfloat16)
        pick = jnp.where(hit & (col >> 6 == k), 1.0, 0.0).astype(jnp.bfloat16)
        seen = seen + jnp.dot(rows, pick, preferred_element_type=jnp.float32)
    seen = seen.astype(jnp.int32)
    lane = lax.broadcasted_iota(jnp.int32, (16, 128), 1)
    blocks = []
    for two in range(2):
        full = terms[0, two]
        for i in range(1, 8):
            full = full + terms[i, two]
        turned = pltpu.roll(full, 64, 1)
        blocks.append(jnp.where(lane < 64, full, turned))
        blocks.append(jnp.where(lane < 64, turned, full))
    mine = (2 * r, 2 * r + 1, 2 * (r ^ 1), 2 * (r ^ 1) + 1)
    for target in range(out.shape[0]):
        wanted = jnp.broadcast_to(seen[target : target + 1, :], (16, 128))
        block = jnp.zeros((16, 128), jnp.float32)
        for q in range(4):
            block = jnp.where(wanted == mine[q], blocks[q], block)
        out[target] = block.astype(out.dtype)


def spread(q_index, terms):
    vmem = pl.BlockSpec(memory_space=pltpu.VMEM)
    return pl.pallas_call(
        spread_kernel,
        in_specs=[vmem, vmem],
        out_specs=vmem,
        out_shape=jax.ShapeDtypeStruct((32, 16, 128), jnp.bfloat16),
        compiler_params=pltpu.CompilerParams(vmem_limit_bytes=4 * MIB),
        name="spread",
    )(q_index, terms)


def settle_kernel(arrived, out):
    lane = lax.broadcasted_iota(jnp.int32, (16, 128), 1) // 32
    sums = []
    for c in range(2):
        full = arrived[c].astype(jnp.float32)
        for r in range(2 + c, arrived.shape[0], 2):
            full = full + arrived[r].astype(jnp.float32)
        sums.append(full)
    for k in range(2):
        block = jnp.zeros((16, 128), jnp.float32)
        for z in range(2):
            for c in range(2):
                move = (z * 64 + c * 32 - k * 64 - z * 32) % 128
                turned = pltpu.roll(sums[c], move, 1) if move else sums[c]
                block = jnp.where(lane == 2 * z + c, turned, block)
        out[16 * k : 16 * k + 16, :] = block


def settle(arrived):
    vmem = pl.BlockSpec(memory_space=pltpu.VMEM)
    return pl.pallas_call(
        settle_kernel,
        in_specs=[vmem],
        out_specs=vmem,
        out_shape=jax.ShapeDtypeStruct((32, 128), jnp.float32),
        compiler_params=pltpu.CompilerParams(vmem_limit_bytes=4 * MIB),
        name="settle",
    )(arrived)


def local(pair_matrix, screened, coulomb, q_index):
    bands, share = pair_matrix.shape[1:]
    r = lax.axis_index("row")
    w_other = send(screened, SWAP)
    own = pair_matrix.reshape(1, 2 * bands, share)
    pair = jnp.concatenate([own, send(own, ZPAIR)], axis=0)
    quads = [send(pair, along_z(s)) for s in ZSHIFTS[1:]]
    q_mine = jnp.stack([2 * r, 2 * r + 1, 2 * (r ^ 1), 2 * (r ^ 1) + 1])
    ks = lax.iota(jnp.int32, q_index.shape[0])
    partner = jnp.sum(
        jnp.where(q_index[None] == q_mine[:, None, None], ks[None, :, None], 0), axis=1
    ).astype(jnp.int32)
    quads, partner, coulomb, w_other = lax.optimization_barrier(
        (quads, partner, coulomb.reshape(1, share), w_other)
    )
    stack = jnp.concatenate([pair] + quads, axis=0).reshape(1, NZ * 32, share)
    parts = [send(stack, first_plane(s)) for s in FIRST[1:]]
    p01 = jnp.concatenate([stack, parts[0]], axis=0)
    p23 = jnp.concatenate([parts[1], parts[2]], axis=0)

    f0 = send(p01, second_plane(1))
    g1 = send(p23, second_plane(-1))
    g0 = send(p01, second_plane(-1))
    f1 = send(p23, second_plane(1))
    ff0 = send(f0, second_plane(1))
    gg1 = send(g1, second_plane(-1))

    core, low = r & 1, r >> 4
    passed = jnp.where(core == 0, stack, jnp.where(low == 0, parts[2], parts[0]))
    w_own, w_other, f0, g1, passed, kept = lax.optimization_barrier(
        (screened, w_other, f0, g1, passed, stack)
    )
    near = send(kept, SWAP)
    far = send(passed, ACROSS)
    w = load(w_own, w_other)
    panels = (p01, p23, f0, f1, g0, g1, ff0, gg1)
    terms = solve(partner, coulomb, w, panels, near, far)
    terms = lax.all_to_all(terms, "col", split_axis=0, concat_axis=0, tiled=True)
    placed = spread(q_index, terms)
    arrived = lax.all_to_all(placed, "row", split_axis=0, concat_axis=0, tiled=True)
    return settle(arrived)


def solution(mesh):
    placed = (P("row", None, "col"), P("row", "col", None), P("col"), P())
    return jax.shard_map(
        local, mesh=mesh, in_specs=placed, out_specs=P("row", "col"), check_vma=False
    )
```

```python
import jax
import jax.numpy as jnp
from jax import lax
from jax.experimental import pallas as pl
from jax.experimental.pallas import tpu as pltpu
from jax.sharding import PartitionSpec as P

AXES = ("row", "col")
NX, NY, NZ, NCORE = 4, 4, 8, 2
FIRST = (0, 2, 1, -1)
SECOND = (0, 2, 1, -1)
ZSHIFTS = (0, 2, 4, -2)
MIB = 1024 * 1024


def device_index(x, y, z, c):
    y_hi, y_lo = divmod(y % NY, 2)
    row = (y_lo * NZ + z % NZ) * NCORE + c
    return row * 8 + y_hi * NX + x % NX


def pairs(move):
    found = []
    for x in range(NX):
        for y in range(NY):
            for z in range(NZ):
                for c in range(NCORE):
                    found.append((device_index(x, y, z, c), device_index(*move(x, y, z, c))))
    return found


SWAP = pairs(lambda x, y, z, c: (x, y, z, 1 - c))
ACROSS = pairs(lambda x, y, z, c: (x, y ^ 1, z, 1) if c == 0 else (x, y, z, 0))
ZPAIR = pairs(lambda x, y, z, c: (x, y, z ^ 1, c))


def along_z(s):
    return pairs(lambda x, y, z, c: (x, y, z + s, c))


def first_plane(s):
    return pairs(lambda x, y, z, c: (x + s, y, z, c) if c == 0 else (x, y + s, z, c))


def second_plane(s):
    return pairs(lambda x, y, z, c: (x, y + s, z, c) if c == 0 else (x + s, y, z, c))


def send(value, perm):
    return lax.ppermute(value, AXES, perm)


def contract(a, b):
    return lax.dot_general(a, b, (((1,), (1,)), ((), ())), preferred_element_type=jnp.float32)


def where_am_i():
    r, j = lax.axis_index("row"), lax.axis_index("col")
    return r, j, r & 1, (r >> 1) & 7, r >> 4


def spot(k, i):
    r, j, c, _, y_lo = where_am_i()
    first, second = FIRST[i], SECOND[k]
    x = ((j & 3) - first - c * (second - first)) & 3
    y = (2 * (j >> 2) + y_lo - second - c * (first - second)) & 3
    return (y >> 1) * NX + x, y & 1


def place_of(z_wanted):
    z = where_am_i()[3]
    side = (z ^ z_wanted) & 1
    return (((z ^ side) - z_wanted) & 7) + side


def load_kernel(own, other, out, sems):
    copies = [
        pltpu.make_async_copy(w.at[q], out.at[2 * i + q], sems.at[2 * i + q])
        for i, w in enumerate((own, other))
        for q in range(2)
    ]
    for copy in copies:
        copy.start()
    for copy in copies:
        copy.wait()


def load(own, other):
    _, share, whole = own.shape
    return pl.pallas_call(
        load_kernel,
        in_specs=[pl.BlockSpec(memory_space=pl.ANY)] * 2,
        out_specs=pl.BlockSpec(memory_space=pltpu.VMEM),
        out_shape=jax.ShapeDtypeStruct((4, share, whole), own.dtype),
        scratch_shapes=[pltpu.SemaphoreType.DMA((4,))],
        compiler_params=pltpu.CompilerParams(vmem_limit_bytes=16 * MIB),
        cost_estimate=pl.CostEstimate(
            flops=0, bytes_accessed=8 * share * whole * 2, transcendentals=0
        ),
        name="load",
    )(own, other)


def solve_kernel(
    partner, coulomb, w, p01, p23, f0, f1, g0, g1, ff0, gg1, near, far, out,
    panel, left_rows, image,
):
    rows, share = p01.shape[1:]
    _, j, c, _, y_lo = where_am_i()
    starts = [pl.multiple_of(place_of(z) * 32, 32) for z in range(NZ)]
    arrays = ((p01, p23), (ff0, gg1), (f0, f1), (g0, g1))
    for k in range(4):
        for i in range(4):
            col, low = spot(k, i)
            for z in range(NZ):
                to = pl.multiple_of(low * rows + z * 32, 32)
                piece = arrays[k][i // 2][i % 2, pl.ds(starts[z], 32), :]
                panel[pl.ds(to, 32), pl.ds(pl.multiple_of(col * share, share), share)] = piece
    left_rows[: 2 * rows, :] = panel[:, pl.ds(pl.multiple_of(j * share, share), share)]
    for low, stack in ((y_lo, near), (1 - y_lo, far)):
        for z in range(NZ):
            to = pl.multiple_of((2 + low) * rows + z * 32, 32)
            left_rows[pl.ds(to, 32), :] = stack[0, pl.ds(starts[z], 32), :]
    for q in range(4):
        image[q] = contract(w[q], panel[...]).astype(image.dtype)

    lane = lax.broadcasted_iota(jnp.int32, (16, 128), 1)
    twice = 2.0 * coulomb[...]
    for pair in range(4):
        columns = left_rows[128 * pair : 128 * pair + 128, :]
        blocks = []
        for q in range(4):
            left = []
            for i in range(8):
                k = partner[q, 16 * pair + 8 * (i // 4) + 4 * (i // 2 % 2) + 2 * c + i % 2]
                block = ((((k >> 1) & 1) ^ c) * 2 + (k >> 5)) * NZ + ((k >> 2) & 7)
                start = pl.multiple_of(block * 32 + (k & 1) * 16, 16)
                left.append(left_rows[pl.ds(start, 16), :])
            left = jnp.concatenate(left, axis=0)
            weighted = (left.astype(jnp.float32) * twice).astype(left.dtype)
            met = contract(weighted, columns) - jnp.dot(
                left,
                image[q, :, 128 * pair : 128 * pair + 128],
                preferred_element_type=jnp.float32,
            )
            block = jnp.zeros((16, 128), jnp.float32)
            for i in range(8):
                block = jnp.where(lane // 16 == i, met[16 * i : 16 * i + 16], block)
            blocks.append(block)
        for two in range(2):
            even, odd = blocks[2 * two], blocks[2 * two + 1]
            out[2 * pair, two] = jnp.where(lane < 64, even, pltpu.roll(odd, 64, 1))
            out[2 * pair + 1, two] = jnp.where(lane < 64, pltpu.roll(even, 64, 1), odd)


def solve(partner, coulomb, w, panels, near, far):
    rows, share = panels[0].shape[1:]
    whole = w.shape[2]
    vmem = pl.BlockSpec(memory_space=pltpu.VMEM)
    return pl.pallas_call(
        solve_kernel,
        in_specs=[pl.BlockSpec(memory_space=pltpu.SMEM)] + [vmem] * 12,
        out_specs=vmem,
        out_shape=jax.ShapeDtypeStruct((8, 2, 16, 128), jnp.float32),
        scratch_shapes=[
            pltpu.VMEM((2 * rows, whole), jnp.bfloat16),
            pltpu.VMEM((4 * rows, share), jnp.bfloat16),
            pltpu.VMEM((4, share, 2 * rows), jnp.bfloat16),
        ],
        compiler_params=pltpu.CompilerParams(vmem_limit_bytes=24 * MIB),
        cost_estimate=pl.CostEstimate(
            flops=2 * 4 * share * whole * 2 * rows,
            bytes_accessed=4 * share * whole * 2,
            transcendentals=0,
        ),
        name="solve",
    )(partner, coulomb, w, *panels, near, far)


def spread_kernel(q_index, terms, out):
    r, j, c, _, _ = where_am_i()
    ks = q_index.shape[0]
    row = lax.broadcasted_iota(jnp.int32, (ks, 128), 0)
    col = lax.broadcasted_iota(jnp.int32, (ks, 128), 1)
    slot = (col & 63) >> 4
    hit = row == 8 * j + 4 * (slot >> 1) + 2 * c + (slot & 1)
    seen = jnp.zeros((ks // 2, 128), jnp.float32)
    for k in range(2):
        rows = q_index[pl.ds(k, ks // 2, stride=2), :].astype(jnp.float32).astype(jnp.bfloat16)
        pick = jnp.where(hit & (col >> 6 == k), 1.0, 0.0).astype(jnp.bfloat16)
        seen = seen + jnp.dot(rows, pick, preferred_element_type=jnp.float32)
    seen = seen.astype(jnp.int32)
    lane = lax.broadcasted_iota(jnp.int32, (16, 128), 1)
    blocks = []
    for two in range(2):
        full = terms[0, two]
        for i in range(1, 8):
            full = full + terms[i, two]
        turned = pltpu.roll(full, 64, 1)
        blocks.append(jnp.where(lane < 64, full, turned))
        blocks.append(jnp.where(lane < 64, turned, full))
    mine = (2 * r, 2 * r + 1, 2 * (r ^ 1), 2 * (r ^ 1) + 1)
    for target in range(out.shape[0]):
        wanted = jnp.broadcast_to(seen[target : target + 1, :], (16, 128))
        block = jnp.zeros((16, 128), jnp.float32)
        for q in range(4):
            block = jnp.where(wanted == mine[q], blocks[q], block)
        out[target] = block.astype(out.dtype)


def spread(q_index, terms):
    vmem = pl.BlockSpec(memory_space=pltpu.VMEM)
    return pl.pallas_call(
        spread_kernel,
        in_specs=[vmem, vmem],
        out_specs=vmem,
        out_shape=jax.ShapeDtypeStruct((32, 16, 128), jnp.bfloat16),
        compiler_params=pltpu.CompilerParams(vmem_limit_bytes=4 * MIB),
        name="spread",
    )(q_index, terms)


def settle_kernel(arrived, out):
    lane = lax.broadcasted_iota(jnp.int32, (16, 128), 1) // 32
    sums = []
    for c in range(2):
        full = arrived[c].astype(jnp.float32)
        for r in range(2 + c, arrived.shape[0], 2):
            full = full + arrived[r].astype(jnp.float32)
        sums.append(full)
    for k in range(2):
        block = jnp.zeros((16, 128), jnp.float32)
        for z in range(2):
            for c in range(2):
                move = (z * 64 + c * 32 - k * 64 - z * 32) % 128
                turned = pltpu.roll(sums[c], move, 1) if move else sums[c]
                block = jnp.where(lane == 2 * z + c, turned, block)
        out[16 * k : 16 * k + 16, :] = block


def settle(arrived):
    vmem = pl.BlockSpec(memory_space=pltpu.VMEM)
    return pl.pallas_call(
        settle_kernel,
        in_specs=[vmem],
        out_specs=vmem,
        out_shape=jax.ShapeDtypeStruct((32, 128), jnp.float32),
        compiler_params=pltpu.CompilerParams(vmem_limit_bytes=4 * MIB),
        name="settle",
    )(arrived)


def local(pair_matrix, screened, coulomb, q_index):
    bands, share = pair_matrix.shape[1:]
    r = lax.axis_index("row")
    w_other = send(screened, SWAP)
    own = pair_matrix.reshape(1, 2 * bands, share)
    pair = jnp.concatenate([own, send(own, ZPAIR)], axis=0)
    quads = [send(pair, along_z(s)) for s in ZSHIFTS[1:]]
    q_mine = jnp.stack([2 * r, 2 * r + 1, 2 * (r ^ 1), 2 * (r ^ 1) + 1])
    ks = lax.iota(jnp.int32, q_index.shape[0])
    partner = jnp.sum(
        jnp.where(q_index[None] == q_mine[:, None, None], ks[None, :, None], 0), axis=1
    ).astype(jnp.int32)
    quads, partner, coulomb, w_other = lax.optimization_barrier(
        (quads, partner, coulomb.reshape(1, share), w_other)
    )
    stack = jnp.concatenate([pair] + quads, axis=0).reshape(1, NZ * 32, share)
    parts = [send(stack, first_plane(s)) for s in FIRST[1:]]
    p01 = jnp.concatenate([stack, parts[0]], axis=0)
    p23 = jnp.concatenate([parts[1], parts[2]], axis=0)

    f0 = send(p01, second_plane(1))
    g1 = send(p23, second_plane(-1))
    g0 = send(p01, second_plane(-1))
    f1 = send(p23, second_plane(1))
    ff0 = send(f0, second_plane(1))
    gg1 = send(g1, second_plane(-1))

    core, low = r & 1, r >> 4
    passed = jnp.where(core == 0, stack, jnp.where(low == 0, parts[2], parts[1]))
    w_own, w_other, f0, g1, passed, kept = lax.optimization_barrier(
        (screened, w_other, f0, g1, passed, stack)
    )
    near = send(kept, SWAP)
    far = send(passed, ACROSS)
    w = load(w_own, w_other)
    panels = (p01, p23, f0, f1, g0, g1, ff0, gg1)
    terms = solve(partner, coulomb, w, panels, near, far)
    terms = lax.all_to_all(terms, "col", split_axis=0, concat_axis=0, tiled=True)
    placed = spread(q_index, terms)
    arrived = lax.all_to_all(placed, "row", split_axis=0, concat_axis=0, tiled=True)
    return settle(arrived)


def solution(mesh):
    placed = (P("row", None, "col"), P("row", "col", None), P("col"), P())
    return jax.shard_map(
        local, mesh=mesh, in_specs=placed, out_specs=P("row", "col"), check_vma=False
    )
```

```python
import jax
import jax.numpy as jnp
from jax import lax
from jax.experimental import pallas as pl
from jax.experimental.pallas import tpu as pltpu
from jax.sharding import PartitionSpec as P

AXES = ("row", "col")
NX, NY, NZ, NCORE = 4, 4, 8, 2
FIRST = (0, 2, 1, -1)
SECOND = (0, 2, 1, -1)
ZSHIFTS = (0, 4, 2, -2)
MIB = 1024 * 1024


def device_index(x, y, z, c):
    y_hi, y_lo = divmod(y % NY, 2)
    row = (y_lo * NZ + z % NZ) * NCORE + c
    return row * 8 + y_hi * NX + x % NX


def pairs(move):
    found = []
    for x in range(NX):
        for y in range(NY):
            for z in range(NZ):
                for c in range(NCORE):
                    found.append((device_index(x, y, z, c), device_index(*move(x, y, z, c))))
    return found


SWAP = pairs(lambda x, y, z, c: (x, y, z, 1 - c))
ACROSS = pairs(lambda x, y, z, c: (x, y ^ 1, z, 1) if c == 0 else (x, y, z, 0))
ZPAIR = pairs(lambda x, y, z, c: (x, y, z ^ 1, c))


def along_z(s):
    return pairs(lambda x, y, z, c: (x, y, z + s, c))


def first_plane(s):
    return pairs(lambda x, y, z, c: (x + s, y, z, c) if c == 0 else (x, y + s, z, c))


def second_plane(s):
    return pairs(lambda x, y, z, c: (x, y + s, z, c) if c == 0 else (x + s, y, z, c))


def send(value, perm):
    return lax.ppermute(value, AXES, perm)


def contract(a, b):
    return lax.dot_general(a, b, (((1,), (1,)), ((), ())), preferred_element_type=jnp.float32)


def where_am_i():
    r, j = lax.axis_index("row"), lax.axis_index("col")
    return r, j, r & 1, (r >> 1) & 7, r >> 4


def spot(k, i):
    r, j, c, _, y_lo = where_am_i()
    first, second = FIRST[i], SECOND[k]
    x = ((j & 3) - first - c * (second - first)) & 3
    y = (2 * (j >> 2) + y_lo - second - c * (first - second)) & 3
    return (y >> 1) * NX + x, y & 1


def place_of(z_wanted):
    z = where_am_i()[3]
    side = (z ^ z_wanted) & 1
    away = ((z ^ side) - z_wanted) & 7
    return 2 * ((away & 2) + (away >> 2)) + side


def load_kernel(own, other, out, sems):
    copies = [
        pltpu.make_async_copy(w.at[q], out.at[2 * i + q], sems.at[2 * i + q])
        for i, w in enumerate((own, other))
        for q in range(2)
    ]
    for copy in copies:
        copy.start()
    for copy in copies:
        copy.wait()


def load(own, other):
    _, share, whole = own.shape
    return pl.pallas_call(
        load_kernel,
        in_specs=[pl.BlockSpec(memory_space=pl.ANY)] * 2,
        out_specs=pl.BlockSpec(memory_space=pltpu.VMEM),
        out_shape=jax.ShapeDtypeStruct((4, share, whole), own.dtype),
        scratch_shapes=[pltpu.SemaphoreType.DMA((4,))],
        compiler_params=pltpu.CompilerParams(vmem_limit_bytes=16 * MIB),
        cost_estimate=pl.CostEstimate(
            flops=0, bytes_accessed=8 * share * whole * 2, transcendentals=0
        ),
        name="load",
    )(own, other)


def solve_kernel(
    partner, coulomb, w, p01, p23, f0, f1, g0, g1, ff0, gg1, near, far, out,
    panel, left_rows, image,
):
    rows, share = p01.shape[1:]
    _, j, c, _, y_lo = where_am_i()
    starts = [pl.multiple_of(place_of(z) * 32, 32) for z in range(NZ)]
    arrays = ((p01, p23), (ff0, gg1), (f0, f1), (g0, g1))
    for k in range(4):
        for i in range(4):
            col, low = spot(k, i)
            for z in range(NZ):
                to = pl.multiple_of(low * rows + z * 32, 32)
                piece = arrays[k][i // 2][i % 2, pl.ds(starts[z], 32), :]
                panel[pl.ds(to, 32), pl.ds(pl.multiple_of(col * share, share), share)] = piece
    left_rows[: 2 * rows, :] = panel[:, pl.ds(pl.multiple_of(j * share, share), share)]
    for low, stack in ((y_lo, near), (1 - y_lo, far)):
        for z in range(NZ):
            to = pl.multiple_of((2 + low) * rows + z * 32, 32)
            left_rows[pl.ds(to, 32), :] = stack[0, pl.ds(starts[z], 32), :]
    for q in range(4):
        image[q] = contract(w[q], panel[...]).astype(image.dtype)

    lane = lax.broadcasted_iota(jnp.int32, (16, 128), 1)
    twice = 2.0 * coulomb[...]
    for pair in range(4):
        columns = left_rows[128 * pair : 128 * pair + 128, :]
        lefts, blocks = [], []
        for q in range(4):
            for i in range(8):
                k = partner[q, 16 * pair + 8 * (i // 4) + 4 * (i // 2 % 2) + 2 * c + i % 2]
                block = ((((k >> 1) & 1) ^ c) * 2 + (k >> 5)) * NZ + ((k >> 2) & 7)
                start = pl.multiple_of(block * 32 + (k & 1) * 16, 16)
                lefts.append(left_rows[pl.ds(start, 16), :])
        lefts = jnp.concatenate(lefts, axis=0)
        weighted = (lefts.astype(jnp.float32) * twice).astype(lefts.dtype)
        bare = contract(weighted, columns)
        for q in range(4):
            met = bare[128 * q : 128 * q + 128] - jnp.dot(
                lefts[128 * q : 128 * q + 128],
                image[q, :, 128 * pair : 128 * pair + 128],
                preferred_element_type=jnp.float32,
            )
            block = jnp.zeros((16, 128), jnp.float32)
            for i in range(8):
                block = jnp.where(lane // 16 == i, met[16 * i : 16 * i + 16], block)
            blocks.append(block)
        for two in range(2):
            even, odd = blocks[2 * two], blocks[2 * two + 1]
            out[2 * pair, two] = jnp.where(lane < 64, even, pltpu.roll(odd, 64, 1))
            out[2 * pair + 1, two] = jnp.where(lane < 64, pltpu.roll(even, 64, 1), odd)


def solve(partner, coulomb, w, panels, near, far):
    rows, share = panels[0].shape[1:]
    whole = w.shape[2]
    vmem = pl.BlockSpec(memory_space=pltpu.VMEM)
    return pl.pallas_call(
        solve_kernel,
        in_specs=[pl.BlockSpec(memory_space=pltpu.SMEM)] + [vmem] * 12,
        out_specs=vmem,
        out_shape=jax.ShapeDtypeStruct((8, 2, 16, 128), jnp.float32),
        scratch_shapes=[
            pltpu.VMEM((2 * rows, whole), jnp.bfloat16),
            pltpu.VMEM((4 * rows, share), jnp.bfloat16),
            pltpu.VMEM((4, share, 2 * rows), jnp.bfloat16),
        ],
        compiler_params=pltpu.CompilerParams(vmem_limit_bytes=24 * MIB),
        cost_estimate=pl.CostEstimate(
            flops=2 * 4 * share * whole * 2 * rows,
            bytes_accessed=4 * share * whole * 2,
            transcendentals=0,
        ),
        name="solve",
    )(partner, coulomb, w, *panels, near, far)


def spread_kernel(q_index, terms, out):
    r, j, c, _, _ = where_am_i()
    ks = q_index.shape[0]
    row = lax.broadcasted_iota(jnp.int32, (ks, 128), 0)
    col = lax.broadcasted_iota(jnp.int32, (ks, 128), 1)
    slot = (col & 63) >> 4
    hit = row == 8 * j + 4 * (slot >> 1) + 2 * c + (slot & 1)
    seen = jnp.zeros((ks // 2, 128), jnp.float32)
    for k in range(2):
        rows = q_index[pl.ds(k, ks // 2, stride=2), :].astype(jnp.float32).astype(jnp.bfloat16)
        pick = jnp.where(hit & (col >> 6 == k), 1.0, 0.0).astype(jnp.bfloat16)
        seen = seen + jnp.dot(rows, pick, preferred_element_type=jnp.float32)
    seen = seen.astype(jnp.int32)
    lane = lax.broadcasted_iota(jnp.int32, (16, 128), 1)
    blocks = []
    for two in range(2):
        full = terms[0, two]
        for i in range(1, 8):
            full = full + terms[i, two]
        turned = pltpu.roll(full, 64, 1)
        blocks.append(jnp.where(lane < 64, full, turned))
        blocks.append(jnp.where(lane < 64, turned, full))
    mine = (2 * r, 2 * r + 1, 2 * (r ^ 1), 2 * (r ^ 1) + 1)
    for target in range(out.shape[0]):
        wanted = jnp.broadcast_to(seen[target : target + 1, :], (16, 128))
        block = jnp.zeros((16, 128), jnp.float32)
        for q in range(4):
            block = jnp.where(wanted == mine[q], blocks[q], block)
        out[target] = block.astype(out.dtype)


def spread(q_index, terms):
    vmem = pl.BlockSpec(memory_space=pltpu.VMEM)
    return pl.pallas_call(
        spread_kernel,
        in_specs=[vmem, vmem],
        out_specs=vmem,
        out_shape=jax.ShapeDtypeStruct((32, 16, 128), jnp.bfloat16),
        compiler_params=pltpu.CompilerParams(vmem_limit_bytes=4 * MIB),
        name="spread",
    )(q_index, terms)


def settle_kernel(arrived, out):
    lane = lax.broadcasted_iota(jnp.int32, (16, 128), 1) // 32
    sums = []
    for c in range(2):
        full = arrived[c].astype(jnp.float32)
        for r in range(2 + c, arrived.shape[0], 2):
            full = full + arrived[r].astype(jnp.float32)
        sums.append(full)
    for k in range(2):
        block = jnp.zeros((16, 128), jnp.float32)
        for z in range(2):
            for c in range(2):
                move = (z * 64 + c * 32 - k * 64 - z * 32) % 128
                turned = pltpu.roll(sums[c], move, 1) if move else sums[c]
                block = jnp.where(lane == 2 * z + c, turned, block)
        out[16 * k : 16 * k + 16, :] = block


def settle(arrived):
    vmem = pl.BlockSpec(memory_space=pltpu.VMEM)
    return pl.pallas_call(
        settle_kernel,
        in_specs=[vmem],
        out_specs=vmem,
        out_shape=jax.ShapeDtypeStruct((32, 128), jnp.float32),
        compiler_params=pltpu.CompilerParams(vmem_limit_bytes=4 * MIB),
        name="settle",
    )(arrived)


def local(pair_matrix, screened, coulomb, q_index):
    bands, share = pair_matrix.shape[1:]
    r = lax.axis_index("row")
    w_other = send(screened, SWAP)
    own = pair_matrix.reshape(1, 2 * bands, share)
    pair = jnp.concatenate([own, send(own, ZPAIR)], axis=0)
    quads = [send(pair, along_z(s)) for s in ZSHIFTS[1:]]
    q_mine = jnp.stack([2 * r, 2 * r + 1, 2 * (r ^ 1), 2 * (r ^ 1) + 1])
    ks = lax.iota(jnp.int32, q_index.shape[0])
    partner = jnp.sum(
        jnp.where(q_index[None] == q_mine[:, None, None], ks[None, :, None], 0), axis=1
    ).astype(jnp.int32)
    quads, partner, coulomb, w_other = lax.optimization_barrier(
        (quads, partner, coulomb.reshape(1, share), w_other)
    )
    stack = jnp.concatenate([pair] + quads, axis=0).reshape(1, NZ * 32, share)
    parts = [send(stack, first_plane(s)) for s in FIRST[1:]]
    p01 = jnp.concatenate([stack, parts[0]], axis=0)
    p23 = jnp.concatenate([parts[1], parts[2]], axis=0)

    f0 = send(p01, second_plane(1))
    g1 = send(p23, second_plane(-1))
    g0 = send(p01, second_plane(-1))
    f1 = send(p23, second_plane(1))
    ff0 = send(f0, second_plane(1))
    gg1 = send(g1, second_plane(-1))

    core, low = r & 1, r >> 4
    passed = jnp.where(core == 0, stack, jnp.where(low == 0, parts[2], parts[1]))
    w_own, w_other, f0, g1, passed, kept = lax.optimization_barrier(
        (screened, w_other, f0, g1, passed, stack)
    )
    near = send(kept, SWAP)
    far = send(passed, ACROSS)
    w = load(w_own, w_other)
    panels = (p01, p23, f0, f1, g0, g1, ff0, gg1)
    terms = solve(partner, coulomb, w, panels, near, far)
    terms = lax.all_to_all(terms, "col", split_axis=0, concat_axis=0, tiled=True)
    placed = spread(q_index, terms)
    arrived = lax.all_to_all(placed, "row", split_axis=0, concat_axis=0, tiled=True)
    return settle(arrived)


def solution(mesh):
    placed = (P("row", None, "col"), P("row", "col", None), P("col"), P())
    return jax.shard_map(
        local, mesh=mesh, in_specs=placed, out_specs=P("row", "col"), check_vma=False
    )
```

```python
import jax
import jax.numpy as jnp
from jax import lax
from jax.experimental import pallas as pl
from jax.experimental.pallas import tpu as pltpu
from jax.sharding import PartitionSpec as P

AXES = ("row", "col")
NX, NY, NZ, NCORE = 4, 4, 8, 2
FIRST = (0, 2, 1, -1)
SECOND = (0, 2, 1, -1)
ZSHIFTS = (0, 4, 2, -2)
MIB = 1024 * 1024


def device_index(x, y, z, c):
    y_hi, y_lo = divmod(y % NY, 2)
    row = (y_lo * NZ + z % NZ) * NCORE + c
    return row * 8 + y_hi * NX + x % NX


def pairs(move):
    found = []
    for x in range(NX):
        for y in range(NY):
            for z in range(NZ):
                for c in range(NCORE):
                    found.append((device_index(x, y, z, c), device_index(*move(x, y, z, c))))
    return found


SWAP = pairs(lambda x, y, z, c: (x, y, z, 1 - c))
ACROSS = pairs(lambda x, y, z, c: (x, y ^ 1, z, 1) if c == 0 else (x, y, z, 0))
ZPAIR = pairs(lambda x, y, z, c: (x, y, z ^ 1, c))


def along_z(s):
    return pairs(lambda x, y, z, c: (x, y, z + s, c))


def first_plane(s):
    return pairs(lambda x, y, z, c: (x + s, y, z, c) if c == 0 else (x, y + s, z, c))


def second_plane(s):
    return pairs(lambda x, y, z, c: (x, y + s, z, c) if c == 0 else (x + s, y, z, c))


def send(value, perm):
    return lax.ppermute(value, AXES, perm)


def contract(a, b):
    return lax.dot_general(a, b, (((1,), (1,)), ((), ())), preferred_element_type=jnp.float32)


def where_am_i():
    r, j = lax.axis_index("row"), lax.axis_index("col")
    return r, j, r & 1, (r >> 1) & 7, r >> 4


def spot(k, i):
    r, j, c, _, y_lo = where_am_i()
    first, second = FIRST[i], SECOND[k]
    x = ((j & 3) - first - c * (second - first)) & 3
    y = (2 * (j >> 2) + y_lo - second - c * (first - second)) & 3
    return (y >> 1) * NX + x, y & 1


def place_of(z_wanted):
    z = where_am_i()[3]
    side = (z ^ z_wanted) & 1
    away = ((z ^ side) - z_wanted) & 7
    return 2 * ((away & 2) + (away >> 2)) + side


def load_kernel(own, other, out, sems):
    copies = [
        pltpu.make_async_copy(w.at[q], out.at[2 * i + q], sems.at[2 * i + q])
        for i, w in enumerate((own, other))
        for q in range(2)
    ]
    for copy in copies:
        copy.start()
    for copy in copies:
        copy.wait()


def load(own, other):
    _, share, whole = own.shape
    return pl.pallas_call(
        load_kernel,
        in_specs=[pl.BlockSpec(memory_space=pl.ANY)] * 2,
        out_specs=pl.BlockSpec(memory_space=pltpu.VMEM),
        out_shape=jax.ShapeDtypeStruct((4, share, whole), own.dtype),
        scratch_shapes=[pltpu.SemaphoreType.DMA((4,))],
        compiler_params=pltpu.CompilerParams(vmem_limit_bytes=16 * MIB),
        cost_estimate=pl.CostEstimate(
            flops=0, bytes_accessed=8 * share * whole * 2, transcendentals=0
        ),
        name="load",
    )(own, other)


def solve_kernel(
    partner, coulomb, w, p01, p23, f0, f1, g0, g1, ff0, gg1, near, far, out,
    panel, left_rows, image,
):
    rows, share = p01.shape[1:]
    _, j, c, _, y_lo = where_am_i()
    starts = [pl.multiple_of(place_of(z) * 32, 32) for z in range(NZ)]
    arrays = ((p01, p23), (ff0, gg1), (f0, f1), (g0, g1))
    for k in range(4):
        for i in range(4):
            col, low = spot(k, i)
            for z in range(NZ):
                to = pl.multiple_of(low * rows + z * 32, 32)
                piece = arrays[k][i // 2][i % 2, pl.ds(starts[z], 32), :]
                panel[pl.ds(to, 32), pl.ds(pl.multiple_of(col * share, share), share)] = piece
    left_rows[: 2 * rows, :] = panel[:, pl.ds(pl.multiple_of(j * share, share), share)]
    for low, stack in ((y_lo, near), (1 - y_lo, far)):
        for z in range(NZ):
            to = pl.multiple_of((2 + low) * rows + z * 32, 32)
            left_rows[pl.ds(to, 32), :] = stack[0, pl.ds(starts[z], 32), :]
    lane = lax.broadcasted_iota(jnp.int32, (16, 128), 1)
    twice = 2.0 * coulomb[...]
    lefts, bares = [], []
    for pair in range(4):
        found = []
        for q in range(4):
            for i in range(8):
                k = partner[q, 16 * pair + 8 * (i // 4) + 4 * (i // 2 % 2) + 2 * c + i % 2]
                block = ((((k >> 1) & 1) ^ c) * 2 + (k >> 5)) * NZ + ((k >> 2) & 7)
                start = pl.multiple_of(block * 32 + (k & 1) * 16, 16)
                found.append(left_rows[pl.ds(start, 16), :])
        found = jnp.concatenate(found, axis=0)
        weighted = (found.astype(jnp.float32) * twice).astype(found.dtype)
        lefts.append(found)
        bares.append(contract(weighted, left_rows[128 * pair : 128 * pair + 128, :]))
    kept = [[None] * 4 for _ in range(4)]
    for q in range(4):
        image[q] = contract(w[q], panel[...]).astype(image.dtype)
        for pair in range(4):
            met = bares[pair][128 * q : 128 * q + 128] - jnp.dot(
                lefts[pair][128 * q : 128 * q + 128],
                image[q, :, 128 * pair : 128 * pair + 128],
                preferred_element_type=jnp.float32,
            )
            block = jnp.zeros((16, 128), jnp.float32)
            for i in range(8):
                block = jnp.where(lane // 16 == i, met[16 * i : 16 * i + 16], block)
            kept[pair][q] = block
    for pair in range(4):
        blocks = kept[pair]
        for two in range(2):
            even, odd = blocks[2 * two], blocks[2 * two + 1]
            out[2 * pair, two] = jnp.where(lane < 64, even, pltpu.roll(odd, 64, 1))
            out[2 * pair + 1, two] = jnp.where(lane < 64, pltpu.roll(even, 64, 1), odd)


def solve(partner, coulomb, w, panels, near, far):
    rows, share = panels[0].shape[1:]
    whole = w.shape[2]
    vmem = pl.BlockSpec(memory_space=pltpu.VMEM)
    return pl.pallas_call(
        solve_kernel,
        in_specs=[pl.BlockSpec(memory_space=pltpu.SMEM)] + [vmem] * 12,
        out_specs=vmem,
        out_shape=jax.ShapeDtypeStruct((8, 2, 16, 128), jnp.float32),
        scratch_shapes=[
            pltpu.VMEM((2 * rows, whole), jnp.bfloat16),
            pltpu.VMEM((4 * rows, share), jnp.bfloat16),
            pltpu.VMEM((4, share, 2 * rows), jnp.bfloat16),
        ],
        compiler_params=pltpu.CompilerParams(vmem_limit_bytes=24 * MIB),
        cost_estimate=pl.CostEstimate(
            flops=2 * 4 * share * whole * 2 * rows,
            bytes_accessed=4 * share * whole * 2,
            transcendentals=0,
        ),
        name="solve",
    )(partner, coulomb, w, *panels, near, far)


def spread_kernel(q_index, terms, out):
    r, j, c, _, _ = where_am_i()
    ks = q_index.shape[0]
    row = lax.broadcasted_iota(jnp.int32, (ks, 128), 0)
    col = lax.broadcasted_iota(jnp.int32, (ks, 128), 1)
    slot = (col & 63) >> 4
    hit = row == 8 * j + 4 * (slot >> 1) + 2 * c + (slot & 1)
    seen = jnp.zeros((ks // 2, 128), jnp.float32)
    for k in range(2):
        rows = q_index[pl.ds(k, ks // 2, stride=2), :].astype(jnp.float32).astype(jnp.bfloat16)
        pick = jnp.where(hit & (col >> 6 == k), 1.0, 0.0).astype(jnp.bfloat16)
        seen = seen + jnp.dot(rows, pick, preferred_element_type=jnp.float32)
    seen = seen.astype(jnp.int32)
    lane = lax.broadcasted_iota(jnp.int32, (16, 128), 1)
    blocks = []
    for two in range(2):
        full = terms[0, two]
        for i in range(1, 8):
            full = full + terms[i, two]
        turned = pltpu.roll(full, 64, 1)
        blocks.append(jnp.where(lane < 64, full, turned))
        blocks.append(jnp.where(lane < 64, turned, full))
    mine = (2 * r, 2 * r + 1, 2 * (r ^ 1), 2 * (r ^ 1) + 1)
    for target in range(out.shape[0]):
        wanted = jnp.broadcast_to(seen[target : target + 1, :], (16, 128))
        block = jnp.zeros((16, 128), jnp.float32)
        for q in range(4):
            block = jnp.where(wanted == mine[q], blocks[q], block)
        out[target] = block.astype(out.dtype)


def spread(q_index, terms):
    vmem = pl.BlockSpec(memory_space=pltpu.VMEM)
    return pl.pallas_call(
        spread_kernel,
        in_specs=[vmem, vmem],
        out_specs=vmem,
        out_shape=jax.ShapeDtypeStruct((32, 16, 128), jnp.bfloat16),
        compiler_params=pltpu.CompilerParams(vmem_limit_bytes=4 * MIB),
        name="spread",
    )(q_index, terms)


def settle_kernel(arrived, out):
    lane = lax.broadcasted_iota(jnp.int32, (16, 128), 1) // 32
    sums = []
    for c in range(2):
        full = arrived[c].astype(jnp.float32)
        for r in range(2 + c, arrived.shape[0], 2):
            full = full + arrived[r].astype(jnp.float32)
        sums.append(full)
    for k in range(2):
        block = jnp.zeros((16, 128), jnp.float32)
        for z in range(2):
            for c in range(2):
                move = (z * 64 + c * 32 - k * 64 - z * 32) % 128
                turned = pltpu.roll(sums[c], move, 1) if move else sums[c]
                block = jnp.where(lane == 2 * z + c, turned, block)
        out[16 * k : 16 * k + 16, :] = block


def settle(arrived):
    vmem = pl.BlockSpec(memory_space=pltpu.VMEM)
    return pl.pallas_call(
        settle_kernel,
        in_specs=[vmem],
        out_specs=vmem,
        out_shape=jax.ShapeDtypeStruct((32, 128), jnp.float32),
        compiler_params=pltpu.CompilerParams(vmem_limit_bytes=4 * MIB),
        name="settle",
    )(arrived)


def local(pair_matrix, screened, coulomb, q_index):
    bands, share = pair_matrix.shape[1:]
    r = lax.axis_index("row")
    w_other = send(screened, SWAP)
    own = pair_matrix.reshape(1, 2 * bands, share)
    pair = jnp.concatenate([own, send(own, ZPAIR)], axis=0)
    quads = [send(pair, along_z(s)) for s in ZSHIFTS[1:]]
    q_mine = jnp.stack([2 * r, 2 * r + 1, 2 * (r ^ 1), 2 * (r ^ 1) + 1])
    ks = lax.iota(jnp.int32, q_index.shape[0])
    partner = jnp.sum(
        jnp.where(q_index[None] == q_mine[:, None, None], ks[None, :, None], 0), axis=1
    ).astype(jnp.int32)
    quads, partner, coulomb, w_other = lax.optimization_barrier(
        (quads, partner, coulomb.reshape(1, share), w_other)
    )
    stack = jnp.concatenate([pair] + quads, axis=0).reshape(1, NZ * 32, share)
    parts = [send(stack, first_plane(s)) for s in FIRST[1:]]
    p01 = jnp.concatenate([stack, parts[0]], axis=0)
    p23 = jnp.concatenate([parts[1], parts[2]], axis=0)

    f0 = send(p01, second_plane(1))
    g1 = send(p23, second_plane(-1))
    g0 = send(p01, second_plane(-1))
    f1 = send(p23, second_plane(1))
    ff0 = send(f0, second_plane(1))
    gg1 = send(g1, second_plane(-1))

    core, low = r & 1, r >> 4
    passed = jnp.where(core == 0, stack, jnp.where(low == 0, parts[2], parts[1]))
    w_own, w_other, f0, g1, passed, kept = lax.optimization_barrier(
        (screened, w_other, f0, g1, passed, stack)
    )
    near = send(kept, SWAP)
    far = send(passed, ACROSS)
    w = load(w_own, w_other)
    panels = (p01, p23, f0, f1, g0, g1, ff0, gg1)
    terms = solve(partner, coulomb, w, panels, near, far)
    terms = lax.all_to_all(terms, "col", split_axis=0, concat_axis=0, tiled=True)
    placed = spread(q_index, terms)
    arrived = lax.all_to_all(placed, "row", split_axis=0, concat_axis=0, tiled=True)
    return settle(arrived)


def solution(mesh):
    placed = (P("row", None, "col"), P("row", "col", None), P("col"), P())
    return jax.shard_map(
        local, mesh=mesh, in_specs=placed, out_specs=P("row", "col"), check_vma=False
    )
```

```python
import jax
import jax.numpy as jnp
from jax import lax
from jax.experimental import pallas as pl
from jax.experimental.pallas import tpu as pltpu
from jax.sharding import PartitionSpec as P

AXES = ("row", "col")
NX, NY, NZ, NCORE = 4, 4, 8, 2
FIRST = (0, 1, 2, -1)
SECOND = (0, 2, 1, -1)
ZSHIFTS = (0, 4, 2, -2)
MIB = 1024 * 1024


def device_index(x, y, z, c):
    y_hi, y_lo = divmod(y % NY, 2)
    row = (y_lo * NZ + z % NZ) * NCORE + c
    return row * 8 + y_hi * NX + x % NX


def pairs(move):
    found = []
    for x in range(NX):
        for y in range(NY):
            for z in range(NZ):
                for c in range(NCORE):
                    found.append((device_index(x, y, z, c), device_index(*move(x, y, z, c))))
    return found


SWAP = pairs(lambda x, y, z, c: (x, y, z, 1 - c))
ACROSS = pairs(lambda x, y, z, c: (x, y ^ 1, z, 1) if c == 0 else (x, y, z, 0))
ZPAIR = pairs(lambda x, y, z, c: (x, y, z ^ 1, c))


def along_z(s):
    return pairs(lambda x, y, z, c: (x, y, z + s, c))


def first_plane(s):
    return pairs(lambda x, y, z, c: (x + s, y, z, c) if c == 0 else (x, y + s, z, c))


def second_plane(s):
    return pairs(lambda x, y, z, c: (x, y + s, z, c) if c == 0 else (x + s, y, z, c))


def send(value, perm):
    return lax.ppermute(value, AXES, perm)


def contract(a, b):
    return lax.dot_general(a, b, (((1,), (1,)), ((), ())), preferred_element_type=jnp.float32)


def where_am_i():
    r, j = lax.axis_index("row"), lax.axis_index("col")
    return r, j, r & 1, (r >> 1) & 7, r >> 4


def spot(k, i):
    r, j, c, _, y_lo = where_am_i()
    first, second = FIRST[i], SECOND[k]
    x = ((j & 3) - first - c * (second - first)) & 3
    y = (2 * (j >> 2) + y_lo - second - c * (first - second)) & 3
    return (y >> 1) * NX + x, y & 1


def place_of(z_wanted):
    z = where_am_i()[3]
    side = (z ^ z_wanted) & 1
    away = ((z ^ side) - z_wanted) & 7
    return 2 * ((away & 2) + (away >> 2)) + side


def load_kernel(own, other, out, sems):
    copies = [
        pltpu.make_async_copy(w.at[q], out.at[2 * i + q], sems.at[2 * i + q])
        for i, w in enumerate((own, other))
        for q in range(2)
    ]
    for copy in copies:
        copy.start()
    for copy in copies:
        copy.wait()


def load(own, other):
    _, share, whole = own.shape
    return pl.pallas_call(
        load_kernel,
        in_specs=[pl.BlockSpec(memory_space=pl.ANY)] * 2,
        out_specs=pl.BlockSpec(memory_space=pltpu.VMEM),
        out_shape=jax.ShapeDtypeStruct((4, share, whole), own.dtype),
        scratch_shapes=[pltpu.SemaphoreType.DMA((4,))],
        compiler_params=pltpu.CompilerParams(vmem_limit_bytes=16 * MIB),
        cost_estimate=pl.CostEstimate(
            flops=0, bytes_accessed=8 * share * whole * 2, transcendentals=0
        ),
        name="load",
    )(own, other)


def solve_kernel(
    partner, coulomb, w, p01, p23, f0, f1, g0, g1, ff0, gg1, near, far, out,
    panel, left_rows, image,
):
    rows, share = p01.shape[1:]
    _, j, c, _, y_lo = where_am_i()
    starts = [pl.multiple_of(place_of(z) * 32, 32) for z in range(NZ)]
    arrays = ((p01, p23), (ff0, gg1), (f0, f1), (g0, g1))
    for k in range(4):
        for i in range(4):
            col, low = spot(k, i)
            for z in range(NZ):
                to = pl.multiple_of(low * rows + z * 32, 32)
                piece = arrays[k][i // 2][i % 2, pl.ds(starts[z], 32), :]
                panel[pl.ds(to, 32), pl.ds(pl.multiple_of(col * share, share), share)] = piece
    left_rows[: 2 * rows, :] = panel[:, pl.ds(pl.multiple_of(j * share, share), share)]
    for low, stack in ((y_lo, near), (1 - y_lo, far)):
        for z in range(NZ):
            to = pl.multiple_of((2 + low) * rows + z * 32, 32)
            left_rows[pl.ds(to, 32), :] = stack[0, pl.ds(starts[z], 32), :]
    for q in range(4):
        image[q] = contract(w[q], panel[...]).astype(image.dtype)

    lane = lax.broadcasted_iota(jnp.int32, (16, 128), 1)
    twice = 2.0 * coulomb[...]
    for pair in range(4):
        columns = left_rows[128 * pair : 128 * pair + 128, :]
        lefts, blocks = [], []
        for q in range(4):
            for i in range(8):
                k = partner[q, 16 * pair + 8 * (i // 4) + 4 * (i // 2 % 2) + 2 * c + i % 2]
                block = ((((k >> 1) & 1) ^ c) * 2 + (k >> 5)) * NZ + ((k >> 2) & 7)
                start = pl.multiple_of(block * 32 + (k & 1) * 16, 16)
                lefts.append(left_rows[pl.ds(start, 16), :])
        lefts = jnp.concatenate(lefts, axis=0)
        weighted = (lefts.astype(jnp.float32) * twice).astype(lefts.dtype)
        bare = contract(weighted, columns)
        for q in range(4):
            met = bare[128 * q : 128 * q + 128] - jnp.dot(
                lefts[128 * q : 128 * q + 128],
                image[q, :, 128 * pair : 128 * pair + 128],
                preferred_element_type=jnp.float32,
            )
            block = jnp.zeros((16, 128), jnp.float32)
            for i in range(8):
                block = jnp.where(lane // 16 == i, met[16 * i : 16 * i + 16], block)
            blocks.append(block)
        for two in range(2):
            even, odd = blocks[2 * two], blocks[2 * two + 1]
            out[2 * pair, two] = jnp.where(lane < 64, even, pltpu.roll(odd, 64, 1))
            out[2 * pair + 1, two] = jnp.where(lane < 64, pltpu.roll(even, 64, 1), odd)


def solve(partner, coulomb, w, panels, near, far):
    rows, share = panels[0].shape[1:]
    whole = w.shape[2]
    vmem = pl.BlockSpec(memory_space=pltpu.VMEM)
    return pl.pallas_call(
        solve_kernel,
        in_specs=[pl.BlockSpec(memory_space=pltpu.SMEM)] + [vmem] * 12,
        out_specs=vmem,
        out_shape=jax.ShapeDtypeStruct((8, 2, 16, 128), jnp.float32),
        scratch_shapes=[
            pltpu.VMEM((2 * rows, whole), jnp.bfloat16),
            pltpu.VMEM((4 * rows, share), jnp.bfloat16),
            pltpu.VMEM((4, share, 2 * rows), jnp.bfloat16),
        ],
        compiler_params=pltpu.CompilerParams(vmem_limit_bytes=24 * MIB),
        cost_estimate=pl.CostEstimate(
            flops=2 * 4 * share * whole * 2 * rows,
            bytes_accessed=4 * share * whole * 2,
            transcendentals=0,
        ),
        name="solve",
    )(partner, coulomb, w, *panels, near, far)


def spread_kernel(q_index, terms, out):
    r, j, c, _, _ = where_am_i()
    ks = q_index.shape[0]
    row = lax.broadcasted_iota(jnp.int32, (ks, 128), 0)
    col = lax.broadcasted_iota(jnp.int32, (ks, 128), 1)
    slot = (col & 63) >> 4
    hit = row == 8 * j + 4 * (slot >> 1) + 2 * c + (slot & 1)
    seen = jnp.zeros((ks // 2, 128), jnp.float32)
    for k in range(2):
        rows = q_index[pl.ds(k, ks // 2, stride=2), :].astype(jnp.float32).astype(jnp.bfloat16)
        pick = jnp.where(hit & (col >> 6 == k), 1.0, 0.0).astype(jnp.bfloat16)
        seen = seen + jnp.dot(rows, pick, preferred_element_type=jnp.float32)
    seen = seen.astype(jnp.int32)
    lane = lax.broadcasted_iota(jnp.int32, (16, 128), 1)
    blocks = []
    for two in range(2):
        full = terms[0, two]
        for i in range(1, 8):
            full = full + terms[i, two]
        turned = pltpu.roll(full, 64, 1)
        blocks.append(jnp.where(lane < 64, full, turned))
        blocks.append(jnp.where(lane < 64, turned, full))
    mine = (2 * r, 2 * r + 1, 2 * (r ^ 1), 2 * (r ^ 1) + 1)
    for target in range(out.shape[0]):
        wanted = jnp.broadcast_to(seen[target : target + 1, :], (16, 128))
        block = jnp.zeros((16, 128), jnp.float32)
        for q in range(4):
            block = jnp.where(wanted == mine[q], blocks[q], block)
        out[target] = block.astype(out.dtype)


def spread(q_index, terms):
    vmem = pl.BlockSpec(memory_space=pltpu.VMEM)
    return pl.pallas_call(
        spread_kernel,
        in_specs=[vmem, vmem],
        out_specs=vmem,
        out_shape=jax.ShapeDtypeStruct((32, 16, 128), jnp.bfloat16),
        compiler_params=pltpu.CompilerParams(vmem_limit_bytes=4 * MIB),
        name="spread",
    )(q_index, terms)


def settle_kernel(arrived, out):
    lane = lax.broadcasted_iota(jnp.int32, (16, 128), 1) // 32
    sums = []
    for c in range(2):
        full = arrived[c].astype(jnp.float32)
        for r in range(2 + c, arrived.shape[0], 2):
            full = full + arrived[r].astype(jnp.float32)
        sums.append(full)
    for k in range(2):
        block = jnp.zeros((16, 128), jnp.float32)
        for z in range(2):
            for c in range(2):
                move = (z * 64 + c * 32 - k * 64 - z * 32) % 128
                turned = pltpu.roll(sums[c], move, 1) if move else sums[c]
                block = jnp.where(lane == 2 * z + c, turned, block)
        out[16 * k : 16 * k + 16, :] = block


def settle(arrived):
    vmem = pl.BlockSpec(memory_space=pltpu.VMEM)
    return pl.pallas_call(
        settle_kernel,
        in_specs=[vmem],
        out_specs=vmem,
        out_shape=jax.ShapeDtypeStruct((32, 128), jnp.float32),
        compiler_params=pltpu.CompilerParams(vmem_limit_bytes=4 * MIB),
        name="settle",
    )(arrived)


def local(pair_matrix, screened, coulomb, q_index):
    bands, share = pair_matrix.shape[1:]
    r = lax.axis_index("row")
    w_other = send(screened, SWAP)
    own = pair_matrix.reshape(1, 2 * bands, share)
    pair = jnp.concatenate([own, send(own, ZPAIR)], axis=0)
    quads = [send(pair, along_z(s)) for s in ZSHIFTS[1:]]
    q_mine = jnp.stack([2 * r, 2 * r + 1, 2 * (r ^ 1), 2 * (r ^ 1) + 1])
    ks = lax.iota(jnp.int32, q_index.shape[0])
    partner = jnp.sum(
        jnp.where(q_index[None] == q_mine[:, None, None], ks[None, :, None], 0), axis=1
    ).astype(jnp.int32)
    quads, partner, coulomb, w_other = lax.optimization_barrier(
        (quads, partner, coulomb.reshape(1, share), w_other)
    )
    stack = jnp.concatenate([pair] + quads, axis=0).reshape(1, NZ * 32, share)
    parts = [send(stack, first_plane(s)) for s in FIRST[1:]]
    p01 = jnp.concatenate([stack, parts[0]], axis=0)
    p23 = jnp.concatenate([parts[1], parts[2]], axis=0)

    f0 = send(p01, second_plane(1))
    g1 = send(p23, second_plane(-1))
    g0 = send(p01, second_plane(-1))
    f1 = send(p23, second_plane(1))
    ff0 = send(f0, second_plane(1))
    gg1 = send(g1, second_plane(-1))

    core, low = r & 1, r >> 4
    passed = jnp.where(core == 0, stack, jnp.where(low == 0, parts[2], parts[0]))
    w_own, w_other, f0, g1, passed, kept = lax.optimization_barrier(
        (screened, w_other, f0, g1, passed, stack)
    )
    near = send(kept, SWAP)
    far = send(passed, ACROSS)
    w = load(w_own, w_other)
    panels = (p01, p23, f0, f1, g0, g1, ff0, gg1)
    terms = solve(partner, coulomb, w, panels, near, far)
    terms = lax.all_to_all(terms, "col", split_axis=0, concat_axis=0, tiled=True)
    placed = spread(q_index, terms)
    arrived = lax.all_to_all(placed, "row", split_axis=0, concat_axis=0, tiled=True)
    return settle(arrived)


def solution(mesh):
    placed = (P("row", None, "col"), P("row", "col", None), P("col"), P())
    return jax.shard_map(
        local, mesh=mesh, in_specs=placed, out_specs=P("row", "col"), check_vma=False
    )
```
